32 devices in a mesh: groups: 2 (over y), row: 4 (over z), col: 4 (over x, core).
Axes of the slice: x: 2, y: 2, z: 4, core: 2. Of those that a mesh axis runs over, the one named last changes fastest.
Arguments:
- positions: float32 [4096, 3, 128], P(('groups', 'row', 'col')), parts along dimension 0, may hold values from -6 to 6
- normals: float32 [4096, 3, 128], P(('groups', 'row', 'col')), parts along dimension 0, may hold values from -6 to 6
- curvature: float32 [4096, 128], P(('groups', 'row', 'col')), parts along dimension 0, may hold values from 0.5 to 3
- pair_targets: int32 [32, 512], P(('groups', 'row', 'col')), parts along dimension 0, may hold values from 0 to 511, as said below
- pair_sources: int32 [32, 512], P(('groups', 'row', 'col')), parts along dimension 0, may hold values from 0 to 511
- pair_count: int32 [32], P(('groups', 'row', 'col')), parts along dimension 0, may hold values from 64 to 512, as said below
- node_counts: int32 [512, 8], P('groups'), parts along dimension 0, may hold values from 1 to 128, 642 in all within a row
- drop_clusters: int32 [512, 8], P('groups'), parts along dimension 0, may hold values from 0 to 2047, as said below
- drop_owner: int32 [512], P('groups'), parts along dimension 0, may hold values from 0 to 15, as said below
Outputs:
- drop_velocity: float32 [4096, 3, 128], P(('groups', 'row', 'col')), parts along dimension 0
The draws below stay inside these ranges and needn't reach their ends.
There are 2 independent parts, one for each index of `groups`. The reference program is written for one: setup_inputs(seed, part) draws one part's arguments, and reference() takes and returns one part's arrays. A program takes and returns all parts, laid end to end along the dimension named above; each array names one. Nothing has to cross between parts.
Inputs may be any that keep to these rules, and one draw needn't show every extreme that they name: `drop_clusters`: every cluster of 0 to 2047 appears exactly once. Of the 128 clusters of one device, at most 16 belong to drops of any one owner, and this many is reached. `drop_owner`: every device owns exactly 16 drops. `pair_count`: the largest count is reached on some device; list entries past a device's count are not pairs. In each device's list, at most 256 entries have the same value of pair_targets // 128, and every device's list reaches this many for some value. `node_counts`: each drop's counts sum to 642.
All inputs are finite; a program needn't handle non-finite values.
Results may differ from the reference program's by a relative error of at most 0.0003.
Values sent between devices are 32-bit elements; how exact they have to be, the bound alone decides.
A program may use at most 64 MiB of HBM per device.

```python
import math
import jax
import jax.numpy as jnp
import numpy as np
from jax import lax

P_SIZE = 128
CPD = 8
NODES_DROP = 642
CL_DEV = 128
PAIRS_DEV = 512
DEVS = 16
CLUSTERS = 2048
DROP_DEV = 16
DROPS = 256
CAP = 16
TCAP = 256
N_ROW = 4
N_COL = 4


def cluster_layout(key):
    base = jax.random.fold_in(key, 7)
    first_key, second_key, third_key = jax.random.split(base, 3)
    group_count = CL_DEV // CAP
    ranking = jax.random.permutation(first_key, DEVS).astype(jnp.int32)
    ranking = ranking.at[1].set(-2)
    ranking = ranking.at[DEVS // 2].set(-1)
    offsets = jnp.argsort(ranking, stable=True)[:group_count].astype(jnp.int32)
    owners = jnp.arange(DEVS, dtype=jnp.int32)[:, None]
    arrival = jnp.arange(CL_DEV, dtype=jnp.int32)[None, :]
    group_of = arrival // CAP
    anchor = (owners - offsets[group_of]) % DEVS
    homes = anchor * CL_DEV + arrival
    shuffle_keys = jax.random.split(second_key, DEVS)
    shuffles = jax.vmap(lambda one_key: jax.random.permutation(one_key, CL_DEV))(shuffle_keys)
    homes = jnp.take_along_axis(homes, shuffles.astype(jnp.int32), axis=1)
    grouped = homes.reshape(DEVS * DROP_DEV, CPD)
    labels = jax.random.permutation(third_key, DROPS).astype(jnp.int32)
    clusters = jnp.zeros((DROPS, CPD), jnp.int32).at[labels].set(grouped)
    owner_of = jnp.zeros((DROPS,), jnp.int32).at[labels].set(jnp.arange(DROPS, dtype=jnp.int32) // DROP_DEV)
    return (clusters, owner_of)


def draw_drop_clusters(key, part):
    return cluster_layout(key)[0]


def draw_drop_owner(key, part):
    return cluster_layout(key)[1]


def draw_pair_count(key, part):
    base = jax.random.fold_in(key, 11)
    first_key, second_key = jax.random.split(base, 2)
    counts = jax.random.randint(first_key, (DEVS,), PAIRS_DEV // 8, PAIRS_DEV // 2 + 1, dtype=jnp.int32)
    busiest = jax.random.randint(second_key, (), 0, DEVS, dtype=jnp.int32)
    return counts.at[busiest].set(PAIRS_DEV)


def draw_pair_targets(key, part):
    base = jax.random.fold_in(key, 13)
    first_key, second_key, third_key = jax.random.split(base, 3)
    perm_keys = jax.random.split(first_key, DEVS)
    orders = jax.vmap(lambda one_key: jax.random.permutation(one_key, PAIRS_DEV))(perm_keys).astype(jnp.int32)
    shifts = jax.random.randint(second_key, (DEVS, 1), 0, N_COL, dtype=jnp.int32)
    home_col = (orders // TCAP + shifts) % N_COL
    within = jax.random.randint(third_key, (DEVS, PAIRS_DEV), 0, CL_DEV, dtype=jnp.int32)
    return home_col * CL_DEV + within


def place_ends(values, stream_key, low, largest):
    index_at = [jax.random.randint(jax.random.fold_in(stream_key, axis), (), 0, length) for axis, length in enumerate(values.shape)]
    main_axis = values.shape.index(max(values.shape))
    neighbour = index_at[:main_axis] + [(index_at[main_axis] + 1) % values.shape[main_axis]] + index_at[main_axis + 1:]
    return values.at[tuple(index_at)].set(low).at[tuple(neighbour)].set(largest)


def level_of(own_key, shape, pieces, smallest, high):
    def one(axis_at, shards_of):
        steps = jax.random.uniform(jax.random.fold_in(jax.random.fold_in(own_key, 6), axis_at), (shards_of,), jnp.float32, smallest / len(pieces), high / len(pieces))
        return jnp.repeat(jnp.exp(steps), shape[axis_at] // shards_of).reshape((-1,) + (1,) * (len(shape) - axis_at - 1))

    loudness = one(*pieces[0])
    for cut in pieces[1:]:
        loudness = loudness * one(*cut)
    return loudness


def length_profile(count, total, most, slope):
    portions = [(1 << 20) // math.isqrt(grade ** slope) + 1 for grade in range(2, count + 1)]
    surplus, given = total - most - (count - 1), [1] * (count - 1)
    while surplus > 0:
        free = [i for i in range(count - 1) if given[i] < most]
        mass, left = sum([portions[i] for i in free]), surplus
        for i in free:
            more = min(most - given[i], max(1, left * portions[i] // mass), surplus)
            given[i] = given[i] + more
            surplus = surplus - more
    return np.array([most] + given)


def uneven_parts(stream_key, number_of, total, most, skew):
    if number_of == 2:
        one = jax.random.randint(stream_key, (), max(1, total - most), min(most, total - 1) + 1)
        return jnp.stack([one, total - one])
    tallies = jnp.asarray(length_profile(number_of, total, most, skew), jnp.int32)
    pairs = (number_of - 1) // 2
    source_of, sink = tallies[1:1 + 2 * pairs:2], tallies[2:2 + 2 * pairs:2]
    slack = jnp.minimum(source_of - 1, most - sink)
    moved = jax.random.randint(jax.random.fold_in(stream_key, 1), (pairs,), 0, 1 << 20) % (slack + 1)
    tallies = tallies.at[1:1 + 2 * pairs:2].set(source_of - moved).at[2:2 + 2 * pairs:2].set(sink + moved)
    return tallies[jax.random.permutation(jax.random.fold_in(stream_key, 2), number_of)]


def gaussian(key, extent, deviation, bound, pieces=(), kind=jnp.bfloat16):
    factor_of = level_of(key, extent, pieces, -0.22, 0.18) if pieces else 1.0
    drawn = jax.random.normal(key, extent, jnp.float32) * deviation * factor_of
    return jnp.minimum(jnp.maximum(drawn, -bound), bound).astype(kind)


def setup_inputs(seed: int = 0, part: int = 0) -> dict:
    splits = jax.random.split(jax.random.key(seed), 10)
    part_keys = jax.random.split(jax.random.fold_in(splits[9], part), 10)
    return {
        "positions": gaussian(part_keys[0], (CLUSTERS, 3, P_SIZE), 1.0, 6.0, ((0, 16),), jnp.float32),
        "normals": gaussian(part_keys[1], (CLUSTERS, 3, P_SIZE), 1.0, 6.0, ((0, 16),), jnp.float32),
        "curvature": jnp.clip(0.5 + 2.5 * jax.random.uniform(part_keys[2], (CLUSTERS, P_SIZE), jnp.float32) ** level_of(part_keys[2], (CLUSTERS, P_SIZE), ((0, 16),), -0.2, 0.2), 0.5, 3.0),
        "pair_targets": draw_pair_targets(jax.random.fold_in(jax.random.fold_in(splits[9], part), 71), part),
        "pair_sources": place_ends(jax.random.randint(part_keys[4], (DEVS, PAIRS_DEV), 0, N_ROW * CL_DEV), jax.random.fold_in(part_keys[4], 1), 0, (N_ROW * CL_DEV) - 1).astype(jnp.int32),
        "pair_count": draw_pair_count(jax.random.fold_in(jax.random.fold_in(splits[9], part), 71), part),
        "node_counts": jax.vmap(lambda own: uneven_parts(own, CPD, NODES_DROP, P_SIZE, 1))(jax.random.split(part_keys[6], DROPS)).reshape((DROPS, CPD)).astype(jnp.int32),
        "drop_clusters": draw_drop_clusters(jax.random.fold_in(jax.random.fold_in(splits[9], part), 71), part),
        "drop_owner": draw_drop_owner(jax.random.fold_in(jax.random.fold_in(splits[9], part), 71), part),
    }


pair_block = 32
regular_sq = 0.0025
stokes_scale = 1.0 / (8.0 * math.pi)

def stokeslet(target_pos, source_pos, source_force):
    delta_x = target_pos[:, 0, :, None] - source_pos[:, 0, None, :]
    delta_y = target_pos[:, 1, :, None] - source_pos[:, 1, None, :]
    delta_z = target_pos[:, 2, :, None] - source_pos[:, 2, None, :]
    dist_sq = delta_x * delta_x + delta_y * delta_y + delta_z * delta_z
    inverse = lax.rsqrt(dist_sq + regular_sq)
    weight = inverse * inverse * inverse
    isotropic = (dist_sq + 2.0 * regular_sq) * weight
    force_x = source_force[:, 0, None, :]
    force_y = source_force[:, 1, None, :]
    force_z = source_force[:, 2, None, :]
    project = (delta_x * force_x + delta_y * force_y + delta_z * force_z) * weight
    speed_x = lax.optimization_barrier(jnp.sum(isotropic * force_x + project * delta_x, axis=2))
    speed_y = lax.optimization_barrier(jnp.sum(isotropic * force_y + project * delta_y, axis=2))
    speed_z = lax.optimization_barrier(jnp.sum(isotropic * force_z + project * delta_z, axis=2))
    return stokes_scale * jnp.stack([speed_x, speed_y, speed_z], axis=1)

def reference(positions, normals, curvature, pair_targets, pair_sources, pair_count, node_counts, drop_clusters, drop_owner):
    entries = DROPS * CPD
    flat_clusters = drop_clusters.reshape(-1)
    flat_counts = node_counts.reshape(-1)
    home_counts = jnp.zeros((entries,), jnp.int32).at[flat_clusters].set(flat_counts)
    slot_index = jnp.arange(P_SIZE, dtype=jnp.int32)
    home_live = (slot_index[None, :] < home_counts[:, None]).astype(jnp.float32)
    forces = (curvature * home_live)[:, None, :] * normals
    devices = jnp.arange(DEVS, dtype=jnp.int32)
    row_of = devices // N_COL
    col_of = devices % N_COL
    target_global = row_of[:, None] * (N_COL * CL_DEV) + pair_targets
    source_global = (pair_sources // CL_DEV * N_COL + col_of[:, None]) * CL_DEV + pair_sources % CL_DEV

    def per_device(speeds, items):
        target_row, source_row, limit = items
        blocks = (limit + pair_block - 1) // pair_block

        def accumulate(block_number, totals):
            picked = block_number * pair_block + jnp.arange(pair_block, dtype=jnp.int32)
            active = picked < limit
            picked = jnp.minimum(picked, PAIRS_DEV - 1)
            target_ids = target_row[picked]
            source_ids = source_row[picked]
            contrib = stokeslet(positions[target_ids], positions[source_ids], forces[source_ids])
            contrib = contrib * active.astype(jnp.float32)[:, None, None]
            return totals.at[target_ids].add(contrib)
        return (lax.fori_loop(0, blocks, accumulate, speeds), None)
    speeds, unused = lax.scan(per_device, jnp.zeros((entries, 3, P_SIZE), jnp.float32), (target_global, source_global, pair_count))
    owner_order = jnp.argsort(drop_owner, stable=True)
    ordered_clusters = drop_clusters[owner_order].reshape(-1)
    ordered_counts = node_counts[owner_order].reshape(-1)
    owned_live = (slot_index[None, :] < ordered_counts[:, None]).astype(jnp.float32)
    return speeds[ordered_clusters] * owned_live[:, None, :]
```

```python
import functools
import math

import jax
import jax.numpy as jnp
from jax import lax
from jax.experimental import pallas as pl
from jax.experimental.pallas import tpu as pltpu
from jax.sharding import PartitionSpec as P

regular_sq = 0.0025
inv_reg = 1.0 / math.sqrt(regular_sq)
stokes_scale = inv_reg / (8.0 * math.pi)
MESH = pl.DeviceIdType.MESH
VMEM = pl.BlockSpec(memory_space=pltpu.VMEM)
SMEM = pl.BlockSpec(memory_space=pltpu.SMEM)


unroll = 16
f32, bf16, ints = jnp.float32, jnp.bfloat16, jnp.int32


def keep(x):
    return pltpu.with_memory_space_constraint(x, pltpu.VMEM)


def split3(x):
    high = x.astype(bf16).astype(f32)
    rest = x - high
    middle = rest.astype(bf16).astype(f32)
    return high, middle, rest - middle


def as_row(column):
    return jnp.transpose(jnp.broadcast_to(column, (column.shape[0], 128)))[0:1]


def gather_kernel(
        nrow, ncol, cap, pos_ref, nrm_ref, curv_ref, nct_ref, dct_ref, own_ref, tgt_ref, src_ref, count_ref,
        near_ref, right_ref, far_ref, lt_ref, ls_ref, lc_ref, pack_ref, from_ref, rank_ref, cnt_ref,
        t_ref, s_ref, tsend, trecv, zsend, zrecv, fsend, frecv, osend, orecv, lsend, lrecv):
    row, col = lax.axis_index("row"), lax.axis_index("col")
    core = lax.rem(col, 2)
    other = col + 1 - 2 * core
    me = row * ncol + col
    local = pos_ref.shape[1]
    drops = own_ref.shape[1]
    per_drop = dct_ref.shape[0]
    barrier = pltpu.get_barrier_semaphore()
    for d in range(1, nrow):
        pl.semaphore_signal(barrier, inc=1, device_id={"row": lax.rem(row + d, nrow)}, device_id_type=MESH)
    for d in range(1, ncol):
        pl.semaphore_signal(barrier, inc=1, device_id={"col": lax.rem(col + d, ncol)}, device_id_type=MESH)
    for k in range(3):
        s_ref[core, row, k] = pos_ref[k]
    lt_ref[core] = tgt_ref[...]
    ls_ref[core] = src_ref[...]
    lc_ref[core] = jnp.full((1, 128), count_ref[0], ints)

    def remote(src, dst, send, recv, where):
        return pltpu.make_async_remote_copy(
            src_ref=src, dst_ref=dst, send_sem=send, recv_sem=recv, device_id=where, device_id_type=MESH)

    sibling = {"col": other}
    small = [remote(ref.at[core], ref.at[core], lsend.at[i], lrecv.at[i], sibling)
             for i, ref in enumerate((lt_ref, ls_ref, lc_ref))]
    rows = [remote(pos_ref, t_ref.at[col], tsend.at[d - 1], trecv.at[d - 1], {"col": lax.rem(col + d, ncol)})
            for d in range(1, ncol)]

    def along(d, k):
        piece = s_ref.at[core, row, k]
        return remote(piece, piece, zsend.at[d - 1, k], zrecv.at[d - 1, k], {"row": lax.rem(row + d, nrow)})

    def arrived(d, k):
        return s_ref.at[core, lax.rem(row + nrow - d, nrow), k]

    def onward(d, k):
        piece = arrived(d, k)
        return remote(piece, piece, fsend.at[d - 1, k], frecv.at[d - 1, k], sibling)

    def own(k):
        piece = s_ref.at[core, row, k]
        return remote(piece, piece, osend.at[k], orecv.at[k], sibling)

    pl.semaphore_wait(barrier, nrow + ncol - 2)
    for k in range(3):
        for d in range(1, nrow):
            along(d, k).start()
    for copy in small + rows:
        copy.start()

    index = lax.broadcasted_iota(ints, (local, 1), 0)
    ids = me * local + index

    def match(chunk, carry):
        counts, owners = carry
        lanes = pl.ds(pl.multiple_of(chunk * 128, 128), 128)
        clusters, nodes_in, owner = dct_ref[:, lanes], nct_ref[:, lanes], own_ref[0:1, lanes]
        for k in range(per_drop):
            hit = ids == clusters[k:k + 1]
            counts = counts + jnp.where(hit, nodes_in[k:k + 1], 0)
            owners = owners + jnp.where(hit, owner, 0)
        return counts, owners

    none = jnp.zeros((local, 128), ints)
    counts, owners = lax.fori_loop(0, drops // 128, match, (none, none))
    home_counts = jnp.sum(counts, axis=1, keepdims=True, dtype=ints)
    home_owner = jnp.sum(owners, axis=1, keepdims=True, dtype=ints)
    scale = jnp.where(lax.broadcasted_iota(ints, (local, 128), 1) < home_counts, curv_ref[...], 0.0)
    for k in range(3):
        s_ref[core, row, 3 + k] = scale * nrm_ref[k]
        for d in range(1, nrow):
            along(d, 3 + k).start()
    for k in range(6):
        own(k).start()

    owner_row = as_row(home_owner.astype(f32)).astype(ints)
    lane = lax.broadcasted_iota(ints, (local, local), 1)
    rank = jnp.sum(((owner_row == home_owner) & (lane < index)).astype(ints), axis=1, keepdims=True, dtype=ints)
    slot = home_owner * cap + rank
    slots = lax.broadcasted_iota(ints, pack_ref.shape, 1)
    pack_ref[...] = jnp.sum(jnp.where(slot == slots, index, 0), axis=0, keepdims=True, dtype=ints)

    here = lax.broadcasted_iota(ints, (local, 1), 0)
    drop_of = lax.div(here, per_drop)
    width = 256 if drops % 256 == 0 else 128
    before = (lax.broadcasted_iota(ints, (width, width), 0) < lax.broadcasted_iota(ints, (width, width), 1)).astype(bf16)

    def owned(chunk, carry):
        clusters, counted, base = carry
        lanes = pl.ds(pl.multiple_of(chunk * width, width), width)
        mine = own_ref[0:1, lanes] == me
        marks = jnp.broadcast_to(mine.astype(f32), (16, width)).astype(bf16)
        place = jnp.dot(marks, before, preferred_element_type=f32)[0:1].astype(ints) + base
        chosen = mine & (place == drop_of)
        clusters = clusters + jnp.where(chosen, jnp.concatenate([dct_ref[:, lanes]] * (local // per_drop), axis=0), 0)
        counted = counted + jnp.where(chosen, jnp.concatenate([nct_ref[:, lanes]] * (local // per_drop), axis=0), 0)
        return clusters, counted, base + jnp.sum(mine.astype(ints), axis=1, keepdims=True, dtype=ints)

    wide = jnp.zeros((local, width), ints)
    clusters, counted, _ = lax.fori_loop(0, drops // width, owned, (wide, wide, jnp.zeros((1, 1), ints)))
    clusters = jnp.sum(clusters, axis=1, keepdims=True, dtype=ints)
    cnt_ref[...] = as_row(jnp.sum(counted, axis=1, keepdims=True, dtype=ints).astype(f32)).astype(ints)
    clusters_row = as_row(clusters.astype(f32)).astype(ints)
    anchor, anchor_row = lax.div(clusters, local), lax.div(clusters_row, local)
    from_ref[...] = anchor_row
    rank_ref[...] = jnp.sum(((anchor == anchor_row) & (clusters < clusters_row)).astype(ints), axis=0, keepdims=True, dtype=ints)

    def fill(i, carry):
        base = pl.multiple_of(i * 64, 64)
        far_ref[pl.ds(base, 64), :] = jnp.zeros((64, 128), f32)
        return carry

    lax.fori_loop(0, far_ref.shape[0] // 64, fill, 0)

    def spread(l, r, k):
        at = (l * nrow + r) * local * 8 + (k if k < 3 else k + 1)
        far_ref[pl.ds(at, local, stride=8), :] = s_ref[l, r, k]

    for k in range(6):
        spread(core, row, k)

    sub = lax.broadcasted_iota(ints, (8, 128), 0)
    low = sub < 4

    def targets(d):
        c = lax.rem(col + ncol - d, ncol)
        square = jnp.ones((local, 128), f32)
        start = c * local * 8
        for k in range(3):
            coord = pos_ref[k] if d == 0 else t_ref[c, k]
            centre = jnp.mean(coord, axis=1, keepdims=True)
            coord = (coord - centre) * inv_reg
            square = square + coord * coord
            near_ref[pl.ds(start + k, local, stride=8), :] = coord
            near_ref[pl.ds(start + 4 + k, local, stride=8), :] = jnp.broadcast_to(centre, coord.shape)
        near_ref[pl.ds(start + 3, local, stride=8), :] = square
        near_ref[pl.ds(start + 7, local, stride=8), :] = jnp.zeros((local, 128), f32)

        def coefficients(i, carry):
            for u in range(8):
                t = c * local + i * 8 + u
                tile = near_ref[pl.ds(pl.multiple_of(t * 8, 8), 8), :]
                high, middle, rest = split3(tile)
                sums = jnp.where(sub == 0, high[3:4], jnp.where(sub == 1, middle[3:4], jnp.where(sub == 2, rest[3:4], 0.0)))
                high = jnp.where(sub < 3, high, jnp.where(sub == 3, 1.0, 0.0))
                middle = jnp.where(sub < 3, middle, 0.0)
                rest = jnp.where(sub < 3, rest, 0.0)
                high_up, middle_up = pltpu.roll(high, 4, 0), pltpu.roll(middle, 4, 0)
                right_ref[t] = jnp.concatenate([
                    high + middle_up, rest + high_up, middle + high_up, sums], axis=0).astype(bf16)
            return carry

        lax.fori_loop(0, local // 8, coefficients, 0)

    targets(0)
    for d in range(1, ncol):
        rows[d - 1].wait_recv()
        targets(d)
    for k in range(6):
        own(k).wait_recv()
        spread(1 - core, row, k)
    for k in range(6):
        for d in range(1, nrow):
            along(d, k).wait_recv()
            onward(d, k).start()
            spread(core, lax.rem(row + nrow - d, nrow), k)
    for k in range(6):
        for d in range(1, nrow):
            onward(d, k).wait_recv()
            spread(1 - core, lax.rem(row + nrow - d, nrow), k)
    for copy in small:
        copy.wait()
    for copy in rows:
        copy.wait_send()
    for k in range(6):
        own(k).wait_send()
        for d in range(1, nrow):
            along(d, k).wait_send()
            onward(d, k).wait_send()


def pair_kernel(lt_ref, ls_ref, lc_ref, near_ref, right_ref, far_ref, v_ref, acc_ref, both_a, both_b, g_a, g_b):
    ncol, _, local, _ = v_ref.shape
    half_far = far_ref.shape[0] // 16
    core = lax.rem(lax.axis_index("col"), 2)
    sub = lax.broadcasted_iota(ints, (8, 128), 0)
    low = sub < 4
    last = (sub == 3) | (sub == 7)
    scale = jnp.where(low, -2.0, 1.0).astype(f32)
    fold = jnp.where(sub == 3, 1.0, jnp.where(sub == 7, -1.0, 0.0)).astype(f32)
    some = jnp.where(low, 1.0, 0.0).astype(f32)
    unit = jnp.where(low, inv_reg, 1.0).astype(f32)
    idle = jnp.where(low, inv_reg, 0.0).astype(f32)
    nothing = jnp.zeros((32, 128), bf16)
    acc_ref[...] = jnp.zeros_like(acc_ref)
    both_b[...] = jnp.ones_like(both_b)
    g_b[...] = jnp.zeros_like(g_b)
    n0 = lc_ref[0, 0, 0]
    total = n0 + lc_ref[1, 0, 0]
    half = (total + 1) // 2
    first = core * half
    n = jnp.where(core == 0, half, total - half)

    def entry(j):
        j = first + jnp.clip(j, 0, n - 1)
        second = j >= n0
        return second.astype(ints), jnp.where(second, j - n0, j)

    def tile(i):
        return pl.ds(pl.multiple_of(i * 8, 8), 8)

    def distances(block, both_ref, g_ref):
        for u in range(unroll):
            j = block * unroll + u
            l, e = entry(j)
            t, s = lt_ref[l, 0, e], ls_ref[l, 0, e] + l * half_far
            centre = jnp.where(low, pltpu.roll(near_ref[tile(t), :], 4, 0), 0.0)
            right = right_ref[t]
            shifted = (far_ref[tile(s), :] - centre) * jnp.where(j < n, unit, idle)
            prod = shifted * jnp.where(low, shifted, pltpu.roll(shifted, 4, 0))
            prod = prod + pltpu.roll(prod, 1, 0)
            prod = prod + pltpu.roll(prod, 2, 0)
            hi, mid, lo = split3(shifted * scale + prod * fold)
            hi_up, mid_up, lo_up = pltpu.roll(hi, 4, 0), pltpu.roll(mid, 4, 0), pltpu.roll(lo, 4, 0)
            left = jnp.concatenate([
                jnp.where(low, hi, hi_up), jnp.where(low, hi, mid_up), jnp.where(low, mid, lo_up), some,
                jnp.where(low, hi_up, hi), jnp.where(low, hi_up, mid), jnp.where(low, mid_up, lo),
                jnp.zeros((8, 128), f32)], axis=0).astype(bf16)
            weights = jnp.concatenate([
                jnp.concatenate([right, nothing], axis=1), jnp.concatenate([nothing, right], axis=1)], axis=0)
            both_ref[u] = lax.dot_general(left, weights, (((0,), (0,)), ((), ())), preferred_element_type=f32)
            g_ref[u] = jnp.concatenate([jnp.where(last, 1.0, hi), jnp.where(last, 0.0, mid)], axis=0).astype(bf16)

    def speeds(block, both_ref, g_ref):
        for u in range(unroll):
            l, e = entry(block * unroll + u)
            t = lt_ref[l, 0, e]
            both, g = both_ref[u], g_ref[u]
            inv = lax.rsqrt(both[:, 0:128])
            weight = inv * inv * inv
            iso = inv + weight
            pro = both[:, 128:256] * weight
            iso_hi, pro_hi = iso.astype(bf16), pro.astype(bf16)
            iso_lo = (iso - iso_hi.astype(f32)).astype(bf16)
            pro_lo = (pro - pro_hi.astype(f32)).astype(bf16)
            m = jnp.concatenate([
                jnp.concatenate([iso_hi, pro_hi], axis=1), jnp.concatenate([iso_lo, pro_lo], axis=1)], axis=0)
            out = jnp.dot(jnp.concatenate([g, g], axis=1), m, preferred_element_type=f32)
            out = out[0:8] + out[8:16]
            from_iso, from_pro = out[:, 0:128], out[:, 128:256]
            acc_ref[tile(t), :] += pltpu.roll(from_iso, 4, 0) + near_ref[tile(t), :] * from_pro[3:4] + 0.5 * from_pro

    def many(i, carry):
        distances(2 * i, both_a, g_a)
        speeds(2 * i - 1, both_b, g_b)
        distances(2 * i + 1, both_b, g_b)
        speeds(2 * i, both_a, g_a)
        return carry

    lax.fori_loop(0, (n + unroll - 1) // unroll // 2 + 1, many, 0)
    for c in range(ncol):
        for k in range(3):
            v_ref[c, k] = stokes_scale * acc_ref[pl.ds(c * local * 8 + k, local, stride=8), :]


def home_kernel(nrow, ncol, cap, pack_ref, from_ref, rank_ref, cnt_ref, v_ref, out_ref, got, part, home, outg, arr, vsend, vrecv, asend, arecv):
    row, col = lax.axis_index("row"), lax.axis_index("col")
    local = out_ref.shape[1]
    devs = nrow * ncol
    me = row * ncol + col
    barrier = pltpu.get_barrier_semaphore()

    def peer(d):
        p = lax.rem(me + d, devs)
        return {"row": p // ncol, "col": lax.rem(p, ncol)}

    for d in range(1, devs):
        pl.semaphore_signal(barrier, inc=1, device_id=peer(d), device_id_type=MESH)
    pl.semaphore_wait(barrier, devs - 1)
    half = ncol // 2
    core = lax.rem(col, 2)
    mine_x = col // 2
    within, across = [], []
    for d in [*range(1, half), 0]:
        x = lax.rem(mine_x + d, half)
        within.append(pltpu.make_async_remote_copy(
            src_ref=v_ref.at[2 * x + 1 - core], dst_ref=got.at[d], send_sem=vsend.at[d], recv_sem=vrecv.at[d],
            device_id={"col": col + 1 - 2 * core}, device_id_type=MESH))
    for copy in within:
        copy.start()
    for d in range(1, half):
        to = 2 * lax.rem(mine_x + d, half) + core
        within[d - 1].wait_recv()
        part[d - 1] = v_ref[to] + got[d]
        copy = pltpu.make_async_remote_copy(
            src_ref=part.at[d - 1], dst_ref=got.at[half + d - 1],
            send_sem=vsend.at[half + d - 1], recv_sem=vrecv.at[half + d - 1],
            device_id={"col": to}, device_id_type=MESH)
        copy.start()
        across.append(copy)
    within[half - 1].wait_recv()
    for copy in across:
        copy.wait_recv()
    for k in range(3):
        mine = v_ref[col, k] + got[0, k]
        for d in range(1, half):
            mine = mine + got[half + d - 1, k]
        home[:, k, :] = mine
    for copy in within + across:
        copy.wait_send()

    def pack(p, carry):
        for j in range(cap):
            one = home[pack_ref[0, p * cap + j]]
            for k in range(3):
                outg[p, k, j:j + 1, :] = one[k:k + 1]
        return carry

    lax.fori_loop(0, devs, pack, 0)
    copies = []
    for d in range(1, devs):
        copies.append(pltpu.make_async_remote_copy(
            src_ref=outg.at[lax.rem(me + d, devs)], dst_ref=arr.at[me],
            send_sem=asend.at[d - 1], recv_sem=arecv.at[d - 1],
            device_id=peer(d), device_id_type=MESH))
    for copy in copies:
        copy.start()
    arr[me] = outg[me]
    for copy in copies:
        copy.wait()
    slots = lax.broadcasted_iota(jnp.int32, (1, 128), 1)

    def unpack(i, carry):
        for u in range(8):
            n = i * 8 + u
            at, place = from_ref[0, n], rank_ref[0, n]
            live = slots < cnt_ref[0, n]
            for k in range(3):
                out_ref[k, pl.ds(n, 1), :] = jnp.where(live, arr[at, k, pl.ds(place, 1), :], 0.0)
        return carry

    lax.fori_loop(0, local // 8, unpack, 0)


def per_device(positions, normals, curvature, pair_targets, pair_sources, pair_count, node_counts, drop_clusters, drop_owner):
    local, _, nodes = positions.shape
    nrow, ncol = lax.axis_size("row"), lax.axis_size("col")
    devs = nrow * ncol
    cap = max(2, 2 * local // devs)
    slots = pair_targets.shape[1]
    dma = pltpu.SemaphoreType.DMA
    shape = jax.ShapeDtypeStruct
    near, right, far, lt, ls, lc, pack, anchor, place_in, owned_counts = pl.pallas_call(
        functools.partial(gather_kernel, nrow, ncol, cap),
        out_shape=(
            pltpu.VMEM((ncol * local * 8, nodes), f32), pltpu.VMEM((ncol * local, 32, nodes), bf16),
            pltpu.VMEM((2 * nrow * local * 8, nodes), f32),
            shape((2, 1, slots), ints), shape((2, 1, slots), ints), shape((2, 1, 128), ints),
            shape((1, devs * cap), ints), shape((1, local), ints), shape((1, local), ints), shape((1, local), ints)),
        in_specs=[VMEM] * 8 + [SMEM], out_specs=(VMEM,) * 10,
        scratch_shapes=[
            pltpu.VMEM((ncol, 3, local, nodes), f32), pltpu.VMEM((2, nrow, 6, local, nodes), f32),
            dma((ncol - 1,)), dma((ncol - 1,)), dma((nrow - 1, 6)), dma((nrow - 1, 6)), dma((nrow - 1, 6)), dma((nrow - 1, 6)),
            dma((6,)), dma((6,)), dma((3,)), dma((3,))],
        compiler_params=pltpu.CompilerParams(collective_id=0, has_side_effects=True, vmem_limit_bytes=24 << 20),
        name="gather_blocks",
    )(jnp.transpose(positions, (1, 0, 2)), jnp.transpose(normals, (1, 0, 2)), curvature, node_counts.T, drop_clusters.T,
      drop_owner[None, :], pair_targets, pair_sources, pair_count)
    speeds = pl.pallas_call(
        pair_kernel,
        out_shape=pltpu.VMEM((ncol, 3, local, nodes), f32),
        in_specs=[SMEM] * 3 + [VMEM] * 3, out_specs=VMEM,
        scratch_shapes=[pltpu.VMEM((ncol * local * 8, nodes), f32)]
        + [pltpu.VMEM((unroll, nodes, 2 * nodes), f32)] * 2 + [pltpu.VMEM((unroll, 16, nodes), bf16)] * 2,
        compiler_params=pltpu.CompilerParams(vmem_limit_bytes=24 << 20),
        name="pairs",
    )(lt, ls, lc, keep(near), keep(right), keep(far))
    owned = pl.pallas_call(
        functools.partial(home_kernel, nrow, ncol, cap),
        out_shape=jax.ShapeDtypeStruct((3, local, nodes), f32),
        in_specs=[SMEM] * 4 + [VMEM], out_specs=VMEM,
        scratch_shapes=[
            pltpu.VMEM((ncol - 1, 3, local, nodes), f32), pltpu.VMEM((max(ncol // 2 - 1, 1), 3, local, nodes), f32),
            pltpu.VMEM((local, 8, nodes), f32),
            pltpu.VMEM((devs, 3, cap, nodes), f32), pltpu.VMEM((devs, 3, cap, nodes), f32),
            dma((ncol - 1,)), dma((ncol - 1,)), dma((devs - 1,)), dma((devs - 1,)),
        ],
        compiler_params=pltpu.CompilerParams(collective_id=1, has_side_effects=True, vmem_limit_bytes=24 << 20),
        name="to_owners",
    )(pack, anchor, place_in, owned_counts, keep(speeds))
    return jnp.transpose(owned, (1, 0, 2))


def solution(mesh):
    every = ("groups", "row", "col")
    in_specs = (
        P(every, None, None), P(every, None, None), P(every, None), P(every, None), P(every, None), P(every),
        P("groups", None), P("groups", None), P("groups"),
    )
    return jax.shard_map(per_device, mesh=mesh, in_specs=in_specs, out_specs=P(every, None, None), check_vma=False)
```

```python
import functools
import math

import jax
import jax.numpy as jnp
from jax import lax
from jax.experimental import pallas as pl
from jax.experimental.pallas import tpu as pltpu
from jax.sharding import PartitionSpec as P

regular_sq = 0.0025
inv_reg = 1.0 / math.sqrt(regular_sq)
stokes_scale = inv_reg / (8.0 * math.pi)
MESH = pl.DeviceIdType.MESH
VMEM = pl.BlockSpec(memory_space=pltpu.VMEM)
SMEM = pl.BlockSpec(memory_space=pltpu.SMEM)


HBM = pl.BlockSpec(memory_space=pltpu.HBM)
unroll = 16
f32, bf16, ints = jnp.float32, jnp.bfloat16, jnp.int32


def keep(x):
    return pltpu.with_memory_space_constraint(x, pltpu.VMEM)


def far_off(x):
    return pltpu.with_memory_space_constraint(x, pltpu.HBM)


def split3(x):
    high = x.astype(bf16).astype(f32)
    rest = x - high
    middle = rest.astype(bf16).astype(f32)
    return high, middle, rest - middle


def as_row(column):
    return jnp.transpose(jnp.broadcast_to(column, (column.shape[0], 128)))[0:1]


def gather_kernel(
        nrow, ncol, cap, pos_in, nrm_in, curv_in, nct_in, dct_in, own_in, tgt_in, src_in, count_ref,
        near_ref, right_ref, far_ref, lt_ref, ls_ref, lc_ref, pack_ref, from_ref, rank_ref, cnt_ref,
        nrm_ref, curv_ref, nct_ref, dct_ref, own_ref, here_sem, t_ref, s_ref, tsend, trecv, zsend, zrecv, fsend, frecv, osend, orecv, lsend, lrecv):
    row, col = lax.axis_index("row"), lax.axis_index("col")
    core = lax.rem(col, 2)
    other = col + 1 - 2 * core
    me = row * ncol + col
    local = pos_in.shape[1]
    drops = own_ref.shape[1]
    per_drop = dct_ref.shape[0]
    pos_ref = s_ref.at[core, row, 0:3]
    loads = [pltpu.make_async_copy(src, dst, here_sem.at[i]) for i, (src, dst) in enumerate((
        (pos_in, pos_ref), (dct_in, dct_ref), (nct_in, nct_ref), (own_in, own_ref), (curv_in, curv_ref), (nrm_in, nrm_ref),
        (tgt_in, lt_ref.at[core]), (src_in, ls_ref.at[core])))]
    for load in loads:
        load.start()
    barrier = pltpu.get_barrier_semaphore()
    for d in range(1, nrow):
        pl.semaphore_signal(barrier, inc=1, device_id={"row": lax.rem(row + d, nrow)}, device_id_type=MESH)
    for d in range(1, ncol):
        pl.semaphore_signal(barrier, inc=1, device_id={"col": lax.rem(col + d, ncol)}, device_id_type=MESH)
    lc_ref[core] = jnp.full((1, 128), count_ref[0], ints)

    def remote(src, dst, send, recv, where):
        return pltpu.make_async_remote_copy(
            src_ref=src, dst_ref=dst, send_sem=send, recv_sem=recv, device_id=where, device_id_type=MESH)

    sibling = {"col": other}
    small = [remote(ref.at[core], ref.at[core], lsend.at[i], lrecv.at[i], sibling)
             for i, ref in enumerate((lt_ref, ls_ref, lc_ref))]
    rows = [remote(pos_ref, t_ref.at[col], tsend.at[d - 1], trecv.at[d - 1], {"col": lax.rem(col + d, ncol)})
            for d in range(1, ncol)]

    def block_of(way, step):
        return jnp.clip(row - way * step, 0, nrow - 1)

    def relay(way, step, k):
        piece = s_ref.at[core, block_of(way, step), k]
        at = step if way > 0 else nrow - 1 + step
        return remote(piece, piece, zsend.at[at, k], zrecv.at[at, k], {"row": jnp.clip(row + way, 0, nrow - 1)})

    def sends(way, step):
        return (row < nrow - 1) & (row >= step) if way > 0 else (row > 0) & (row + step < nrow)

    def receives(way, step):
        return row >= step + 1 if way > 0 else row + step + 1 < nrow

    def onward(way, step, k):
        piece = s_ref.at[core, block_of(way, step + 1), k]
        at = step if way > 0 else nrow - 1 + step
        return remote(piece, piece, fsend.at[at, k], frecv.at[at, k], sibling)

    def start(way, step, k):
        @pl.when(sends(way, step))
        def _():
            relay(way, step, k).start()

    def own(k):
        piece = s_ref.at[core, row, k]
        return remote(piece, piece, osend.at[k], orecv.at[k], sibling)

    loads[0].wait()
    pl.semaphore_wait(barrier, nrow + ncol - 2)
    for k in range(3):
        for way in (1, -1):
            start(way, 0, k)
    for copy in rows:
        copy.start()
    for load in loads[1:]:
        load.wait()
    for copy in small:
        copy.start()

    index = lax.broadcasted_iota(ints, (local, 1), 0)
    ids = me * local + index

    def match(chunk, carry):
        counts, owners = carry
        lanes = pl.ds(pl.multiple_of(chunk * 128, 128), 128)
        clusters, nodes_in, owner = dct_ref[:, lanes], nct_ref[:, lanes], own_ref[0:1, lanes]
        for k in range(per_drop):
            hit = ids == clusters[k:k + 1]
            counts = counts + jnp.where(hit, nodes_in[k:k + 1], 0)
            owners = owners + jnp.where(hit, owner, 0)
        return counts, owners

    none = jnp.zeros((local, 128), ints)
    counts, owners = lax.fori_loop(0, drops // 128, match, (none, none))
    home_counts = jnp.sum(counts, axis=1, keepdims=True, dtype=ints)
    home_owner = jnp.sum(owners, axis=1, keepdims=True, dtype=ints)
    scale = jnp.where(lax.broadcasted_iota(ints, (local, 128), 1) < home_counts, curv_ref[...], 0.0)
    for k in range(3):
        s_ref[core, row, 3 + k] = scale * nrm_ref[k]
        for way in (1, -1):
            start(way, 0, 3 + k)
    for k in range(6):
        own(k).start()

    owner_row = as_row(home_owner.astype(f32)).astype(ints)
    lane = lax.broadcasted_iota(ints, (local, local), 1)
    rank = jnp.sum(((owner_row == home_owner) & (lane < index)).astype(ints), axis=1, keepdims=True, dtype=ints)
    slot = home_owner * cap + rank
    slots = lax.broadcasted_iota(ints, pack_ref.shape, 1)
    pack_ref[...] = jnp.sum(jnp.where(slot == slots, index, 0), axis=0, keepdims=True, dtype=ints)

    here = lax.broadcasted_iota(ints, (local, 1), 0)
    drop_of = lax.div(here, per_drop)
    width = 256 if drops % 256 == 0 else 128
    before = (lax.broadcasted_iota(ints, (width, width), 0) < lax.broadcasted_iota(ints, (width, width), 1)).astype(bf16)

    def owned(chunk, carry):
        clusters, counted, base = carry
        lanes = pl.ds(pl.multiple_of(chunk * width, width), width)
        mine = own_ref[0:1, lanes] == me
        marks = jnp.broadcast_to(mine.astype(f32), (16, width)).astype(bf16)
        place = jnp.dot(marks, before, preferred_element_type=f32)[0:1].astype(ints) + base
        chosen = mine & (place == drop_of)
        clusters = clusters + jnp.where(chosen, jnp.concatenate([dct_ref[:, lanes]] * (local // per_drop), axis=0), 0)
        counted = counted + jnp.where(chosen, jnp.concatenate([nct_ref[:, lanes]] * (local // per_drop), axis=0), 0)
        return clusters, counted, base + jnp.sum(mine.astype(ints), axis=1, keepdims=True, dtype=ints)

    wide = jnp.zeros((local, width), ints)
    clusters, counted, _ = lax.fori_loop(0, drops // width, owned, (wide, wide, jnp.zeros((1, 1), ints)))
    clusters = jnp.sum(clusters, axis=1, keepdims=True, dtype=ints)
    cnt_ref[...] = as_row(jnp.sum(counted, axis=1, keepdims=True, dtype=ints).astype(f32)).astype(ints)
    clusters_row = as_row(clusters.astype(f32)).astype(ints)
    anchor, anchor_row = lax.div(clusters, local), lax.div(clusters_row, local)
    from_ref[...] = anchor_row
    rank_ref[...] = jnp.sum(((anchor == anchor_row) & (clusters < clusters_row)).astype(ints), axis=0, keepdims=True, dtype=ints)

    def fill(i, carry):
        base = pl.multiple_of(i * 64, 64)
        far_ref[pl.ds(base, 64), :] = jnp.zeros((64, 128), f32)
        return carry

    lax.fori_loop(0, far_ref.shape[0] // 64, fill, 0)

    def spread(l, r, k):
        at = (l * nrow + r) * local * 8 + (k if k < 3 else k + 1)
        far_ref[pl.ds(at, local, stride=8), :] = s_ref[l, r, k]

    for k in range(6):
        spread(core, row, k)

    sub = lax.broadcasted_iota(ints, (8, 128), 0)
    low = sub < 4

    def targets(d):
        c = lax.rem(col + ncol - d, ncol)
        square = jnp.ones((local, 128), f32)
        start = c * local * 8
        for k in range(3):
            coord = s_ref[core, row, k] if d == 0 else t_ref[c, k]
            centre = jnp.mean(coord, axis=1, keepdims=True)
            coord = (coord - centre) * inv_reg
            square = square + coord * coord
            near_ref[pl.ds(start + k, local, stride=8), :] = coord
            near_ref[pl.ds(start + 4 + k, local, stride=8), :] = jnp.broadcast_to(centre, coord.shape)
        near_ref[pl.ds(start + 3, local, stride=8), :] = square
        near_ref[pl.ds(start + 7, local, stride=8), :] = jnp.zeros((local, 128), f32)

        def coefficients(i, carry):
            for u in range(8):
                t = c * local + i * 8 + u
                tile = near_ref[pl.ds(pl.multiple_of(t * 8, 8), 8), :]
                high, middle, rest = split3(tile)
                sums = jnp.where(sub == 0, high[3:4], jnp.where(sub == 1, middle[3:4], jnp.where(sub == 2, rest[3:4], 0.0)))
                high = jnp.where(sub < 3, high, jnp.where(sub == 3, 1.0, 0.0))
                middle = jnp.where(sub < 3, middle, 0.0)
                rest = jnp.where(sub < 3, rest, 0.0)
                high_up, middle_up = pltpu.roll(high, 4, 0), pltpu.roll(middle, 4, 0)
                right_ref[t] = jnp.concatenate([
                    high + middle_up, rest + high_up, middle + high_up, sums], axis=0).astype(bf16)
            return carry

        lax.fori_loop(0, local // 8, coefficients, 0)

    targets(0)
    for d in range(1, ncol):
        rows[d - 1].wait_recv()
        targets(d)
    for k in range(6):
        own(k).wait_recv()
        spread(1 - core, row, k)
    for step in range(nrow - 1):
        for k in range(6):
            for way in (1, -1):
                @pl.when(receives(way, step))
                def _():
                    relay(way, step, k).wait_recv()
                    if step < nrow - 2:
                        start(way, step + 1, k)
                    onward(way, step, k).start()
                    spread(core, block_of(way, step + 1), k)
    for step in range(nrow - 1):
        for k in range(6):
            for way in (1, -1):
                @pl.when(receives(way, step))
                def _():
                    onward(way, step, k).wait_recv()
                    spread(1 - core, block_of(way, step + 1), k)
    for copy in small:
        copy.wait()
    for copy in rows:
        copy.wait_send()
    for k in range(6):
        own(k).wait_send()
        for step in range(nrow - 1):
            for way in (1, -1):
                @pl.when(sends(way, step))
                def _():
                    relay(way, step, k).wait_send()

                @pl.when(receives(way, step))
                def _():
                    onward(way, step, k).wait_send()


def pair_kernel(lt_ref, ls_ref, lc_ref, near_ref, right_ref, far_ref, v_ref, acc_ref, both_a, both_b, g_a, g_b):
    ncol, _, local, _ = v_ref.shape
    half_far = far_ref.shape[0] // 16
    core = lax.rem(lax.axis_index("col"), 2)
    sub = lax.broadcasted_iota(ints, (8, 128), 0)
    low = sub < 4
    last = (sub == 3) | (sub == 7)
    scale = jnp.where(low, -2.0, 1.0).astype(f32)
    fold = jnp.where(sub == 3, 1.0, jnp.where(sub == 7, -1.0, 0.0)).astype(f32)
    some = jnp.where(low, 1.0, 0.0).astype(f32)
    unit = jnp.where(low, inv_reg, 1.0).astype(f32)
    idle = jnp.where(low, inv_reg, 0.0).astype(f32)
    nothing = jnp.zeros((32, 128), bf16)
    acc_ref[...] = jnp.zeros_like(acc_ref)
    both_b[...] = jnp.ones_like(both_b)
    g_b[...] = jnp.zeros_like(g_b)
    n0 = lc_ref[0, 0, 0]
    total = n0 + lc_ref[1, 0, 0]
    half = (total + 1) // 2
    first = core * half
    n = jnp.where(core == 0, half, total - half)

    def entry(j):
        j = first + jnp.clip(j, 0, n - 1)
        second = j >= n0
        return second.astype(ints), jnp.where(second, j - n0, j)

    def tile(i):
        return pl.ds(pl.multiple_of(i * 8, 8), 8)

    def distances(block, both_ref, g_ref):
        for u in range(unroll):
            j = block * unroll + u
            l, e = entry(j)
            t, s = lt_ref[l, 0, e], ls_ref[l, 0, e] + l * half_far
            centre = jnp.where(low, pltpu.roll(near_ref[tile(t), :], 4, 0), 0.0)
            right = right_ref[t]
            shifted = (far_ref[tile(s), :] - centre) * jnp.where(j < n, unit, idle)
            prod = shifted * jnp.where(low, shifted, pltpu.roll(shifted, 4, 0))
            prod = prod + pltpu.roll(prod, 1, 0)
            prod = prod + pltpu.roll(prod, 2, 0)
            hi, mid, lo = split3(shifted * scale + prod * fold)
            hi_up, mid_up, lo_up = pltpu.roll(hi, 4, 0), pltpu.roll(mid, 4, 0), pltpu.roll(lo, 4, 0)
            left = jnp.concatenate([
                jnp.where(low, hi, hi_up), jnp.where(low, hi, mid_up), jnp.where(low, mid, lo_up), some,
                jnp.where(low, hi_up, hi), jnp.where(low, hi_up, mid), jnp.where(low, mid_up, lo),
                jnp.zeros((8, 128), f32)], axis=0).astype(bf16)
            weights = jnp.concatenate([
                jnp.concatenate([right, nothing], axis=1), jnp.concatenate([nothing, right], axis=1)], axis=0)
            both_ref[u] = lax.dot_general(left, weights, (((0,), (0,)), ((), ())), preferred_element_type=f32)
            g_ref[u] = jnp.concatenate([jnp.where(last, 1.0, hi), jnp.where(last, 0.0, mid)], axis=0).astype(bf16)

    def speeds(block, both_ref, g_ref):
        for u in range(unroll):
            l, e = entry(block * unroll + u)
            t = lt_ref[l, 0, e]
            both, g = both_ref[u], g_ref[u]
            inv = lax.rsqrt(both[:, 0:128])
            weight = inv * inv * inv
            iso = inv + weight
            pro = both[:, 128:256] * weight
            iso_hi, pro_hi = iso.astype(bf16), pro.astype(bf16)
            iso_lo = (iso - iso_hi.astype(f32)).astype(bf16)
            pro_lo = (pro - pro_hi.astype(f32)).astype(bf16)
            m = jnp.concatenate([
                jnp.concatenate([iso_hi, pro_hi], axis=1), jnp.concatenate([iso_lo, pro_lo], axis=1)], axis=0)
            out = jnp.dot(jnp.concatenate([g, g], axis=1), m, preferred_element_type=f32)
            out = out[0:8] + out[8:16]
            from_iso, from_pro = out[:, 0:128], out[:, 128:256]
            acc_ref[tile(t), :] += pltpu.roll(from_iso, 4, 0) + near_ref[tile(t), :] * from_pro[3:4] + 0.5 * from_pro

    def many(i, carry):
        distances(2 * i, both_a, g_a)
        speeds(2 * i - 1, both_b, g_b)
        distances(2 * i + 1, both_b, g_b)
        speeds(2 * i, both_a, g_a)
        return carry

    lax.fori_loop(0, (n + unroll - 1) // unroll // 2 + 1, many, 0)
    for c in range(ncol):
        for k in range(3):
            v_ref[c, k] = stokes_scale * acc_ref[pl.ds(c * local * 8 + k, local, stride=8), :]


def home_kernel(nrow, ncol, cap, pack_ref, from_ref, rank_ref, cnt_ref, v_ref, out_ref, got, part, home, outg, arr, vsend, vrecv, asend, arecv):
    row, col = lax.axis_index("row"), lax.axis_index("col")
    local = out_ref.shape[1]
    devs = nrow * ncol
    me = row * ncol + col
    barrier = pltpu.get_barrier_semaphore()

    def peer(d):
        p = lax.rem(me + d, devs)
        return {"row": p // ncol, "col": lax.rem(p, ncol)}

    for d in range(1, devs):
        pl.semaphore_signal(barrier, inc=1, device_id=peer(d), device_id_type=MESH)
    pl.semaphore_wait(barrier, devs - 1)
    half = ncol // 2
    core = lax.rem(col, 2)
    mine_x = col // 2
    within, across = [], []
    for d in [*range(1, half), 0]:
        x = lax.rem(mine_x + d, half)
        within.append(pltpu.make_async_remote_copy(
            src_ref=v_ref.at[2 * x + 1 - core], dst_ref=got.at[d], send_sem=vsend.at[d], recv_sem=vrecv.at[d],
            device_id={"col": col + 1 - 2 * core}, device_id_type=MESH))
    for copy in within:
        copy.start()
    for d in range(1, half):
        to = 2 * lax.rem(mine_x + d, half) + core
        within[d - 1].wait_recv()
        part[d - 1] = v_ref[to] + got[d]
        copy = pltpu.make_async_remote_copy(
            src_ref=part.at[d - 1], dst_ref=got.at[half + d - 1],
            send_sem=vsend.at[half + d - 1], recv_sem=vrecv.at[half + d - 1],
            device_id={"col": to}, device_id_type=MESH)
        copy.start()
        across.append(copy)
    within[half - 1].wait_recv()
    for copy in across:
        copy.wait_recv()
    for k in range(3):
        mine = v_ref[col, k] + got[0, k]
        for d in range(1, half):
            mine = mine + got[half + d - 1, k]
        home[:, k, :] = mine
    for copy in within + across:
        copy.wait_send()

    def pack(p, carry):
        for j in range(cap):
            one = home[pack_ref[0, p * cap + j]]
            for k in range(3):
                outg[p, k, j:j + 1, :] = one[k:k + 1]
        return carry

    lax.fori_loop(0, devs, pack, 0)
    copies = []
    for d in range(1, devs):
        copies.append(pltpu.make_async_remote_copy(
            src_ref=outg.at[lax.rem(me + d, devs)], dst_ref=arr.at[me],
            send_sem=asend.at[d - 1], recv_sem=arecv.at[d - 1],
            device_id=peer(d), device_id_type=MESH))
    for copy in copies:
        copy.start()
    arr[me] = outg[me]
    for copy in copies:
        copy.wait()
    slots = lax.broadcasted_iota(jnp.int32, (1, 128), 1)

    def unpack(i, carry):
        for u in range(8):
            n = i * 8 + u
            at, place = from_ref[0, n], rank_ref[0, n]
            live = slots < cnt_ref[0, n]
            for k in range(3):
                out_ref[k, pl.ds(n, 1), :] = jnp.where(live, arr[at, k, pl.ds(place, 1), :], 0.0)
        return carry

    lax.fori_loop(0, local // 8, unpack, 0)


def per_device(positions, normals, curvature, pair_targets, pair_sources, pair_count, node_counts, drop_clusters, drop_owner):
    local, _, nodes = positions.shape
    nrow, ncol = lax.axis_size("row"), lax.axis_size("col")
    devs = nrow * ncol
    cap = max(2, 2 * local // devs)
    slots = pair_targets.shape[1]
    dma = pltpu.SemaphoreType.DMA
    shape = jax.ShapeDtypeStruct
    near, right, far, lt, ls, lc, pack, anchor, place_in, owned_counts = pl.pallas_call(
        functools.partial(gather_kernel, nrow, ncol, cap),
        out_shape=(
            pltpu.VMEM((ncol * local * 8, nodes), f32), pltpu.VMEM((ncol * local, 32, nodes), bf16),
            pltpu.VMEM((2 * nrow * local * 8, nodes), f32),
            shape((2, 1, slots), ints), shape((2, 1, slots), ints), shape((2, 1, 128), ints),
            shape((1, devs * cap), ints), shape((1, local), ints), shape((1, local), ints), shape((1, local), ints)),
        in_specs=[HBM] * 8 + [SMEM], out_specs=(VMEM,) * 10,
        scratch_shapes=[
            pltpu.VMEM((3, local, nodes), f32), pltpu.VMEM((local, nodes), f32), *[pltpu.VMEM(drop_clusters.shape[::-1], ints)] * 2,
            pltpu.VMEM((1, drop_owner.shape[0]), ints), dma((8,)),
            pltpu.VMEM((ncol, 3, local, nodes), f32), pltpu.VMEM((2, nrow, 6, local, nodes), f32),
            dma((ncol - 1,)), dma((ncol - 1,)), *[dma((2 * nrow - 2, 6))] * 4,
            dma((6,)), dma((6,)), dma((3,)), dma((3,))],
        compiler_params=pltpu.CompilerParams(collective_id=0, has_side_effects=True, vmem_limit_bytes=24 << 20),
        name="gather_blocks",
    )(*map(far_off, (jnp.transpose(positions, (1, 0, 2)), jnp.transpose(normals, (1, 0, 2)), curvature, node_counts.T,
                     drop_clusters.T, drop_owner[None, :], pair_targets, pair_sources)), pair_count)
    speeds = pl.pallas_call(
        pair_kernel,
        out_shape=pltpu.VMEM((ncol, 3, local, nodes), f32),
        in_specs=[SMEM] * 3 + [VMEM] * 3, out_specs=VMEM,
        scratch_shapes=[pltpu.VMEM((ncol * local * 8, nodes), f32)]
        + [pltpu.VMEM((unroll, nodes, 2 * nodes), f32)] * 2 + [pltpu.VMEM((unroll, 16, nodes), bf16)] * 2,
        compiler_params=pltpu.CompilerParams(vmem_limit_bytes=24 << 20),
        name="pairs",
    )(lt, ls, lc, keep(near), keep(right), keep(far))
    owned = pl.pallas_call(
        functools.partial(home_kernel, nrow, ncol, cap),
        out_shape=jax.ShapeDtypeStruct((3, local, nodes), f32),
        in_specs=[SMEM] * 4 + [VMEM], out_specs=VMEM,
        scratch_shapes=[
            pltpu.VMEM((ncol - 1, 3, local, nodes), f32), pltpu.VMEM((max(ncol // 2 - 1, 1), 3, local, nodes), f32),
            pltpu.VMEM((local, 8, nodes), f32),
            pltpu.VMEM((devs, 3, cap, nodes), f32), pltpu.VMEM((devs, 3, cap, nodes), f32),
            dma((ncol - 1,)), dma((ncol - 1,)), dma((devs - 1,)), dma((devs - 1,)),
        ],
        compiler_params=pltpu.CompilerParams(collective_id=1, has_side_effects=True, vmem_limit_bytes=24 << 20),
        name="to_owners",
    )(pack, anchor, place_in, owned_counts, keep(speeds))
    return jnp.transpose(owned, (1, 0, 2))


def solution(mesh):
    every = ("groups", "row", "col")
    in_specs = (
        P(every, None, None), P(every, None, None), P(every, None), P(every, None), P(every, None), P(every),
        P("groups", None), P("groups", None), P("groups"),
    )
    return jax.shard_map(per_device, mesh=mesh, in_specs=in_specs, out_specs=P(every, None, None), check_vma=False)
```

```python
import functools
import math

import jax
import jax.numpy as jnp
from jax import lax
from jax.experimental import pallas as pl
from jax.experimental.pallas import tpu as pltpu
from jax.sharding import PartitionSpec as P

regular_sq = 0.0025
inv_reg = 1.0 / math.sqrt(regular_sq)
stokes_scale = inv_reg / (8.0 * math.pi)
MESH = pl.DeviceIdType.MESH
VMEM = pl.BlockSpec(memory_space=pltpu.VMEM)
SMEM = pl.BlockSpec(memory_space=pltpu.SMEM)


HBM = pl.BlockSpec(memory_space=pltpu.HBM)
unroll = 16
f32, bf16, ints = jnp.float32, jnp.bfloat16, jnp.int32


def keep(x):
    return pltpu.with_memory_space_constraint(x, pltpu.VMEM)


def far_off(x):
    return pltpu.with_memory_space_constraint(x, pltpu.HBM)


def split3(x):
    high = x.astype(bf16).astype(f32)
    rest = x - high
    middle = rest.astype(bf16).astype(f32)
    return high, middle, rest - middle


def as_row(column):
    return jnp.transpose(jnp.broadcast_to(column, (column.shape[0], 128)))[0:1]


def gather_kernel(
        nrow, ncol, cap, pos_in, nrm_in, curv_in, nct_in, dct_in, own_in, tgt_in, src_in, count_ref,
        near_ref, right_ref, far_ref, lt_ref, ls_ref, lc_ref, slot_ref, place_ref, cnt_ref,
        nrm_ref, curv_ref, nct_ref, dct_ref, own_ref, here_sem, t_ref, s_ref, tsend, trecv, zsend, zrecv, fsend, frecv, osend, orecv, lsend, lrecv):
    row, col = lax.axis_index("row"), lax.axis_index("col")
    core = lax.rem(col, 2)
    other = col + 1 - 2 * core
    me = row * ncol + col
    local = pos_in.shape[1]
    drops = own_ref.shape[1]
    per_drop = dct_ref.shape[0]
    pos_ref = s_ref.at[core, row, 0:3]
    loads = [pltpu.make_async_copy(src, dst, here_sem.at[i]) for i, (src, dst) in enumerate((
        (pos_in, pos_ref), (dct_in, dct_ref), (nct_in, nct_ref), (own_in, own_ref), (curv_in, curv_ref), (nrm_in, nrm_ref),
        (tgt_in, lt_ref.at[core]), (src_in, ls_ref.at[core])))]
    for load in loads:
        load.start()
    barrier = pltpu.get_barrier_semaphore()
    for d in range(1, nrow):
        pl.semaphore_signal(barrier, inc=1, device_id={"row": lax.rem(row + d, nrow)}, device_id_type=MESH)
    for d in range(1, ncol):
        pl.semaphore_signal(barrier, inc=1, device_id={"col": lax.rem(col + d, ncol)}, device_id_type=MESH)
    lc_ref[core] = jnp.full((1, 128), count_ref[0], ints)

    def remote(src, dst, send, recv, where):
        return pltpu.make_async_remote_copy(
            src_ref=src, dst_ref=dst, send_sem=send, recv_sem=recv, device_id=where, device_id_type=MESH)

    sibling = {"col": other}
    small = [remote(ref.at[core], ref.at[core], lsend.at[i], lrecv.at[i], sibling)
             for i, ref in enumerate((lt_ref, ls_ref, lc_ref))]
    rows = [remote(pos_ref, t_ref.at[col], tsend.at[d - 1], trecv.at[d - 1], {"col": lax.rem(col + d, ncol)})
            for d in range(1, ncol)]

    def block_of(way, step):
        return jnp.clip(row - way * step, 0, nrow - 1)

    def relay(way, step, k):
        piece = s_ref.at[core, block_of(way, step), k]
        at = step if way > 0 else nrow - 1 + step
        return remote(piece, piece, zsend.at[at, k], zrecv.at[at, k], {"row": jnp.clip(row + way, 0, nrow - 1)})

    def sends(way, step):
        return (row < nrow - 1) & (row >= step) if way > 0 else (row > 0) & (row + step < nrow)

    def receives(way, step):
        return row >= step + 1 if way > 0 else row + step + 1 < nrow

    def onward(way, step, k):
        piece = s_ref.at[core, block_of(way, step + 1), k]
        at = step if way > 0 else nrow - 1 + step
        return remote(piece, piece, fsend.at[at, k], frecv.at[at, k], sibling)

    def start(way, step, k):
        @pl.when(sends(way, step))
        def _():
            relay(way, step, k).start()

    def own(k):
        piece = s_ref.at[core, row, k]
        return remote(piece, piece, osend.at[k], orecv.at[k], sibling)

    loads[0].wait()
    pl.semaphore_wait(barrier, nrow + ncol - 2)
    for k in range(3):
        for way in (1, -1):
            start(way, 0, k)
    for copy in rows:
        copy.start()
    for load in loads[1:]:
        load.wait()
    for copy in small:
        copy.start()

    index = lax.broadcasted_iota(ints, (local, 1), 0)
    ids = me * local + index

    def match(chunk, carry):
        counts, owners = carry
        lanes = pl.ds(pl.multiple_of(chunk * 128, 128), 128)
        clusters, nodes_in, owner = dct_ref[:, lanes], nct_ref[:, lanes], own_ref[0:1, lanes]
        for k in range(per_drop):
            hit = ids == clusters[k:k + 1]
            counts = counts + jnp.where(hit, nodes_in[k:k + 1], 0)
            owners = owners + jnp.where(hit, owner, 0)
        return counts, owners

    none = jnp.zeros((local, 128), ints)
    counts, owners = lax.fori_loop(0, drops // 128, match, (none, none))
    home_counts = jnp.sum(counts, axis=1, keepdims=True, dtype=ints)
    home_owner = jnp.sum(owners, axis=1, keepdims=True, dtype=ints)
    scale = jnp.where(lax.broadcasted_iota(ints, (local, 128), 1) < home_counts, curv_ref[...], 0.0)
    for k in range(3):
        s_ref[core, row, 3 + k] = scale * nrm_ref[k]
        for way in (1, -1):
            start(way, 0, 3 + k)
    for k in range(6):
        own(k).start()

    owner_row = as_row(home_owner.astype(f32)).astype(ints)
    lane = lax.broadcasted_iota(ints, (local, local), 1)
    rank = jnp.sum(((owner_row == home_owner) & (lane < index)).astype(ints), axis=1, keepdims=True, dtype=ints)
    slot_ref[...] = as_row((home_owner * cap + rank).astype(f32)).astype(ints)

    here = lax.broadcasted_iota(ints, (local, 1), 0)
    drop_of = lax.div(here, per_drop)
    width = 256 if drops % 256 == 0 else 128
    before = (lax.broadcasted_iota(ints, (width, width), 0) < lax.broadcasted_iota(ints, (width, width), 1)).astype(bf16)

    def owned(chunk, carry):
        clusters, counted, base = carry
        lanes = pl.ds(pl.multiple_of(chunk * width, width), width)
        mine = own_ref[0:1, lanes] == me
        marks = jnp.broadcast_to(mine.astype(f32), (16, width)).astype(bf16)
        place = jnp.dot(marks, before, preferred_element_type=f32)[0:1].astype(ints) + base
        chosen = mine & (place == drop_of)
        clusters = clusters + jnp.where(chosen, jnp.concatenate([dct_ref[:, lanes]] * (local // per_drop), axis=0), 0)
        counted = counted + jnp.where(chosen, jnp.concatenate([nct_ref[:, lanes]] * (local // per_drop), axis=0), 0)
        return clusters, counted, base + jnp.sum(mine.astype(ints), axis=1, keepdims=True, dtype=ints)

    wide = jnp.zeros((local, width), ints)
    clusters, counted, _ = lax.fori_loop(0, drops // width, owned, (wide, wide, jnp.zeros((1, 1), ints)))
    clusters = jnp.sum(clusters, axis=1, keepdims=True, dtype=ints)
    cnt_ref[...] = jnp.sum(counted, axis=1, keepdims=True, dtype=ints)
    clusters_row = as_row(clusters.astype(f32)).astype(ints)
    anchor, anchor_row = lax.div(clusters, local), lax.div(clusters_row, local)
    same = (anchor == anchor_row) & (clusters_row < clusters)
    place_ref[...] = anchor * cap + jnp.sum(same.astype(ints), axis=1, keepdims=True, dtype=ints)

    def fill(i, carry):
        base = pl.multiple_of(i * 64, 64)
        far_ref[pl.ds(base, 64), :] = jnp.zeros((64, 128), f32)
        return carry

    lax.fori_loop(0, far_ref.shape[0] // 64, fill, 0)

    def spread(l, r, k):
        at = (l * nrow + r) * local * 8 + (k if k < 3 else k + 1)
        far_ref[pl.ds(at, local, stride=8), :] = s_ref[l, r, k]

    for k in range(6):
        spread(core, row, k)

    sub = lax.broadcasted_iota(ints, (8, 128), 0)
    low = sub < 4

    def targets(d):
        c = lax.rem(col + ncol - d, ncol)
        square = jnp.ones((local, 128), f32)
        start = c * local * 8
        for k in range(3):
            coord = s_ref[core, row, k] if d == 0 else t_ref[c, k]
            centre = jnp.mean(coord, axis=1, keepdims=True)
            coord = (coord - centre) * inv_reg
            square = square + coord * coord
            near_ref[pl.ds(start + k, local, stride=8), :] = coord
            near_ref[pl.ds(start + 4 + k, local, stride=8), :] = jnp.broadcast_to(centre, coord.shape)
        near_ref[pl.ds(start + 3, local, stride=8), :] = square
        near_ref[pl.ds(start + 7, local, stride=8), :] = jnp.zeros((local, 128), f32)

        def coefficients(i, carry):
            for u in range(8):
                t = c * local + i * 8 + u
                tile = near_ref[pl.ds(pl.multiple_of(t * 8, 8), 8), :]
                high, middle, rest = split3(tile)
                sums = jnp.where(sub == 0, high[3:4], jnp.where(sub == 1, middle[3:4], jnp.where(sub == 2, rest[3:4], 0.0)))
                high = jnp.where(sub < 3, high, jnp.where(sub == 3, 1.0, 0.0))
                middle = jnp.where(sub < 3, middle, 0.0)
                rest = jnp.where(sub < 3, rest, 0.0)
                high_up, middle_up = pltpu.roll(high, 4, 0), pltpu.roll(middle, 4, 0)
                right_ref[t] = jnp.concatenate([
                    high + middle_up, rest + high_up, middle + high_up, sums], axis=0).astype(bf16)
            return carry

        lax.fori_loop(0, local // 8, coefficients, 0)

    targets(0)
    for d in range(1, ncol):
        rows[d - 1].wait_recv()
        targets(d)
    for k in range(6):
        own(k).wait_recv()
        spread(1 - core, row, k)
    for step in range(nrow - 1):
        for k in range(6):
            for way in (1, -1):
                @pl.when(receives(way, step))
                def _():
                    relay(way, step, k).wait_recv()
                    if step < nrow - 2:
                        start(way, step + 1, k)
                    onward(way, step, k).start()
                    spread(core, block_of(way, step + 1), k)
    for step in range(nrow - 1):
        for k in range(6):
            for way in (1, -1):
                @pl.when(receives(way, step))
                def _():
                    onward(way, step, k).wait_recv()
                    spread(1 - core, block_of(way, step + 1), k)
    for copy in small:
        copy.wait()
    for copy in rows:
        copy.wait_send()
    for k in range(6):
        own(k).wait_send()
        for step in range(nrow - 1):
            for way in (1, -1):
                @pl.when(sends(way, step))
                def _():
                    relay(way, step, k).wait_send()

                @pl.when(receives(way, step))
                def _():
                    onward(way, step, k).wait_send()


def pair_kernel(lt_ref, ls_ref, lc_ref, near_ref, right_ref, far_ref, v_ref, acc_ref, both_a, both_b, g_a, g_b):
    ncol, _, local, _ = v_ref.shape
    half_far = far_ref.shape[0] // 16
    core = lax.rem(lax.axis_index("col"), 2)
    sub = lax.broadcasted_iota(ints, (8, 128), 0)
    low = sub < 4
    last = (sub == 3) | (sub == 7)
    scale = jnp.where(low, -2.0, 1.0).astype(f32)
    fold = jnp.where(sub == 3, 1.0, jnp.where(sub == 7, -1.0, 0.0)).astype(f32)
    some = jnp.where(low, 1.0, 0.0).astype(f32)
    unit = jnp.where(low, inv_reg, 1.0).astype(f32)
    idle = jnp.where(low, inv_reg, 0.0).astype(f32)
    nothing = jnp.zeros((32, 128), bf16)
    acc_ref[...] = jnp.zeros_like(acc_ref)
    both_b[...] = jnp.ones_like(both_b)
    g_b[...] = jnp.zeros_like(g_b)
    n0 = lc_ref[0, 0, 0]
    total = n0 + lc_ref[1, 0, 0]
    half = (total + 1) // 2
    first = core * half
    n = jnp.where(core == 0, half, total - half)

    def entry(j):
        j = first + jnp.clip(j, 0, n - 1)
        second = j >= n0
        return second.astype(ints), jnp.where(second, j - n0, j)

    def tile(i):
        return pl.ds(pl.multiple_of(i * 8, 8), 8)

    def distances(block, both_ref, g_ref):
        for u in range(unroll):
            j = block * unroll + u
            l, e = entry(j)
            t, s = lt_ref[l, 0, e], ls_ref[l, 0, e] + l * half_far
            centre = jnp.where(low, pltpu.roll(near_ref[tile(t), :], 4, 0), 0.0)
            right = right_ref[t]
            shifted = (far_ref[tile(s), :] - centre) * jnp.where(j < n, unit, idle)
            prod = shifted * jnp.where(low, shifted, pltpu.roll(shifted, 4, 0))
            prod = prod + pltpu.roll(prod, 1, 0)
            prod = prod + pltpu.roll(prod, 2, 0)
            hi, mid, lo = split3(shifted * scale + prod * fold)
            hi_up, mid_up, lo_up = pltpu.roll(hi, 4, 0), pltpu.roll(mid, 4, 0), pltpu.roll(lo, 4, 0)
            left = jnp.concatenate([
                jnp.where(low, hi, hi_up), jnp.where(low, hi, mid_up), jnp.where(low, mid, lo_up), some,
                jnp.where(low, hi_up, hi), jnp.where(low, hi_up, mid), jnp.where(low, mid_up, lo),
                jnp.zeros((8, 128), f32)], axis=0).astype(bf16)
            weights = jnp.concatenate([
                jnp.concatenate([right, nothing], axis=1), jnp.concatenate([nothing, right], axis=1)], axis=0)
            both_ref[u] = lax.dot_general(left, weights, (((0,), (0,)), ((), ())), preferred_element_type=f32)
            g_ref[u] = jnp.concatenate([jnp.where(last, 1.0, hi), jnp.where(last, 0.0, mid)], axis=0).astype(bf16)

    def speeds(block, both_ref, g_ref):
        for u in range(unroll):
            l, e = entry(block * unroll + u)
            t = lt_ref[l, 0, e]
            both, g = both_ref[u], g_ref[u]
            inv = lax.rsqrt(both[:, 0:128])
            weight = inv * inv * inv
            iso = inv + weight
            pro = both[:, 128:256] * weight
            iso_hi, pro_hi = iso.astype(bf16), pro.astype(bf16)
            iso_lo = (iso - iso_hi.astype(f32)).astype(bf16)
            pro_lo = (pro - pro_hi.astype(f32)).astype(bf16)
            m = jnp.concatenate([
                jnp.concatenate([iso_hi, pro_hi], axis=1), jnp.concatenate([iso_lo, pro_lo], axis=1)], axis=0)
            out = jnp.dot(jnp.concatenate([g, g], axis=1), m, preferred_element_type=f32)
            out = out[0:8] + out[8:16]
            from_iso, from_pro = out[:, 0:128], out[:, 128:256]
            acc_ref[tile(t), :] += pltpu.roll(from_iso, 4, 0) + near_ref[tile(t), :] * from_pro[3:4] + 0.5 * from_pro

    def many(i, carry):
        distances(2 * i, both_a, g_a)
        speeds(2 * i - 1, both_b, g_b)
        distances(2 * i + 1, both_b, g_b)
        speeds(2 * i, both_a, g_a)
        return carry

    lax.fori_loop(0, (n + unroll - 1) // unroll // 2 + 1, many, 0)
    for c in range(ncol):
        for k in range(3):
            v_ref[c, k] = stokes_scale * acc_ref[pl.ds(c * local * 8 + k, local, stride=8), :]


def home_kernel(
        nrow, ncol, cap, slot_ref, place_ref, cnt_ref, v_ref, out_ref, got, part, outg, arr, vsend, vrecv, asend, arecv):
    row, col = lax.axis_index("row"), lax.axis_index("col")
    local = out_ref.shape[1]
    devs = nrow * ncol
    me = row * ncol + col
    barrier = pltpu.get_barrier_semaphore()

    def peer(d):
        p = lax.rem(me + d, devs)
        return {"row": p // ncol, "col": lax.rem(p, ncol)}

    for d in range(1, devs):
        pl.semaphore_signal(barrier, inc=1, device_id=peer(d), device_id_type=MESH)
    half = ncol // 2
    core = lax.rem(col, 2)
    mine_x = col // 2

    def remote(src, dst, send, recv, where):
        return pltpu.make_async_remote_copy(
            src_ref=src, dst_ref=dst, send_sem=send, recv_sem=recv, device_id=where, device_id_type=MESH)

    def within(d, k):
        x = lax.rem(mine_x + d, half)
        return remote(v_ref.at[2 * x + 1 - core, k], got.at[d, k], vsend.at[d, k], vrecv.at[d, k], {"col": col + 1 - 2 * core})

    def facing(d):
        return 2 * lax.rem(mine_x + d, half) + core

    def across(d, k):
        at = half + d - 1
        return remote(part.at[d - 1, k], got.at[at, k], vsend.at[at, k], vrecv.at[at, k], {"col": facing(d)})

    def deal(d, k):
        return remote(outg.at[k, lax.rem(me + d, devs)], arr.at[k, me], asend.at[d - 1, k], arecv.at[d - 1, k], peer(d))

    def move(pick, values):
        parts = jnp.concatenate(split3(values), axis=1).astype(bf16)
        moved = jnp.dot(pick, parts, preferred_element_type=f32)
        return moved[:, 0:128] + moved[:, 128:256] + moved[:, 256:384]

    pick = (lax.broadcasted_iota(ints, (devs * cap, local), 0) == slot_ref[...]).astype(f32).astype(bf16)
    pl.semaphore_wait(barrier, devs - 1)
    for k in range(3):
        for d in [*range(1, half), 0]:
            within(d, k).start()
    for k in range(3):
        for d in range(1, half):
            within(d, k).wait_recv()
            part[d - 1, k] = v_ref[facing(d), k] + got[d, k]
            across(d, k).start()
    for k in range(3):
        within(0, k).wait_recv()
        mine = v_ref[col, k] + got[0, k]
        for d in range(1, half):
            across(d, k).wait_recv()
            mine = mine + got[half + d - 1, k]
        outg[k] = move(pick, mine).reshape(devs, cap, 128)
        for d in range(1, devs):
            deal(d, k).start()
        arr[k, me] = outg[k, me]
    fetch = (lax.broadcasted_iota(ints, (local, devs * cap), 1) == place_ref[...]).astype(f32).astype(bf16)
    live = lax.broadcasted_iota(ints, (local, 128), 1) < cnt_ref[...]
    for k in range(3):
        for d in range(1, devs):
            deal(d, k).wait_recv()
        out_ref[k] = jnp.where(live, move(fetch, arr[k].reshape(devs * cap, 128)), 0.0)
    for k in range(3):
        for d in range(half):
            within(d, k).wait_send()
        for d in range(1, half):
            across(d, k).wait_send()
        for d in range(1, devs):
            deal(d, k).wait_send()


def per_device(positions, normals, curvature, pair_targets, pair_sources, pair_count, node_counts, drop_clusters, drop_owner):
    local, _, nodes = positions.shape
    nrow, ncol = lax.axis_size("row"), lax.axis_size("col")
    devs = nrow * ncol
    cap = max(2, 2 * local // devs)
    slots = pair_targets.shape[1]
    dma = pltpu.SemaphoreType.DMA
    shape = jax.ShapeDtypeStruct
    near, right, far, lt, ls, lc, slot, place, owned_counts = pl.pallas_call(
        functools.partial(gather_kernel, nrow, ncol, cap),
        out_shape=(
            pltpu.VMEM((ncol * local * 8, nodes), f32), pltpu.VMEM((ncol * local, 32, nodes), bf16),
            pltpu.VMEM((2 * nrow * local * 8, nodes), f32),
            shape((2, 1, slots), ints), shape((2, 1, slots), ints), shape((2, 1, 128), ints),
            pltpu.VMEM((1, local), ints), pltpu.VMEM((local, 1), ints), pltpu.VMEM((local, 1), ints)),
        in_specs=[HBM] * 8 + [SMEM], out_specs=(VMEM,) * 9,
        scratch_shapes=[
            pltpu.VMEM((3, local, nodes), f32), pltpu.VMEM((local, nodes), f32), *[pltpu.VMEM(drop_clusters.shape[::-1], ints)] * 2,
            pltpu.VMEM((1, drop_owner.shape[0]), ints), dma((8,)),
            pltpu.VMEM((ncol, 3, local, nodes), f32), pltpu.VMEM((2, nrow, 6, local, nodes), f32),
            dma((ncol - 1,)), dma((ncol - 1,)), *[dma((2 * nrow - 2, 6))] * 4,
            dma((6,)), dma((6,)), dma((3,)), dma((3,))],
        compiler_params=pltpu.CompilerParams(collective_id=0, has_side_effects=True, vmem_limit_bytes=24 << 20),
        name="gather_blocks",
    )(*map(far_off, (jnp.transpose(positions, (1, 0, 2)), jnp.transpose(normals, (1, 0, 2)), curvature, node_counts.T,
                     drop_clusters.T, drop_owner[None, :], pair_targets, pair_sources)), pair_count)
    speeds = pl.pallas_call(
        pair_kernel,
        out_shape=pltpu.VMEM((ncol, 3, local, nodes), f32),
        in_specs=[SMEM] * 3 + [VMEM] * 3, out_specs=VMEM,
        scratch_shapes=[pltpu.VMEM((ncol * local * 8, nodes), f32)]
        + [pltpu.VMEM((unroll, nodes, 2 * nodes), f32)] * 2 + [pltpu.VMEM((unroll, 16, nodes), bf16)] * 2,
        compiler_params=pltpu.CompilerParams(vmem_limit_bytes=24 << 20),
        name="pairs",
    )(lt, ls, lc, keep(near), keep(right), keep(far))
    owned = pl.pallas_call(
        functools.partial(home_kernel, nrow, ncol, cap),
        out_shape=jax.ShapeDtypeStruct((3, local, nodes), f32),
        in_specs=[VMEM] * 4, out_specs=VMEM,
        scratch_shapes=[
            pltpu.VMEM((ncol - 1, 3, local, nodes), f32), pltpu.VMEM((max(ncol // 2 - 1, 1), 3, local, nodes), f32),
            pltpu.VMEM((3, devs, cap, nodes), f32), pltpu.VMEM((3, devs, cap, nodes), f32),
            dma((ncol - 1, 3)), dma((ncol - 1, 3)), dma((devs - 1, 3)), dma((devs - 1, 3)),
        ],
        compiler_params=pltpu.CompilerParams(collective_id=1, has_side_effects=True, vmem_limit_bytes=24 << 20),
        name="to_owners",
    )(keep(slot), keep(place), keep(owned_counts), keep(speeds))
    return jnp.transpose(owned, (1, 0, 2))


def solution(mesh):
    every = ("groups", "row", "col")
    in_specs = (
        P(every, None, None), P(every, None, None), P(every, None), P(every, None), P(every, None), P(every),
        P("groups", None), P("groups", None), P("groups"),
    )
    return jax.shard_map(per_device, mesh=mesh, in_specs=in_specs, out_specs=P(every, None, None), check_vma=False)
```

```python
import functools
import math

import jax
import jax.numpy as jnp
from jax import lax
from jax.experimental import pallas as pl
from jax.experimental.pallas import tpu as pltpu
from jax.sharding import PartitionSpec as P

regular_sq = 0.0025
inv_reg = 1.0 / math.sqrt(regular_sq)
stokes_scale = inv_reg / (8.0 * math.pi)
MESH = pl.DeviceIdType.MESH
VMEM = pl.BlockSpec(memory_space=pltpu.VMEM)
SMEM = pl.BlockSpec(memory_space=pltpu.SMEM)


HBM = pl.BlockSpec(memory_space=pltpu.HBM)
unroll = 16
f32, bf16, ints = jnp.float32, jnp.bfloat16, jnp.int32


def keep(x):
    return pltpu.with_memory_space_constraint(x, pltpu.VMEM)


def far_off(x):
    return pltpu.with_memory_space_constraint(x, pltpu.HBM)


def split3(x):
    high = x.astype(bf16).astype(f32)
    rest = x - high
    middle = rest.astype(bf16).astype(f32)
    return high, middle, rest - middle


def as_row(column):
    return jnp.transpose(jnp.broadcast_to(column, (column.shape[0], 128)))[0:1]


def gather_kernel(
        nrow, ncol, cap, pos_in, nrm_in, curv_in, nct_in, dct_in, own_in, tgt_in, src_in, count_ref,
        near_ref, far_ref, tl_ref, sl_ref, lc_ref, slot_ref, place_ref, cnt_ref,
        nrm_ref, curv_ref, nct_ref, dct_ref, own_ref, tgt_ref, src_ref, here_sem, mine_ref, lists_ref, t_ref, s_ref,
        zsend, zrecv, fsend, frecv, osend, orecv, tsend, trecv, bsend, brecv, xsend, xrecv, gsend, grecv, lsend, lrecv, hsend, hrecv):
    row, col = lax.axis_index("row"), lax.axis_index("col")
    core = lax.rem(col, 2)
    chip = col // 2
    half = ncol // 2
    part = nrow // 2
    i, j = row // part, lax.rem(row, part)
    me = row * ncol + col
    local = pos_in.shape[1]
    drops = own_ref.shape[1]
    per_drop = dct_ref.shape[0]
    slots = tgt_in.shape[1]
    pos_ref = s_ref.at[core, j, 0:3]
    loads = [pltpu.make_async_copy(src, dst, here_sem.at[n]) for n, (src, dst) in enumerate((
        (pos_in, pos_ref), (tgt_in, tgt_ref), (src_in, src_ref), (dct_in, dct_ref), (nct_in, nct_ref), (own_in, own_ref),
        (curv_in, curv_ref), (nrm_in, nrm_ref)))]
    for load in loads:
        load.start()
    barrier = pltpu.get_barrier_semaphore()
    for d in range(1, nrow):
        pl.semaphore_signal(barrier, inc=1, device_id={"row": lax.rem(row + d, nrow)}, device_id_type=MESH)
    for d in range(1, ncol):
        pl.semaphore_signal(barrier, inc=1, device_id={"col": lax.rem(col + d, ncol)}, device_id_type=MESH)

    def remote(src, dst, send, recv, where):
        return pltpu.make_async_remote_copy(
            src_ref=src, dst_ref=dst, send_sem=send, recv_sem=recv, device_id=where, device_id_type=MESH)

    sibling = {"col": col + 1 - 2 * core}

    def along(d, k):
        piece = s_ref.at[core, j, k]
        return remote(piece, piece, zsend.at[d - 1, k], zrecv.at[d - 1, k], {"row": i * part + lax.rem(j + d, part)})

    def source(d):
        return lax.rem(j + part - d, part)

    def onward(d, k):
        piece = s_ref.at[core, source(d), k]
        return remote(piece, piece, fsend.at[d - 1, k], frecv.at[d - 1, k], sibling)

    def own(k):
        piece = s_ref.at[core, j, k]
        return remote(piece, piece, osend.at[k], orecv.at[k], sibling)

    mirror = nrow - 1 - row
    mirror_j = part - 1 - j
    gives = (2 * mirror_j) // part == i
    takes = (2 * j) // part != i

    def index_given(a):
        return jnp.clip(2 * mirror_j + a - i * part, 0, part - 1)

    def index_held(a):
        return jnp.clip(2 * j + a - i * part, 0, part - 1)

    def give(a, k):
        return remote(
            s_ref.at[core, index_given(a), k], t_ref.at[a, col, k], tsend.at[a, k], trecv.at[a, k], {"row": mirror})

    def beside(a):
        piece = t_ref.at[a, col]
        return remote(piece, piece, bsend.at[a], brecv.at[a], sibling)

    def facing(d):
        return 2 * lax.rem(chip + d, half) + core

    def opposite(a, d):
        piece = t_ref.at[a, col]
        return remote(piece, piece, xsend.at[d - 1, a], xrecv.at[d - 1, a], {"col": facing(d)})

    def behind(d):
        return 2 * lax.rem(chip + half - d, half) + core

    def passed(a, d):
        piece = t_ref.at[a, behind(d)]
        return remote(piece, piece, gsend.at[d - 1, a], grecv.at[d - 1, a], sibling)

    def share(a):
        beside(a).start()
        for d in range(1, half):
            opposite(a, d).start()

    def on_positions(index, k):
        for a in range(2):
            @pl.when(gives & (index_given(a) == index))
            def _():
                give(a, k).start()

            @pl.when(jnp.logical_not(takes) & (index_held(a) == index))
            def _():
                t_ref[a, col, k] = s_ref[core, index, k]
                if k == 2:
                    share(a)

    def list_to(e):
        return remote(
            mine_ref, lists_ref.at[lax.rem(row, 2), core], lsend.at[e], lrecv.at[lax.rem(row, 2)], {"row": e * part + row // 2})

    def list_on(a):
        piece = lists_ref.at[a, core]
        return remote(piece, piece, hsend.at[a], hrecv.at[a], sibling)

    loads[0].wait()
    pl.semaphore_wait(barrier, nrow + ncol - 2)
    for k in range(3):
        for d in range(1, part):
            along(d, k).start()
    for k in range(3):
        on_positions(j, k)
    for load in loads[1:]:
        load.wait()
    zero = jnp.zeros((1, slots), ints)
    mine_ref[...] = jnp.concatenate(
        [tgt_ref[...], src_ref[...], jnp.full((1, slots), count_ref[0], ints), zero, zero, zero, zero, zero], axis=0)
    for e in range(2):
        @pl.when(e * part + row // 2 != row)
        def _():
            list_to(e).start()

        @pl.when(e * part + row // 2 == row)
        def _():
            lists_ref[lax.rem(row, 2), core] = mine_ref[...]

    index = lax.broadcasted_iota(ints, (local, 1), 0)
    ids = me * local + index
    home = (2 * j + i) * ncol + col
    home_ids = home * local + index

    def match(chunk, carry):
        counts, owners = carry
        lanes = pl.ds(pl.multiple_of(chunk * 128, 128), 128)
        clusters, nodes_in, owner = dct_ref[:, lanes], nct_ref[:, lanes], own_ref[0:1, lanes]
        for k in range(per_drop):
            counts = counts + jnp.where(ids == clusters[k:k + 1], nodes_in[k:k + 1], 0)
            owners = owners + jnp.where(home_ids == clusters[k:k + 1], owner, 0)
        return counts, owners

    none = jnp.zeros((local, 128), ints)
    counts, owners = lax.fori_loop(0, drops // 128, match, (none, none))
    home_counts = jnp.sum(counts, axis=1, keepdims=True, dtype=ints)
    home_owner = jnp.sum(owners, axis=1, keepdims=True, dtype=ints)
    scale = jnp.where(lax.broadcasted_iota(ints, (local, 128), 1) < home_counts, curv_ref[...], 0.0)
    for k in range(3):
        s_ref[core, j, 3 + k] = scale * nrm_ref[k]
        for d in range(1, part):
            along(d, 3 + k).start()
    for k in range(6):
        own(k).start()

    def spread(l, r, k):
        at = (l * part + r) * local * 8 + (k if k < 3 else k + 1)
        far_ref[pl.ds(at, local, stride=8), :] = s_ref[l, r, k]

    def blank(l, r):
        for k in (3, 7):
            far_ref[pl.ds((l * part + r) * local * 8 + k, local, stride=8), :] = jnp.zeros((local, 128), f32)

    def arrive(k):
        for d in range(1, part):
            along(d, k).wait_recv()
            onward(d, k).start()
            if k < 3:
                on_positions(source(d), k)

    def targets(a, c):
        square = jnp.ones((local, 128), f32)
        start = (a * ncol + c) * local * 8
        for k in range(3):
            coord = t_ref[a, c, k]
            centre = jnp.mean(coord, axis=1, keepdims=True)
            coord = (coord - centre) * inv_reg
            square = square + coord * coord
            near_ref[pl.ds(start + k, local, stride=8), :] = coord
            near_ref[pl.ds(start + 4 + k, local, stride=8), :] = jnp.broadcast_to(centre, coord.shape)
        near_ref[pl.ds(start + 3, local, stride=8), :] = square
        near_ref[pl.ds(start + 7, local, stride=8), :] = jnp.zeros((local, 128), f32)

    for k in range(3):
        arrive(k)
    for a in range(2):
        @pl.when(2 * j + a != row)
        def _():
            remote(mine_ref, lists_ref.at[a, core], lsend.at[0], lrecv.at[a], sibling).wait_recv()

        list_on(a).start()

    owner_row = as_row(home_owner.astype(f32)).astype(ints)
    lane = lax.broadcasted_iota(ints, (local, local), 1)
    rank = jnp.sum(((owner_row == home_owner) & (lane < index)).astype(ints), axis=1, keepdims=True, dtype=ints)
    slot_ref[...] = as_row((home_owner * cap + rank).astype(f32)).astype(ints)
    drop_of = lax.div(index, per_drop)
    width = 256 if drops % 256 == 0 else 128
    before = (lax.broadcasted_iota(ints, (width, width), 0) < lax.broadcasted_iota(ints, (width, width), 1)).astype(bf16)

    def owned(chunk, carry):
        clusters, counted, base = carry
        lanes = pl.ds(pl.multiple_of(chunk * width, width), width)
        mine = own_ref[0:1, lanes] == me
        marks = jnp.broadcast_to(mine.astype(f32), (16, width)).astype(bf16)
        place = jnp.dot(marks, before, preferred_element_type=f32)[0:1].astype(ints) + base
        chosen = mine & (place == drop_of)
        clusters = clusters + jnp.where(chosen, jnp.concatenate([dct_ref[:, lanes]] * (local // per_drop), axis=0), 0)
        counted = counted + jnp.where(chosen, jnp.concatenate([nct_ref[:, lanes]] * (local // per_drop), axis=0), 0)
        return clusters, counted, base + jnp.sum(mine.astype(ints), axis=1, keepdims=True, dtype=ints)

    wide = jnp.zeros((local, width), ints)
    clusters, counted, _ = lax.fori_loop(0, drops // width, owned, (wide, wide, jnp.zeros((1, 1), ints)))
    clusters = jnp.sum(clusters, axis=1, keepdims=True, dtype=ints)
    cnt_ref[...] = jnp.sum(counted, axis=1, keepdims=True, dtype=ints)
    clusters_row = as_row(clusters.astype(f32)).astype(ints)
    anchor, anchor_row = lax.div(clusters, local), lax.div(clusters_row, local)
    same = (anchor == anchor_row) & (clusters_row < clusters)
    home_row, home_col = lax.div(anchor, ncol), lax.rem(anchor, ncol)
    keeper = (lax.rem(home_row, 2) * part + lax.div(home_row, 2)) * ncol + home_col
    place_ref[...] = keeper * cap + jnp.sum(same.astype(ints), axis=1, keepdims=True, dtype=ints)

    @pl.when(takes)
    def _():
        for a in range(2):
            for k in range(3):
                give(a, k).wait_recv()
            share(a)

    for k in range(6):
        spread(core, j, k)
    for l in range(2):
        for r in range(part):
            blank(l, r)
    for a in range(2):
        targets(a, col)

    for a in range(2):
        list_on(a).wait_recv()
    lane_of = lax.broadcasted_iota(ints, (1, slots), 1)
    lowest = i * part * local
    square_rows = lax.broadcasted_iota(ints, (slots, slots), 0)
    earlier = (square_rows < lax.broadcasted_iota(ints, (slots, slots), 1)).astype(f32).astype(bf16)
    for a in range(2):
        for l in range(2):
            t, s, count = lists_ref[a, l, 0:1, :], lists_ref[a, l, 1:2, :], lists_ref[a, l, 2:3, :]
            taken = (lane_of < count) & (s >= lowest) & (s < lowest + part * local)
            marks = taken.astype(f32)
            ranks = jnp.dot(jnp.broadcast_to(marks, (16, slots)).astype(bf16), earlier, preferred_element_type=f32)[0:1]
            ranks = jnp.where(taken, ranks.astype(ints), -1)
            to = (square_rows == ranks).astype(f32).astype(bf16)
            digits = [lax.div(t, 256), lax.rem(t, 256), lax.div(s, 256), lax.rem(s, 256)]
            values = jnp.concatenate([v.astype(f32) for v in digits] + [jnp.zeros((12, slots), f32)], axis=0).astype(bf16)
            moved = lax.dot_general(values, to, (((1,), (1,)), ((), ())), preferred_element_type=f32).astype(ints)
            n = a * 2 + l
            tl_ref[n:n + 1, :] = moved[0:1] * 256 + moved[1:2] + a * ncol * local
            sl_ref[n:n + 1, :] = jnp.maximum(moved[2:3] * 256 + moved[3:4] - lowest, 0) + l * part * local
            lc_ref[n:n + 1, :] = jnp.broadcast_to(jnp.sum(marks, axis=1, keepdims=True).astype(ints), (1, 128))

    for a in range(2):
        for d in range(1, half):
            opposite(a, d).wait_recv()
            passed(a, d).start()
        beside(a).wait_recv()
        targets(a, col + 1 - 2 * core)
        for d in range(1, half):
            targets(a, behind(d))
    for k in range(3, 6):
        arrive(k)
    for k in range(6):
        own(k).wait_recv()
        spread(1 - core, j, k)
        for d in range(1, part):
            spread(core, source(d), k)
    for a in range(2):
        for d in range(1, half):
            passed(a, d).wait_recv()
            targets(a, behind(d) + 1 - 2 * core)
    for k in range(6):
        for d in range(1, part):
            onward(d, k).wait_recv()
            spread(1 - core, source(d), k)
    for k in range(6):
        own(k).wait_send()
        for d in range(1, part):
            along(d, k).wait_send()
            onward(d, k).wait_send()
    for a in range(2):
        @pl.when(gives)
        def _():
            for k in range(3):
                give(a, k).wait_send()

        beside(a).wait_send()
        list_on(a).wait_send()
        for d in range(1, half):
            opposite(a, d).wait_send()
            passed(a, d).wait_send()
    for e in range(2):
        @pl.when(e * part + row // 2 != row)
        def _():
            list_to(e).wait_send()


def pair_kernel(tl_ref, sl_ref, lc_ref, near_ref, far_ref, v_ref, acc_ref, both_a, both_b, g_a, g_b):
    _, ncol, _, local, _ = v_ref.shape
    core = lax.rem(lax.axis_index("col"), 2)
    sub = lax.broadcasted_iota(ints, (8, 128), 0)
    low = sub < 4
    last = (sub == 3) | (sub == 7)
    scale = jnp.where(low, -2.0, 1.0).astype(f32)
    fold = jnp.where(sub == 3, 1.0, jnp.where(sub == 7, -1.0, 0.0)).astype(f32)
    some = jnp.where(low, 1.0, 0.0).astype(f32)
    unit = jnp.where(low, inv_reg, 1.0).astype(f32)
    idle = jnp.where(low, inv_reg, 0.0).astype(f32)
    nothing = jnp.zeros((32, 128), bf16)
    acc_ref[...] = jnp.zeros_like(acc_ref)
    both_b[...] = jnp.ones_like(both_b)
    g_b[...] = jnp.zeros_like(g_b)
    ends = [lc_ref[0, 0]]
    for l in range(1, 4):
        ends.append(ends[-1] + lc_ref[l, 0])
    total = ends[3]
    half = (total + 1) // 2
    first = core * half
    n = jnp.where(core == 0, half, total - half)

    def entry(j):
        j = jnp.minimum(first + jnp.clip(j, 0, jnp.maximum(n - 1, 0)), jnp.maximum(total - 1, 0))
        past = [(j >= end).astype(ints) for end in ends[:3]]
        start = jnp.where(j >= ends[2], ends[2], jnp.where(j >= ends[1], ends[1], jnp.where(j >= ends[0], ends[0], 0)))
        return past[0] + past[1] + past[2], j - start

    def tile(i):
        return pl.ds(pl.multiple_of(i * 8, 8), 8)

    def distances(block, both_ref, g_ref):
        for u in range(unroll):
            j = block * unroll + u
            l, e = entry(j)
            t, s = tl_ref[l, e], sl_ref[l, e]
            near = near_ref[tile(t), :]
            centre = jnp.where(low, pltpu.roll(near, 4, 0), 0.0)
            high, middle, rest = split3(near)
            sums = jnp.where(sub == 0, high[3:4], jnp.where(sub == 1, middle[3:4], jnp.where(sub == 2, rest[3:4], 0.0)))
            high = jnp.where(sub < 3, high, jnp.where(sub == 3, 1.0, 0.0))
            middle = jnp.where(sub < 3, middle, 0.0)
            rest = jnp.where(sub < 3, rest, 0.0)
            high_up = pltpu.roll(high, 4, 0)
            right = jnp.concatenate([
                high + pltpu.roll(middle, 4, 0), rest + high_up, middle + high_up, sums], axis=0).astype(bf16)
            shifted = (far_ref[tile(s), :] - centre) * jnp.where(j < n, unit, idle)
            prod = shifted * jnp.where(low, shifted, pltpu.roll(shifted, 4, 0))
            prod = prod + pltpu.roll(prod, 1, 0)
            prod = prod + pltpu.roll(prod, 2, 0)
            hi, mid, lo = split3(shifted * scale + prod * fold)
            hi_up, mid_up, lo_up = pltpu.roll(hi, 4, 0), pltpu.roll(mid, 4, 0), pltpu.roll(lo, 4, 0)
            left = jnp.concatenate([
                jnp.where(low, hi, hi_up), jnp.where(low, hi, mid_up), jnp.where(low, mid, lo_up), some,
                jnp.where(low, hi_up, hi), jnp.where(low, hi_up, mid), jnp.where(low, mid_up, lo),
                jnp.zeros((8, 128), f32)], axis=0).astype(bf16)
            weights = jnp.concatenate([
                jnp.concatenate([right, nothing], axis=1), jnp.concatenate([nothing, right], axis=1)], axis=0)
            both_ref[u] = lax.dot_general(left, weights, (((0,), (0,)), ((), ())), preferred_element_type=f32)
            g_ref[u] = jnp.concatenate([jnp.where(last, 1.0, hi), jnp.where(last, 0.0, mid)], axis=0).astype(bf16)

    def speeds(block, both_ref, g_ref):
        for u in range(unroll):
            l, e = entry(block * unroll + u)
            t = tl_ref[l, e]
            both, g = both_ref[u], g_ref[u]
            inv = lax.rsqrt(both[:, 0:128])
            weight = inv * inv * inv
            iso = inv + weight
            pro = both[:, 128:256] * weight
            iso_hi, pro_hi = iso.astype(bf16), pro.astype(bf16)
            iso_lo = (iso - iso_hi.astype(f32)).astype(bf16)
            pro_lo = (pro - pro_hi.astype(f32)).astype(bf16)
            m = jnp.concatenate([
                jnp.concatenate([iso_hi, pro_hi], axis=1), jnp.concatenate([iso_lo, pro_lo], axis=1)], axis=0)
            out = jnp.dot(jnp.concatenate([g, g], axis=1), m, preferred_element_type=f32)
            out = out[0:8] + out[8:16]
            from_iso, from_pro = out[:, 0:128], out[:, 128:256]
            acc_ref[tile(t), :] += pltpu.roll(from_iso, 4, 0) + near_ref[tile(t), :] * from_pro[3:4] + 0.5 * from_pro

    def many(i, carry):
        distances(2 * i, both_a, g_a)
        speeds(2 * i - 1, both_b, g_b)
        distances(2 * i + 1, both_b, g_b)
        speeds(2 * i, both_a, g_a)
        return carry

    lax.fori_loop(0, (n + unroll - 1) // unroll // 2 + 1, many, 0)
    for a in range(2):
        for c in range(ncol):
            for k in range(3):
                v_ref[a, c, k] = stokes_scale * acc_ref[pl.ds((a * ncol + c) * local * 8 + k, local, stride=8), :]


def home_kernel(
        nrow, ncol, cap, slot_ref, place_ref, cnt_ref, v_ref, out_ref, got, part, swap, outg, arr, vsend, vrecv, zsend, zrecv, asend, arecv):
    row, col = lax.axis_index("row"), lax.axis_index("col")
    local = out_ref.shape[1]
    devs = nrow * ncol
    me = row * ncol + col
    barrier = pltpu.get_barrier_semaphore()

    def peer(d):
        p = lax.rem(me + d, devs)
        return {"row": p // ncol, "col": lax.rem(p, ncol)}

    for d in range(1, devs):
        pl.semaphore_signal(barrier, inc=1, device_id=peer(d), device_id_type=MESH)
    half = ncol // 2
    core = lax.rem(col, 2)
    mine_x = col // 2

    def remote(src, dst, send, recv, where):
        return pltpu.make_async_remote_copy(
            src_ref=src, dst_ref=dst, send_sem=send, recv_sem=recv, device_id=where, device_id_type=MESH)

    rows = nrow // 2
    keep_a = row // rows
    order = (1 - keep_a, keep_a)

    def within(n, d, k):
        x = lax.rem(mine_x + d, half)
        return remote(
            v_ref.at[order[n], 2 * x + 1 - core, k], got.at[n, d, k], vsend.at[n, d, k], vrecv.at[n, d, k],
            {"col": col + 1 - 2 * core})

    def facing(d):
        return 2 * lax.rem(mine_x + d, half) + core

    def across(n, d, k):
        at = half + d - 1
        return remote(
            part.at[n, d - 1, k], got.at[n, at, k], vsend.at[n, at, k], vrecv.at[n, at, k], {"col": facing(d)})

    def exchange(k):
        return remote(swap.at[0, k], swap.at[1, k], zsend.at[k], zrecv.at[k], {"row": lax.rem(row + rows, nrow)})

    def total(n, k):
        within(n, 0, k).wait_recv()
        mine = v_ref[order[n], col, k] + got[n, 0, k]
        for d in range(1, half):
            across(n, d, k).wait_recv()
            mine = mine + got[n, half + d - 1, k]
        return mine

    def deal(d, k):
        return remote(outg.at[k, lax.rem(me + d, devs)], arr.at[k, me], asend.at[d - 1, k], arecv.at[d - 1, k], peer(d))

    def move(pick, values):
        parts = jnp.concatenate(split3(values), axis=1).astype(bf16)
        moved = jnp.dot(pick, parts, preferred_element_type=f32)
        return moved[:, 0:128] + moved[:, 128:256] + moved[:, 256:384]

    pick = (lax.broadcasted_iota(ints, (devs * cap, local), 0) == slot_ref[...]).astype(f32).astype(bf16)
    pl.semaphore_wait(barrier, devs - 1)
    for n in range(2):
        for k in range(3):
            for d in [*range(1, half), 0]:
                within(n, d, k).start()

    def pass_on(n, k):
        for d in range(1, half):
            within(n, d, k).wait_recv()
            part[n, d - 1, k] = v_ref[order[n], facing(d), k] + got[n, d, k]
            across(n, d, k).start()

    for k in range(3):
        pass_on(0, k)
    for k in range(3):
        swap[0, k] = total(0, k)
        exchange(k).start()
        pass_on(1, k)
    for k in range(3):
        mine = total(1, k)
        exchange(k).wait_recv()
        outg[k] = move(pick, mine + swap[1, k]).reshape(devs, cap, 128)
        for d in range(1, devs):
            deal(d, k).start()
        arr[k, me] = outg[k, me]
    fetch = (lax.broadcasted_iota(ints, (local, devs * cap), 1) == place_ref[...]).astype(f32).astype(bf16)
    live = lax.broadcasted_iota(ints, (local, 128), 1) < cnt_ref[...]
    for k in range(3):
        for d in range(1, devs):
            deal(d, k).wait_recv()
        out_ref[k] = jnp.where(live, move(fetch, arr[k].reshape(devs * cap, 128)), 0.0)
    for k in range(3):
        exchange(k).wait_send()
        for n in range(2):
            for d in range(half):
                within(n, d, k).wait_send()
            for d in range(1, half):
                across(n, d, k).wait_send()
        for d in range(1, devs):
            deal(d, k).wait_send()


def per_device(positions, normals, curvature, pair_targets, pair_sources, pair_count, node_counts, drop_clusters, drop_owner):
    local, _, nodes = positions.shape
    nrow, ncol = lax.axis_size("row"), lax.axis_size("col")
    devs = nrow * ncol
    part, half = nrow // 2, ncol // 2
    cap = max(2, 2 * local // devs)
    slots = pair_targets.shape[1]
    dma = pltpu.SemaphoreType.DMA
    shape = jax.ShapeDtypeStruct
    near, far, tl, sl, lc, slot, place, owned_counts = pl.pallas_call(
        functools.partial(gather_kernel, nrow, ncol, cap),
        out_shape=(
            pltpu.VMEM((2 * ncol * local * 8, nodes), f32), pltpu.VMEM((2 * part * local * 8, nodes), f32),
            shape((4, slots), ints), shape((4, slots), ints), shape((4, 128), ints),
            pltpu.VMEM((1, local), ints), pltpu.VMEM((local, 1), ints), pltpu.VMEM((local, 1), ints)),
        in_specs=[HBM] * 8 + [SMEM], out_specs=(VMEM,) * 8,
        scratch_shapes=[
            pltpu.VMEM((3, local, nodes), f32), pltpu.VMEM((local, nodes), f32), *[pltpu.VMEM(drop_clusters.shape[::-1], ints)] * 2,
            pltpu.VMEM((1, drop_owner.shape[0]), ints), *[pltpu.VMEM((1, slots), ints)] * 2, dma((8,)),
            pltpu.VMEM((8, slots), ints), pltpu.VMEM((2, 2, 8, slots), ints),
            pltpu.VMEM((2, ncol, 3, local, nodes), f32), pltpu.VMEM((2, part, 6, local, nodes), f32),
            *[dma((part - 1, 6))] * 4, *[dma((6,))] * 2, *[dma((2, 3))] * 2, *[dma((2,))] * 2,
            *[dma((max(half - 1, 1), 2))] * 4, *[dma((2,))] * 4],
        compiler_params=pltpu.CompilerParams(collective_id=0, has_side_effects=True, vmem_limit_bytes=30 << 20),
        name="gather_blocks",
    )(*map(far_off, (jnp.transpose(positions, (1, 0, 2)), jnp.transpose(normals, (1, 0, 2)), curvature, node_counts.T,
                     drop_clusters.T, drop_owner[None, :], pair_targets, pair_sources)), pair_count)
    speeds = pl.pallas_call(
        pair_kernel,
        out_shape=pltpu.VMEM((2, ncol, 3, local, nodes), f32),
        in_specs=[SMEM] * 3 + [VMEM] * 2, out_specs=VMEM,
        scratch_shapes=[pltpu.VMEM((2 * ncol * local * 8, nodes), f32)]
        + [pltpu.VMEM((unroll, nodes, 2 * nodes), f32)] * 2 + [pltpu.VMEM((unroll, 16, nodes), bf16)] * 2,
        compiler_params=pltpu.CompilerParams(vmem_limit_bytes=30 << 20),
        name="pairs",
    )(tl, sl, lc, keep(near), keep(far))
    owned = pl.pallas_call(
        functools.partial(home_kernel, nrow, ncol, cap),
        out_shape=jax.ShapeDtypeStruct((3, local, nodes), f32),
        in_specs=[VMEM] * 4, out_specs=VMEM,
        scratch_shapes=[
            pltpu.VMEM((2, ncol - 1, 3, local, nodes), f32), pltpu.VMEM((2, max(half - 1, 1), 3, local, nodes), f32),
            pltpu.VMEM((2, 3, local, nodes), f32),
            pltpu.VMEM((3, devs, cap, nodes), f32), pltpu.VMEM((3, devs, cap, nodes), f32),
            dma((2, ncol - 1, 3)), dma((2, ncol - 1, 3)), dma((3,)), dma((3,)), dma((devs - 1, 3)), dma((devs - 1, 3)),
        ],
        compiler_params=pltpu.CompilerParams(collective_id=1, has_side_effects=True, vmem_limit_bytes=30 << 20),
        name="to_owners",
    )(keep(slot), keep(place), keep(owned_counts), keep(speeds))
    return jnp.transpose(owned, (1, 0, 2))


def solution(mesh):
    every = ("groups", "row", "col")
    in_specs = (
        P(every, None, None), P(every, None, None), P(every, None), P(every, None), P(every, None), P(every),
        P("groups", None), P("groups", None), P("groups"),
    )
    return jax.shard_map(per_device, mesh=mesh, in_specs=in_specs, out_specs=P(every, None, None), check_vma=False)
```

```python
import functools
import math

import jax
import jax.numpy as jnp
from jax import lax
from jax.experimental import pallas as pl
from jax.experimental.pallas import tpu as pltpu
from jax.sharding import PartitionSpec as P

regular_sq = 0.0025
inv_reg = 1.0 / math.sqrt(regular_sq)
stokes_scale = inv_reg / (8.0 * math.pi)
MESH = pl.DeviceIdType.MESH
VMEM = pl.BlockSpec(memory_space=pltpu.VMEM)
SMEM = pl.BlockSpec(memory_space=pltpu.SMEM)


HBM = pl.BlockSpec(memory_space=pltpu.HBM)
unroll = 16
f32, bf16, ints = jnp.float32, jnp.bfloat16, jnp.int32


def keep(x):
    return pltpu.with_memory_space_constraint(x, pltpu.VMEM)


def far_off(x):
    return pltpu.with_memory_space_constraint(x, pltpu.HBM)


def split3(x):
    high = x.astype(bf16).astype(f32)
    rest = x - high
    middle = rest.astype(bf16).astype(f32)
    return high, middle, rest - middle


def as_row(column):
    return jnp.transpose(jnp.broadcast_to(column, (column.shape[0], 128)))[0:1]


def gather_kernel(
        nrow, ncol, cap, pos_in, nrm_in, curv_in, nct_in, dct_in, own_in, tgt_in, src_in, count_ref,
        near_ref, far_ref, tl_ref, sl_ref, lc_ref, slot_ref, place_ref, cnt_ref,
        nrm_ref, curv_ref, nct_ref, dct_ref, own_ref, tgt_ref, src_ref, here_sem, mine_ref, lists_ref, t_ref, s_ref,
        zsend, zrecv, fsend, frecv, osend, orecv, bsend, brecv, xsend, xrecv, gsend, grecv, lsend, lrecv, hsend, hrecv):
    row, col = lax.axis_index("row"), lax.axis_index("col")
    core = lax.rem(col, 2)
    chip = col // 2
    half = ncol // 2
    part = nrow // 2
    i = lax.rem(row, 2)
    mate = row + 1 - 2 * i
    based = row // part == i
    me = row * ncol + col
    local = pos_in.shape[1]
    drops = own_ref.shape[1]
    per_drop = dct_ref.shape[0]
    slots = tgt_in.shape[1]
    pos_ref = s_ref.at[core, row, 0:3]
    loads = [pltpu.make_async_copy(src, dst, here_sem.at[n]) for n, (src, dst) in enumerate((
        (pos_in, pos_ref), (tgt_in, tgt_ref), (src_in, src_ref), (dct_in, dct_ref), (nct_in, nct_ref), (own_in, own_ref),
        (curv_in, curv_ref), (nrm_in, nrm_ref)))]
    for load in loads:
        load.start()
    barrier = pltpu.get_barrier_semaphore()
    for d in range(1, nrow):
        pl.semaphore_signal(barrier, inc=1, device_id={"row": lax.rem(row + d, nrow)}, device_id_type=MESH)
    for d in range(1, ncol):
        pl.semaphore_signal(barrier, inc=1, device_id={"col": lax.rem(col + d, ncol)}, device_id_type=MESH)

    def remote(src, dst, send, recv, where):
        return pltpu.make_async_remote_copy(
            src_ref=src, dst_ref=dst, send_sem=send, recv_sem=recv, device_id=where, device_id_type=MESH)

    sibling = {"col": col + 1 - 2 * core}

    def block_of(way, step):
        return jnp.clip(row - way * step, 0, nrow - 1)

    def relay(way, step, k):
        piece = s_ref.at[core, block_of(way, step), k]
        at = step if way > 0 else nrow - 1 + step
        return remote(piece, piece, zsend.at[at, k], zrecv.at[at, k], {"row": jnp.clip(row + way, 0, nrow - 1)})

    def reaches(way, block, place):
        inside = (block >= 0) & (block < nrow)
        half_of = jnp.clip(block, 0, nrow - 1) // part
        return inside & (place <= nrow - 2 + half_of if way > 0 else place >= half_of)

    def sends(way, step):
        return reaches(way, row - way * step, row + way)

    def receives(way, step):
        return reaches(way, row - way * (step + 1), row)

    def wanted(way, step):
        return receives(way, step) & (block_of(way, step + 1) // part == i)

    def onward(way, step, k):
        piece = s_ref.at[core, block_of(way, step + 1), k]
        at = step if way > 0 else nrow - 1 + step
        return remote(piece, piece, fsend.at[at, k], frecv.at[at, k], sibling)

    def start(way, step, k):
        @pl.when(sends(way, step))
        def _():
            relay(way, step, k).start()

    def own(k):
        piece = s_ref.at[core, row, k]
        return remote(piece, piece, osend.at[k], orecv.at[k], sibling)

    def beside(a):
        piece = t_ref.at[a, col]
        return remote(piece, piece, bsend.at[a], brecv.at[a], sibling)

    def facing(d):
        return 2 * lax.rem(chip + d, half) + core

    def opposite(a, d):
        piece = t_ref.at[a, col]
        return remote(piece, piece, xsend.at[d - 1, a], xrecv.at[d - 1, a], {"col": facing(d)})

    def behind(d):
        return 2 * lax.rem(chip + half - d, half) + core

    def passed(a, d):
        piece = t_ref.at[a, behind(d)]
        return remote(piece, piece, gsend.at[d - 1, a], grecv.at[d - 1, a], sibling)

    def share(a):
        beside(a).start()
        for d in range(1, half):
            opposite(a, d).start()

    def list_to(a):
        return remote(mine_ref, lists_ref.at[a, core], lsend.at[0], lrecv.at[0], {"row": mate})

    def list_on(a):
        piece = lists_ref.at[a, core]
        return remote(piece, piece, hsend.at[a], hrecv.at[a], sibling)

    loads[0].wait()
    pl.semaphore_wait(barrier, nrow + ncol - 2)
    for k in range(3):
        for way in (1, -1):
            start(way, 0, k)
        t_ref[i, col, k] = s_ref[core, row, k]
    share(i)
    for load in loads[1:]:
        load.wait()
    zero = jnp.zeros((1, slots), ints)
    mine_ref[...] = jnp.concatenate(
        [tgt_ref[...], src_ref[...], jnp.full((1, slots), count_ref[0], ints), zero, zero, zero, zero, zero], axis=0)
    list_to(i).start()
    lists_ref[i, core] = mine_ref[...]
    index = lax.broadcasted_iota(ints, (local, 1), 0)
    ids = me * local + index

    def match(chunk, carry):
        counts, owners = carry
        lanes = pl.ds(pl.multiple_of(chunk * 128, 128), 128)
        clusters, nodes_in, owner = dct_ref[:, lanes], nct_ref[:, lanes], own_ref[0:1, lanes]
        for k in range(per_drop):
            hit = ids == clusters[k:k + 1]
            counts = counts + jnp.where(hit, nodes_in[k:k + 1], 0)
            owners = owners + jnp.where(hit, owner, 0)
        return counts, owners

    none = jnp.zeros((local, 128), ints)
    counts, owners = lax.fori_loop(0, drops // 128, match, (none, none))
    home_counts = jnp.sum(counts, axis=1, keepdims=True, dtype=ints)
    home_owner = jnp.sum(owners, axis=1, keepdims=True, dtype=ints)
    scale = jnp.where(lax.broadcasted_iota(ints, (local, 128), 1) < home_counts, curv_ref[...], 0.0)
    for k in range(3):
        s_ref[core, row, 3 + k] = scale * nrm_ref[k]
        for way in (1, -1):
            start(way, 0, 3 + k)

    @pl.when(based)
    def _():
        for k in range(6):
            own(k).start()

    def spread(l, block, k):
        at = (l * part + lax.rem(block, part)) * local * 8 + (k if k < 3 else k + 1)
        far_ref[pl.ds(at, local, stride=8), :] = s_ref[l, block, k]

    def blank(l, r):
        for k in (3, 7):
            far_ref[pl.ds((l * part + r) * local * 8 + k, local, stride=8), :] = jnp.zeros((local, 128), f32)

    def arrive(step, k):
        for way in (1, -1):
            @pl.when(receives(way, step))
            def _():
                relay(way, step, k).wait_recv()
                if step < nrow - 2:
                    start(way, step + 1, k)

                @pl.when(wanted(way, step))
                def _():
                    onward(way, step, k).start()

    def collect(step, k):
        for way in (1, -1):
            @pl.when(wanted(way, step))
            def _():
                spread(core, block_of(way, step + 1), k)

    def received(step, k):
        for way in (1, -1):
            @pl.when(wanted(way, step))
            def _():
                onward(way, step, k).wait_recv()
                spread(1 - core, block_of(way, step + 1), k)

    def targets(a, c):
        square = jnp.ones((local, 128), f32)
        start = (a * ncol + c) * local * 8
        for k in range(3):
            coord = t_ref[a, c, k]
            centre = jnp.mean(coord, axis=1, keepdims=True)
            coord = (coord - centre) * inv_reg
            square = square + coord * coord
            near_ref[pl.ds(start + k, local, stride=8), :] = coord
            near_ref[pl.ds(start + 4 + k, local, stride=8), :] = jnp.broadcast_to(centre, coord.shape)
        near_ref[pl.ds(start + 3, local, stride=8), :] = square
        near_ref[pl.ds(start + 7, local, stride=8), :] = jnp.zeros((local, 128), f32)

    for k in range(3):
        arrive(0, k)
        t_ref[1 - i, col, k] = s_ref[core, mate, k]
    share(1 - i)
    list_to(1 - i).wait_recv()
    for a in range(2):
        list_on(a).start()

    owner_row = as_row(home_owner.astype(f32)).astype(ints)
    lane = lax.broadcasted_iota(ints, (local, local), 1)
    rank = jnp.sum(((owner_row == home_owner) & (lane < index)).astype(ints), axis=1, keepdims=True, dtype=ints)
    slot_ref[...] = as_row((home_owner * cap + rank).astype(f32)).astype(ints)
    drop_of = lax.div(index, per_drop)
    width = 256 if drops % 256 == 0 else 128
    before = (lax.broadcasted_iota(ints, (width, width), 0) < lax.broadcasted_iota(ints, (width, width), 1)).astype(bf16)

    def owned(chunk, carry):
        clusters, counted, base = carry
        lanes = pl.ds(pl.multiple_of(chunk * width, width), width)
        mine = own_ref[0:1, lanes] == me
        marks = jnp.broadcast_to(mine.astype(f32), (16, width)).astype(bf16)
        place = jnp.dot(marks, before, preferred_element_type=f32)[0:1].astype(ints) + base
        chosen = mine & (place == drop_of)
        clusters = clusters + jnp.where(chosen, jnp.concatenate([dct_ref[:, lanes]] * (local // per_drop), axis=0), 0)
        counted = counted + jnp.where(chosen, jnp.concatenate([nct_ref[:, lanes]] * (local // per_drop), axis=0), 0)
        return clusters, counted, base + jnp.sum(mine.astype(ints), axis=1, keepdims=True, dtype=ints)

    wide = jnp.zeros((local, width), ints)
    clusters, counted, _ = lax.fori_loop(0, drops // width, owned, (wide, wide, jnp.zeros((1, 1), ints)))
    clusters = jnp.sum(clusters, axis=1, keepdims=True, dtype=ints)
    cnt_ref[...] = jnp.sum(counted, axis=1, keepdims=True, dtype=ints)
    clusters_row = as_row(clusters.astype(f32)).astype(ints)
    anchor, anchor_row = lax.div(clusters, local), lax.div(clusters_row, local)
    same = (anchor == anchor_row) & (clusters_row < clusters)
    place_ref[...] = anchor * cap + jnp.sum(same.astype(ints), axis=1, keepdims=True, dtype=ints)

    for k in range(3, 6):
        arrive(0, k)
    for l in range(2):
        for r in range(part):
            blank(l, r)
    for a in range(2):
        targets(a, col)

    for a in range(2):
        list_on(a).wait_recv()
    lane_of = lax.broadcasted_iota(ints, (1, slots), 1)
    lowest = i * part * local
    square_rows = lax.broadcasted_iota(ints, (slots, slots), 0)
    earlier = (square_rows < lax.broadcasted_iota(ints, (slots, slots), 1)).astype(f32).astype(bf16)
    for a in range(2):
        for l in range(2):
            t, s, count = lists_ref[a, l, 0:1, :], lists_ref[a, l, 1:2, :], lists_ref[a, l, 2:3, :]
            taken = (lane_of < count) & (s >= lowest) & (s < lowest + part * local)
            marks = taken.astype(f32)
            ranks = jnp.dot(jnp.broadcast_to(marks, (16, slots)).astype(bf16), earlier, preferred_element_type=f32)[0:1]
            ranks = jnp.where(taken, ranks.astype(ints), -1)
            to = (square_rows == ranks).astype(f32).astype(bf16)
            digits = [lax.div(t, 256), lax.rem(t, 256), lax.div(s, 256), lax.rem(s, 256)]
            values = jnp.concatenate([v.astype(f32) for v in digits] + [jnp.zeros((12, slots), f32)], axis=0).astype(bf16)
            moved = lax.dot_general(values, to, (((1,), (1,)), ((), ())), preferred_element_type=f32).astype(ints)
            n = a * 2 + l
            tl_ref[n:n + 1, :] = moved[0:1] * 256 + moved[1:2] + a * ncol * local
            sl_ref[n:n + 1, :] = jnp.maximum(moved[2:3] * 256 + moved[3:4] - lowest, 0) + l * part * local
            lc_ref[n:n + 1, :] = jnp.broadcast_to(jnp.sum(marks, axis=1, keepdims=True).astype(ints), (1, 128))

    for a in range(2):
        for d in range(1, half):
            opposite(a, d).wait_recv()
            passed(a, d).start()
        beside(a).wait_recv()
        targets(a, col + 1 - 2 * core)
        for d in range(1, half):
            targets(a, behind(d))
    @pl.when(based)
    def _():
        for k in range(6):
            spread(core, row, k)
            own(k).wait_recv()
            spread(1 - core, row, k)

    for k in range(6):
        collect(0, k)
    for step in range(1, nrow - 1):
        for k in range(6):
            arrive(step, k)
            collect(step, k)
    for a in range(2):
        for d in range(1, half):
            passed(a, d).wait_recv()
            targets(a, behind(d) + 1 - 2 * core)
    for step in range(nrow - 1):
        for k in range(6):
            received(step, k)
    for k in range(6):
        @pl.when(based)
        def _():
            own(k).wait_send()

        for step in range(nrow - 1):
            for way in (1, -1):
                @pl.when(sends(way, step))
                def _():
                    relay(way, step, k).wait_send()

                @pl.when(wanted(way, step))
                def _():
                    onward(way, step, k).wait_send()
    for a in range(2):
        beside(a).wait_send()
        list_on(a).wait_send()
        for d in range(1, half):
            opposite(a, d).wait_send()
            passed(a, d).wait_send()
    list_to(i).wait_send()


def pair_kernel(tl_ref, sl_ref, lc_ref, near_ref, far_ref, v_ref, acc_ref, both_a, both_b, g_a, g_b):
    _, ncol, _, local, _ = v_ref.shape
    core = lax.rem(lax.axis_index("col"), 2)
    sub = lax.broadcasted_iota(ints, (8, 128), 0)
    low = sub < 4
    last = (sub == 3) | (sub == 7)
    scale = jnp.where(low, -2.0, 1.0).astype(f32)
    fold = jnp.where(sub == 3, 1.0, jnp.where(sub == 7, -1.0, 0.0)).astype(f32)
    some = jnp.where(low, 1.0, 0.0).astype(f32)
    unit = jnp.where(low, inv_reg, 1.0).astype(f32)
    idle = jnp.where(low, inv_reg, 0.0).astype(f32)
    nothing = jnp.zeros((32, 128), bf16)
    acc_ref[...] = jnp.zeros_like(acc_ref)
    both_b[...] = jnp.ones_like(both_b)
    g_b[...] = jnp.zeros_like(g_b)
    ends = [lc_ref[0, 0]]
    for l in range(1, 4):
        ends.append(ends[-1] + lc_ref[l, 0])
    total = ends[3]
    half = (total + 1) // 2
    first = core * half
    n = jnp.where(core == 0, half, total - half)

    def entry(j):
        j = jnp.minimum(first + jnp.clip(j, 0, jnp.maximum(n - 1, 0)), jnp.maximum(total - 1, 0))
        past = [(j >= end).astype(ints) for end in ends[:3]]
        start = jnp.where(j >= ends[2], ends[2], jnp.where(j >= ends[1], ends[1], jnp.where(j >= ends[0], ends[0], 0)))
        return past[0] + past[1] + past[2], j - start

    def tile(i):
        return pl.ds(pl.multiple_of(i * 8, 8), 8)

    def distances(block, both_ref, g_ref):
        for u in range(unroll):
            j = block * unroll + u
            l, e = entry(j)
            t, s = tl_ref[l, e], sl_ref[l, e]
            near = near_ref[tile(t), :]
            centre = jnp.where(low, pltpu.roll(near, 4, 0), 0.0)
            high, middle, rest = split3(near)
            sums = jnp.where(sub == 0, high[3:4], jnp.where(sub == 1, middle[3:4], jnp.where(sub == 2, rest[3:4], 0.0)))
            high = jnp.where(sub < 3, high, jnp.where(sub == 3, 1.0, 0.0))
            middle = jnp.where(sub < 3, middle, 0.0)
            rest = jnp.where(sub < 3, rest, 0.0)
            high_up = pltpu.roll(high, 4, 0)
            right = jnp.concatenate([
                high + pltpu.roll(middle, 4, 0), rest + high_up, middle + high_up, sums], axis=0).astype(bf16)
            shifted = (far_ref[tile(s), :] - centre) * jnp.where(j < n, unit, idle)
            prod = shifted * jnp.where(low, shifted, pltpu.roll(shifted, 4, 0))
            prod = prod + pltpu.roll(prod, 1, 0)
            prod = prod + pltpu.roll(prod, 2, 0)
            hi, mid, lo = split3(shifted * scale + prod * fold)
            hi_up, mid_up, lo_up = pltpu.roll(hi, 4, 0), pltpu.roll(mid, 4, 0), pltpu.roll(lo, 4, 0)
            left = jnp.concatenate([
                jnp.where(low, hi, hi_up), jnp.where(low, hi, mid_up), jnp.where(low, mid, lo_up), some,
                jnp.where(low, hi_up, hi), jnp.where(low, hi_up, mid), jnp.where(low, mid_up, lo),
                jnp.zeros((8, 128), f32)], axis=0).astype(bf16)
            weights = jnp.concatenate([
                jnp.concatenate([right, nothing], axis=1), jnp.concatenate([nothing, right], axis=1)], axis=0)
            both_ref[u] = lax.dot_general(left, weights, (((0,), (0,)), ((), ())), preferred_element_type=f32)
            g_ref[u] = jnp.concatenate([jnp.where(last, 1.0, hi), jnp.where(last, 0.0, mid)], axis=0).astype(bf16)

    def speeds(block, both_ref, g_ref):
        for u in range(unroll):
            l, e = entry(block * unroll + u)
            t = tl_ref[l, e]
            both, g = both_ref[u], g_ref[u]
            inv = lax.rsqrt(both[:, 0:128])
            weight = inv * inv * inv
            iso = inv + weight
            pro = both[:, 128:256] * weight
            iso_hi, pro_hi = iso.astype(bf16), pro.astype(bf16)
            iso_lo = (iso - iso_hi.astype(f32)).astype(bf16)
            pro_lo = (pro - pro_hi.astype(f32)).astype(bf16)
            m = jnp.concatenate([
                jnp.concatenate([iso_hi, pro_hi], axis=1), jnp.concatenate([iso_lo, pro_lo], axis=1)], axis=0)
            out = jnp.dot(jnp.concatenate([g, g], axis=1), m, preferred_element_type=f32)
            out = out[0:8] + out[8:16]
            from_iso, from_pro = out[:, 0:128], out[:, 128:256]
            acc_ref[tile(t), :] += pltpu.roll(from_iso, 4, 0) + near_ref[tile(t), :] * from_pro[3:4] + 0.5 * from_pro

    def many(i, carry):
        distances(2 * i, both_a, g_a)
        speeds(2 * i - 1, both_b, g_b)
        distances(2 * i + 1, both_b, g_b)
        speeds(2 * i, both_a, g_a)
        return carry

    lax.fori_loop(0, (n + unroll - 1) // unroll // 2 + 1, many, 0)
    for a in range(2):
        for c in range(ncol):
            for k in range(3):
                v_ref[a, c, k] = stokes_scale * acc_ref[pl.ds((a * ncol + c) * local * 8 + k, local, stride=8), :]


def home_kernel(
        nrow, ncol, cap, slot_ref, place_ref, cnt_ref, v_ref, out_ref, got, part, swap, outg, arr, vsend, vrecv, zsend, zrecv, asend, arecv):
    row, col = lax.axis_index("row"), lax.axis_index("col")
    local = out_ref.shape[1]
    devs = nrow * ncol
    me = row * ncol + col
    barrier = pltpu.get_barrier_semaphore()

    def peer(d):
        p = lax.rem(me + d, devs)
        return {"row": p // ncol, "col": lax.rem(p, ncol)}

    for d in range(1, devs):
        pl.semaphore_signal(barrier, inc=1, device_id=peer(d), device_id_type=MESH)
    half = ncol // 2
    core = lax.rem(col, 2)
    mine_x = col // 2

    def remote(src, dst, send, recv, where):
        return pltpu.make_async_remote_copy(
            src_ref=src, dst_ref=dst, send_sem=send, recv_sem=recv, device_id=where, device_id_type=MESH)

    keep_a = lax.rem(row, 2)
    order = (1 - keep_a, keep_a)

    def within(n, d, k):
        x = lax.rem(mine_x + d, half)
        return remote(
            v_ref.at[order[n], 2 * x + 1 - core, k], got.at[n, d, k], vsend.at[n, d, k], vrecv.at[n, d, k],
            {"col": col + 1 - 2 * core})

    def facing(d):
        return 2 * lax.rem(mine_x + d, half) + core

    def across(n, d, k):
        at = half + d - 1
        return remote(
            part.at[n, d - 1, k], got.at[n, at, k], vsend.at[n, at, k], vrecv.at[n, at, k], {"col": facing(d)})

    def exchange(k):
        return remote(swap.at[0, k], swap.at[1, k], zsend.at[k], zrecv.at[k], {"row": row + 1 - 2 * keep_a})

    def total(n, k):
        within(n, 0, k).wait_recv()
        mine = v_ref[order[n], col, k] + got[n, 0, k]
        for d in range(1, half):
            across(n, d, k).wait_recv()
            mine = mine + got[n, half + d - 1, k]
        return mine

    def deal(d, k):
        return remote(outg.at[k, lax.rem(me + d, devs)], arr.at[k, me], asend.at[d - 1, k], arecv.at[d - 1, k], peer(d))

    def move(pick, values):
        parts = jnp.concatenate(split3(values), axis=1).astype(bf16)
        moved = jnp.dot(pick, parts, preferred_element_type=f32)
        return moved[:, 0:128] + moved[:, 128:256] + moved[:, 256:384]

    pick = (lax.broadcasted_iota(ints, (devs * cap, local), 0) == slot_ref[...]).astype(f32).astype(bf16)
    pl.semaphore_wait(barrier, devs - 1)
    for n in range(2):
        for k in range(3):
            for d in [*range(1, half), 0]:
                within(n, d, k).start()

    def pass_on(n, k):
        for d in range(1, half):
            within(n, d, k).wait_recv()
            part[n, d - 1, k] = v_ref[order[n], facing(d), k] + got[n, d, k]
            across(n, d, k).start()

    for k in range(3):
        pass_on(0, k)
    for k in range(3):
        swap[0, k] = total(0, k)
        exchange(k).start()
        pass_on(1, k)
    for k in range(3):
        mine = total(1, k)
        exchange(k).wait_recv()
        outg[k] = move(pick, mine + swap[1, k]).reshape(devs, cap, 128)
        for d in range(1, devs):
            deal(d, k).start()
        arr[k, me] = outg[k, me]
    fetch = (lax.broadcasted_iota(ints, (local, devs * cap), 1) == place_ref[...]).astype(f32).astype(bf16)
    live = lax.broadcasted_iota(ints, (local, 128), 1) < cnt_ref[...]
    for k in range(3):
        for d in range(1, devs):
            deal(d, k).wait_recv()
        out_ref[k] = jnp.where(live, move(fetch, arr[k].reshape(devs * cap, 128)), 0.0)
    for k in range(3):
        exchange(k).wait_send()
        for n in range(2):
            for d in range(half):
                within(n, d, k).wait_send()
            for d in range(1, half):
                across(n, d, k).wait_send()
        for d in range(1, devs):
            deal(d, k).wait_send()


def per_device(positions, normals, curvature, pair_targets, pair_sources, pair_count, node_counts, drop_clusters, drop_owner):
    local, _, nodes = positions.shape
    nrow, ncol = lax.axis_size("row"), lax.axis_size("col")
    devs = nrow * ncol
    part, half = nrow // 2, ncol // 2
    cap = max(2, 2 * local // devs)
    slots = pair_targets.shape[1]
    dma = pltpu.SemaphoreType.DMA
    shape = jax.ShapeDtypeStruct
    near, far, tl, sl, lc, slot, place, owned_counts = pl.pallas_call(
        functools.partial(gather_kernel, nrow, ncol, cap),
        out_shape=(
            pltpu.VMEM((2 * ncol * local * 8, nodes), f32), pltpu.VMEM((2 * part * local * 8, nodes), f32),
            shape((4, slots), ints), shape((4, slots), ints), shape((4, 128), ints),
            pltpu.VMEM((1, local), ints), pltpu.VMEM((local, 1), ints), pltpu.VMEM((local, 1), ints)),
        in_specs=[HBM] * 8 + [SMEM], out_specs=(VMEM,) * 8,
        scratch_shapes=[
            pltpu.VMEM((3, local, nodes), f32), pltpu.VMEM((local, nodes), f32), *[pltpu.VMEM(drop_clusters.shape[::-1], ints)] * 2,
            pltpu.VMEM((1, drop_owner.shape[0]), ints), *[pltpu.VMEM((1, slots), ints)] * 2, dma((8,)),
            pltpu.VMEM((8, slots), ints), pltpu.VMEM((2, 2, 8, slots), ints),
            pltpu.VMEM((2, ncol, 3, local, nodes), f32), pltpu.VMEM((2, nrow, 6, local, nodes), f32),
            *[dma((2 * nrow - 2, 6))] * 4, *[dma((6,))] * 2, *[dma((2,))] * 2,
            *[dma((max(half - 1, 1), 2))] * 4, *[dma((2,))] * 4],
        compiler_params=pltpu.CompilerParams(collective_id=0, has_side_effects=True, vmem_limit_bytes=30 << 20),
        name="gather_blocks",
    )(*map(far_off, (jnp.transpose(positions, (1, 0, 2)), jnp.transpose(normals, (1, 0, 2)), curvature, node_counts.T,
                     drop_clusters.T, drop_owner[None, :], pair_targets, pair_sources)), pair_count)
    speeds = pl.pallas_call(
        pair_kernel,
        out_shape=pltpu.VMEM((2, ncol, 3, local, nodes), f32),
        in_specs=[SMEM] * 3 + [VMEM] * 2, out_specs=VMEM,
        scratch_shapes=[pltpu.VMEM((2 * ncol * local * 8, nodes), f32)]
        + [pltpu.VMEM((unroll, nodes, 2 * nodes), f32)] * 2 + [pltpu.VMEM((unroll, 16, nodes), bf16)] * 2,
        compiler_params=pltpu.CompilerParams(vmem_limit_bytes=30 << 20),
        name="pairs",
    )(tl, sl, lc, keep(near), keep(far))
    owned = pl.pallas_call(
        functools.partial(home_kernel, nrow, ncol, cap),
        out_shape=jax.ShapeDtypeStruct((3, local, nodes), f32),
        in_specs=[VMEM] * 4, out_specs=VMEM,
        scratch_shapes=[
            pltpu.VMEM((2, ncol - 1, 3, local, nodes), f32), pltpu.VMEM((2, max(half - 1, 1), 3, local, nodes), f32),
            pltpu.VMEM((2, 3, local, nodes), f32),
            pltpu.VMEM((3, devs, cap, nodes), f32), pltpu.VMEM((3, devs, cap, nodes), f32),
            dma((2, ncol - 1, 3)), dma((2, ncol - 1, 3)), dma((3,)), dma((3,)), dma((devs - 1, 3)), dma((devs - 1, 3)),
        ],
        compiler_params=pltpu.CompilerParams(collective_id=1, has_side_effects=True, vmem_limit_bytes=30 << 20),
        name="to_owners",
    )(keep(slot), keep(place), keep(owned_counts), keep(speeds))
    return jnp.transpose(owned, (1, 0, 2))


def solution(mesh):
    every = ("groups", "row", "col")
    in_specs = (
        P(every, None, None), P(every, None, None), P(every, None), P(every, None), P(every, None), P(every),
        P("groups", None), P("groups", None), P("groups"),
    )
    return jax.shard_map(per_device, mesh=mesh, in_specs=in_specs, out_specs=P(every, None, None), check_vma=False)
```

```python
import functools
import math

import jax
import jax.numpy as jnp
from jax import lax
from jax.experimental import pallas as pl
from jax.experimental.pallas import tpu as pltpu
from jax.sharding import PartitionSpec as P

regular_sq = 0.0025
inv_reg = 1.0 / math.sqrt(regular_sq)
stokes_scale = inv_reg / (8.0 * math.pi)
MESH = pl.DeviceIdType.MESH
VMEM = pl.BlockSpec(memory_space=pltpu.VMEM)
SMEM = pl.BlockSpec(memory_space=pltpu.SMEM)


HBM = pl.BlockSpec(memory_space=pltpu.HBM)
unroll = 16
f32, bf16, ints = jnp.float32, jnp.bfloat16, jnp.int32


def keep(x):
    return pltpu.with_memory_space_constraint(x, pltpu.VMEM)


def far_off(x):
    return pltpu.with_memory_space_constraint(x, pltpu.HBM)


def split3(x):
    high = x.astype(bf16).astype(f32)
    rest = x - high
    middle = rest.astype(bf16).astype(f32)
    return high, middle, rest - middle


def as_row(column):
    return jnp.transpose(jnp.broadcast_to(column, (column.shape[0], 128)))[0:1]


def gather_kernel(
        nrow, ncol, cap, pos_in, nrm_in, curv_in, nct_in, dct_in, own_in, tgt_in, src_in, count_ref,
        near_ref, far_ref, tl_ref, sl_ref, lc_ref, slot_ref, place_ref, cnt_ref,
        nrm_ref, curv_ref, nct_ref, dct_ref, own_ref, tgt_ref, src_ref, here_sem, mine_ref, lists_ref, t_ref, s_ref,
        zsend, zrecv, fsend, frecv, osend, orecv, bsend, brecv, xsend, xrecv, gsend, grecv, lsend, lrecv, hsend, hrecv):
    row, col = lax.axis_index("row"), lax.axis_index("col")
    core = lax.rem(col, 2)
    chip = col // 2
    half = ncol // 2
    part = nrow // 2
    i = lax.rem(row, 2)
    mate = row + 1 - 2 * i
    based = row // part == i
    me = row * ncol + col
    local = pos_in.shape[1]
    drops = own_ref.shape[1]
    per_drop = dct_ref.shape[0]
    slots = tgt_in.shape[1]
    pos_ref = s_ref.at[core, row, 0:3]
    loads = [pltpu.make_async_copy(src, dst, here_sem.at[n]) for n, (src, dst) in enumerate((
        (pos_in, pos_ref), (tgt_in, tgt_ref), (src_in, src_ref), (dct_in, dct_ref), (nct_in, nct_ref), (own_in, own_ref),
        (curv_in, curv_ref), (nrm_in, nrm_ref)))]
    for load in loads:
        load.start()
    barrier = pltpu.get_barrier_semaphore()
    for d in range(1, nrow):
        pl.semaphore_signal(barrier, inc=1, device_id={"row": lax.rem(row + d, nrow)}, device_id_type=MESH)
    for d in range(1, ncol):
        pl.semaphore_signal(barrier, inc=1, device_id={"col": lax.rem(col + d, ncol)}, device_id_type=MESH)

    def remote(src, dst, send, recv, where):
        return pltpu.make_async_remote_copy(
            src_ref=src, dst_ref=dst, send_sem=send, recv_sem=recv, device_id=where, device_id_type=MESH)

    sibling = {"col": col + 1 - 2 * core}

    def block_of(way, step):
        return jnp.clip(row - way * step, 0, nrow - 1)

    def relay(way, step, k):
        piece = s_ref.at[core, block_of(way, step), k]
        at = step if way > 0 else nrow - 1 + step
        return remote(piece, piece, zsend.at[at, k], zrecv.at[at, k], {"row": jnp.clip(row + way, 0, nrow - 1)})

    def reaches(way, block, place):
        inside = (block >= 0) & (block < nrow)
        half_of = jnp.clip(block, 0, nrow - 1) // part
        return inside & (place <= nrow - 2 + half_of if way > 0 else place >= half_of)

    def sends(way, step):
        return reaches(way, row - way * step, row + way)

    def receives(way, step):
        return reaches(way, row - way * (step + 1), row)

    def wanted(way, step):
        return receives(way, step) & (block_of(way, step + 1) // part == i)

    def onward(way, step, k):
        piece = s_ref.at[core, block_of(way, step + 1), k]
        at = step if way > 0 else nrow - 1 + step
        return remote(piece, piece, fsend.at[at, k], frecv.at[at, k], sibling)

    def start(way, step, k):
        @pl.when(sends(way, step))
        def _():
            relay(way, step, k).start()

    def own(k):
        piece = s_ref.at[core, row, k]
        return remote(piece, piece, osend.at[k], orecv.at[k], sibling)

    def beside(a):
        piece = t_ref.at[a, col]
        return remote(piece, piece, bsend.at[a], brecv.at[a], sibling)

    def facing(d):
        return 2 * lax.rem(chip + d, half) + core

    def opposite(a, d):
        piece = t_ref.at[a, col]
        return remote(piece, piece, xsend.at[d - 1, a], xrecv.at[d - 1, a], {"col": facing(d)})

    def behind(d):
        return 2 * lax.rem(chip + half - d, half) + core

    def passed(a, d):
        piece = t_ref.at[a, behind(d)]
        return remote(piece, piece, gsend.at[d - 1, a], grecv.at[d - 1, a], sibling)

    def share(a):
        beside(a).start()
        for d in range(1, half):
            opposite(a, d).start()

    def list_to(a):
        return remote(mine_ref, lists_ref.at[a, core], lsend.at[0], lrecv.at[0], {"row": mate})

    def list_on(a):
        piece = lists_ref.at[a, core]
        return remote(piece, piece, hsend.at[a], hrecv.at[a], sibling)

    loads[0].wait()
    pl.semaphore_wait(barrier, nrow + ncol - 2)
    for k in range(3):
        for way in (1, -1):
            start(way, 0, k)
        t_ref[i, col, k] = s_ref[core, row, k]
    share(i)
    for load in loads[1:]:
        load.wait()
    zero = jnp.zeros((1, slots), ints)
    mine_ref[...] = jnp.concatenate(
        [tgt_ref[...], src_ref[...], jnp.full((1, slots), count_ref[0], ints), zero, zero, zero, zero, zero], axis=0)
    list_to(i).start()
    lists_ref[i, core] = mine_ref[...]
    index = lax.broadcasted_iota(ints, (local, 1), 0)
    ids = me * local + index

    def match(chunk, carry):
        counts, owners = carry
        lanes = pl.ds(pl.multiple_of(chunk * 128, 128), 128)
        clusters, nodes_in, owner = dct_ref[:, lanes], nct_ref[:, lanes], own_ref[0:1, lanes]
        for k in range(per_drop):
            hit = ids == clusters[k:k + 1]
            counts = counts + jnp.where(hit, nodes_in[k:k + 1], 0)
            owners = owners + jnp.where(hit, owner, 0)
        return counts, owners

    none = jnp.zeros((local, 128), ints)
    counts, owners = lax.fori_loop(0, drops // 128, match, (none, none))
    home_counts = jnp.sum(counts, axis=1, keepdims=True, dtype=ints)
    home_owner = jnp.sum(owners, axis=1, keepdims=True, dtype=ints)
    scale = jnp.where(lax.broadcasted_iota(ints, (local, 128), 1) < home_counts, curv_ref[...], 0.0)
    for k in range(3):
        s_ref[core, row, 3 + k] = scale * nrm_ref[k]
        for way in (1, -1):
            start(way, 0, 3 + k)

    @pl.when(based)
    def _():
        for k in range(6):
            own(k).start()

    def spread(l, block, k):
        at = (l * part + lax.rem(block, part)) * local * 8 + (k if k < 3 else k + 1)
        far_ref[pl.ds(at, local, stride=8), :] = s_ref[l, block, k]

    def blank(l, r):
        for k in (3, 7):
            far_ref[pl.ds((l * part + r) * local * 8 + k, local, stride=8), :] = jnp.zeros((local, 128), f32)

    def arrive(step, k):
        for way in (1, -1):
            @pl.when(receives(way, step))
            def _():
                relay(way, step, k).wait_recv()
                if step < nrow - 2:
                    start(way, step + 1, k)

                @pl.when(wanted(way, step))
                def _():
                    onward(way, step, k).start()

    def collect(step, k):
        for way in (1, -1):
            @pl.when(wanted(way, step))
            def _():
                spread(core, block_of(way, step + 1), k)

    def received(step, k):
        for way in (1, -1):
            @pl.when(wanted(way, step))
            def _():
                onward(way, step, k).wait_recv()
                spread(1 - core, block_of(way, step + 1), k)

    def targets(a, c):
        square = jnp.ones((local, 128), f32)
        start = (a * ncol + c) * local * 8
        for k in range(3):
            coord = t_ref[a, c, k]
            centre = jnp.mean(coord, axis=1, keepdims=True)
            coord = (coord - centre) * inv_reg
            square = square + coord * coord
            near_ref[pl.ds(start + k, local, stride=8), :] = coord
            near_ref[pl.ds(start + 4 + k, local, stride=8), :] = jnp.broadcast_to(centre, coord.shape)
        near_ref[pl.ds(start + 3, local, stride=8), :] = square
        near_ref[pl.ds(start + 7, local, stride=8), :] = jnp.zeros((local, 128), f32)

    for k in range(3):
        arrive(0, k)
        t_ref[1 - i, col, k] = s_ref[core, mate, k]
    share(1 - i)
    list_to(1 - i).wait_recv()
    for a in range(2):
        list_on(a).start()

    owner_row = as_row(home_owner.astype(f32)).astype(ints)
    lane = lax.broadcasted_iota(ints, (local, local), 1)
    rank = jnp.sum(((owner_row == home_owner) & (lane < index)).astype(ints), axis=1, keepdims=True, dtype=ints)
    slot_ref[...] = as_row((home_owner * cap + rank).astype(f32)).astype(ints)
    drop_of = lax.div(index, per_drop)
    width = 256 if drops % 256 == 0 else 128
    before = (lax.broadcasted_iota(ints, (width, width), 0) < lax.broadcasted_iota(ints, (width, width), 1)).astype(bf16)

    def owned(chunk, carry):
        clusters, counted, base = carry
        lanes = pl.ds(pl.multiple_of(chunk * width, width), width)
        mine = own_ref[0:1, lanes] == me
        marks = jnp.broadcast_to(mine.astype(f32), (16, width)).astype(bf16)
        place = jnp.dot(marks, before, preferred_element_type=f32)[0:1].astype(ints) + base
        chosen = mine & (place == drop_of)
        clusters = clusters + jnp.where(chosen, jnp.concatenate([dct_ref[:, lanes]] * (local // per_drop), axis=0), 0)
        counted = counted + jnp.where(chosen, jnp.concatenate([nct_ref[:, lanes]] * (local // per_drop), axis=0), 0)
        return clusters, counted, base + jnp.sum(mine.astype(ints), axis=1, keepdims=True, dtype=ints)

    wide = jnp.zeros((local, width), ints)
    clusters, counted, _ = lax.fori_loop(0, drops // width, owned, (wide, wide, jnp.zeros((1, 1), ints)))
    clusters = jnp.sum(clusters, axis=1, keepdims=True, dtype=ints)
    cnt_ref[...] = jnp.sum(counted, axis=1, keepdims=True, dtype=ints)
    clusters_row = as_row(clusters.astype(f32)).astype(ints)
    anchor, anchor_row = lax.div(clusters, local), lax.div(clusters_row, local)
    same = (anchor == anchor_row) & (clusters_row < clusters)
    place_ref[...] = anchor * cap + jnp.sum(same.astype(ints), axis=1, keepdims=True, dtype=ints)

    for k in range(3, 6):
        arrive(0, k)
    for l in range(2):
        for r in range(part):
            blank(l, r)
    for a in range(2):
        targets(a, col)

    for a in range(2):
        list_on(a).wait_recv()
    lane_of = lax.broadcasted_iota(ints, (1, slots), 1)
    lowest = i * part * local
    square_rows = lax.broadcasted_iota(ints, (slots, slots), 0)
    earlier = (square_rows < lax.broadcasted_iota(ints, (slots, slots), 1)).astype(f32).astype(bf16)
    for a in range(2):
        for l in range(2):
            t, s, count = lists_ref[a, l, 0:1, :], lists_ref[a, l, 1:2, :], lists_ref[a, l, 2:3, :]
            taken = (lane_of < count) & (s >= lowest) & (s < lowest + part * local)
            marks = taken.astype(f32)
            ranks = jnp.dot(jnp.broadcast_to(marks, (16, slots)).astype(bf16), earlier, preferred_element_type=f32)[0:1]
            ranks = jnp.where(taken, ranks.astype(ints), -1)
            to = (square_rows == ranks).astype(f32).astype(bf16)
            digits = [lax.div(t, 256), lax.rem(t, 256), lax.div(s, 256), lax.rem(s, 256)]
            values = jnp.concatenate([v.astype(f32) for v in digits] + [jnp.zeros((12, slots), f32)], axis=0).astype(bf16)
            moved = lax.dot_general(values, to, (((1,), (1,)), ((), ())), preferred_element_type=f32).astype(ints)
            n = a * 2 + l
            tl_ref[n:n + 1, :] = moved[0:1] * 256 + moved[1:2] + a * ncol * local
            sl_ref[n:n + 1, :] = jnp.maximum(moved[2:3] * 256 + moved[3:4] - lowest, 0) + l * part * local
            lc_ref[n:n + 1, :] = jnp.broadcast_to(jnp.sum(marks, axis=1, keepdims=True).astype(ints), (1, 128))

    for a in range(2):
        for d in range(1, half):
            opposite(a, d).wait_recv()
            passed(a, d).start()
        beside(a).wait_recv()
        targets(a, col + 1 - 2 * core)
        for d in range(1, half):
            targets(a, behind(d))
    @pl.when(based)
    def _():
        for k in range(6):
            spread(core, row, k)
            own(k).wait_recv()
            spread(1 - core, row, k)

    for k in range(6):
        collect(0, k)
    for step in range(1, nrow - 1):
        for k in range(6):
            arrive(step, k)
            collect(step, k)
    for a in range(2):
        for d in range(1, half):
            passed(a, d).wait_recv()
            targets(a, behind(d) + 1 - 2 * core)
    for step in range(nrow - 1):
        for k in range(6):
            received(step, k)
    for k in range(6):
        @pl.when(based)
        def _():
            own(k).wait_send()

        for step in range(nrow - 1):
            for way in (1, -1):
                @pl.when(sends(way, step))
                def _():
                    relay(way, step, k).wait_send()

                @pl.when(wanted(way, step))
                def _():
                    onward(way, step, k).wait_send()
    for a in range(2):
        beside(a).wait_send()
        list_on(a).wait_send()
        for d in range(1, half):
            opposite(a, d).wait_send()
            passed(a, d).wait_send()
    list_to(i).wait_send()


def pair_kernel(tl_ref, sl_ref, lc_ref, near_ref, far_ref, v_ref, acc_ref, both_a, both_b, g_a, g_b):
    _, ncol, _, local, _ = v_ref.shape
    core = lax.rem(lax.axis_index("col"), 2)
    sub = lax.broadcasted_iota(ints, (8, 128), 0)
    low = sub < 4
    last = (sub == 3) | (sub == 7)
    scale = jnp.where(low, -2.0, 1.0).astype(f32)
    fold = jnp.where(sub == 3, 1.0, jnp.where(sub == 7, -1.0, 0.0)).astype(f32)
    some = jnp.where(low, 1.0, 0.0).astype(f32)
    unit = jnp.where(low, inv_reg, 1.0).astype(f32)
    idle = jnp.where(low, inv_reg, 0.0).astype(f32)
    nothing = jnp.zeros((32, 128), bf16)
    acc_ref[...] = jnp.zeros_like(acc_ref)
    both_b[...] = jnp.ones_like(both_b)
    g_b[...] = jnp.zeros_like(g_b)
    ends = [lc_ref[0, 0]]
    for l in range(1, 4):
        ends.append(ends[-1] + lc_ref[l, 0])
    total = ends[3]
    half = (total + 1) // 2
    first = core * half
    n = jnp.where(core == 0, half, total - half)

    def entry(j):
        j = jnp.minimum(first + jnp.clip(j, 0, jnp.maximum(n - 1, 0)), jnp.maximum(total - 1, 0))
        past = [(j >= end).astype(ints) for end in ends[:3]]
        start = jnp.where(j >= ends[2], ends[2], jnp.where(j >= ends[1], ends[1], jnp.where(j >= ends[0], ends[0], 0)))
        return past[0] + past[1] + past[2], j - start

    def tile(i):
        return pl.ds(pl.multiple_of(i * 8, 8), 8)

    def distances(block, both_ref, g_ref):
        for u in range(unroll):
            j = block * unroll + u
            l, e = entry(j)
            t, s = tl_ref[l, e], sl_ref[l, e]
            near = near_ref[tile(t), :]
            centre = jnp.where(low, pltpu.roll(near, 4, 0), 0.0)
            high, middle, rest = split3(near)
            sums = jnp.where(sub == 0, high[3:4], jnp.where(sub == 1, middle[3:4], jnp.where(sub == 2, rest[3:4], 0.0)))
            high = jnp.where(sub < 3, high, jnp.where(sub == 3, 1.0, 0.0))
            middle = jnp.where(sub < 3, middle, 0.0)
            rest = jnp.where(sub < 3, rest, 0.0)
            high_up = pltpu.roll(high, 4, 0)
            right = jnp.concatenate([
                high + pltpu.roll(middle, 4, 0), rest + high_up, middle + high_up, sums], axis=0).astype(bf16)
            shifted = (far_ref[tile(s), :] - centre) * jnp.where(j < n, unit, idle)
            prod = shifted * jnp.where(low, shifted, pltpu.roll(shifted, 4, 0))
            prod = prod + pltpu.roll(prod, 1, 0)
            prod = prod + pltpu.roll(prod, 2, 0)
            hi, mid, lo = split3(shifted * scale + prod * fold)
            hi_up, mid_up, lo_up = pltpu.roll(hi, 4, 0), pltpu.roll(mid, 4, 0), pltpu.roll(lo, 4, 0)
            left = jnp.concatenate([
                jnp.where(low, hi, hi_up), jnp.where(low, hi, mid_up), jnp.where(low, mid, lo_up), some,
                jnp.where(low, hi_up, hi), jnp.where(low, hi_up, mid), jnp.where(low, mid_up, lo),
                jnp.zeros((8, 128), f32)], axis=0).astype(bf16)
            weights = jnp.concatenate([
                jnp.concatenate([right, nothing], axis=1), jnp.concatenate([nothing, right], axis=1)], axis=0)
            both_ref[u] = lax.dot_general(left, weights, (((0,), (0,)), ((), ())), preferred_element_type=f32)
            g_ref[u] = jnp.concatenate([jnp.where(last, 1.0, hi), jnp.where(last, 0.0, mid)], axis=0).astype(bf16)

    def speeds(block, both_ref, g_ref):
        for u in range(unroll):
            l, e = entry(block * unroll + u)
            t = tl_ref[l, e]
            both, g = both_ref[u], g_ref[u]
            inv = lax.rsqrt(both[:, 0:128])
            weight = inv * inv * inv
            iso = inv + weight
            pro = both[:, 128:256] * weight
            iso_hi, pro_hi = iso.astype(bf16), pro.astype(bf16)
            iso_lo = (iso - iso_hi.astype(f32)).astype(bf16)
            pro_lo = (pro - pro_hi.astype(f32)).astype(bf16)
            m = jnp.concatenate([
                jnp.concatenate([iso_hi, pro_hi], axis=1), jnp.concatenate([iso_lo, pro_lo], axis=1)], axis=0)
            out = jnp.dot(jnp.concatenate([g, g], axis=1), m, preferred_element_type=f32)
            out = out[0:8] + out[8:16]
            from_iso, from_pro = out[:, 0:128], out[:, 128:256]
            acc_ref[tile(t), :] += pltpu.roll(from_iso, 4, 0) + near_ref[tile(t), :] * from_pro[3:4] + 0.5 * from_pro

    def many(i, carry):
        distances(2 * i, both_a, g_a)
        speeds(2 * i - 1, both_b, g_b)
        distances(2 * i + 1, both_b, g_b)
        speeds(2 * i, both_a, g_a)
        return carry

    blocks = (n + unroll - 1) // unroll
    lax.fori_loop(0, blocks // 2, many, 0)
    tail = lax.rem(blocks, 2) == 1

    @pl.when(tail)
    def _():
        distances(blocks - 1, both_a, g_a)
        speeds(blocks - 2, both_b, g_b)
        speeds(blocks - 1, both_a, g_a)

    @pl.when(jnp.logical_not(tail))
    def _():
        speeds(blocks - 1, both_b, g_b)

    for a in range(2):
        for c in range(ncol):
            for k in range(3):
                v_ref[a, c, k] = stokes_scale * acc_ref[pl.ds((a * ncol + c) * local * 8 + k, local, stride=8), :]


def home_kernel(
        nrow, ncol, cap, slot_ref, place_ref, cnt_ref, v_ref, out_ref, got, part, swap, outg, arr, vsend, vrecv, zsend, zrecv, asend, arecv):
    row, col = lax.axis_index("row"), lax.axis_index("col")
    local = out_ref.shape[1]
    devs = nrow * ncol
    me = row * ncol + col
    barrier = pltpu.get_barrier_semaphore()

    def peer(d):
        p = lax.rem(me + d, devs)
        return {"row": p // ncol, "col": lax.rem(p, ncol)}

    for d in range(1, devs):
        pl.semaphore_signal(barrier, inc=1, device_id=peer(d), device_id_type=MESH)
    half = ncol // 2
    core = lax.rem(col, 2)
    mine_x = col // 2

    def remote(src, dst, send, recv, where):
        return pltpu.make_async_remote_copy(
            src_ref=src, dst_ref=dst, send_sem=send, recv_sem=recv, device_id=where, device_id_type=MESH)

    keep_a = lax.rem(row, 2)
    order = (1 - keep_a, keep_a)

    def within(n, d, k):
        x = lax.rem(mine_x + d, half)
        return remote(
            v_ref.at[order[n], 2 * x + 1 - core, k], got.at[n, d, k], vsend.at[n, d, k], vrecv.at[n, d, k],
            {"col": col + 1 - 2 * core})

    def facing(d):
        return 2 * lax.rem(mine_x + d, half) + core

    def across(n, d, k):
        at = half + d - 1
        return remote(
            part.at[n, d - 1, k], got.at[n, at, k], vsend.at[n, at, k], vrecv.at[n, at, k], {"col": facing(d)})

    def exchange(k):
        return remote(swap.at[0, k], swap.at[1, k], zsend.at[k], zrecv.at[k], {"row": row + 1 - 2 * keep_a})

    def total(n, k):
        within(n, 0, k).wait_recv()
        mine = v_ref[order[n], col, k] + got[n, 0, k]
        for d in range(1, half):
            across(n, d, k).wait_recv()
            mine = mine + got[n, half + d - 1, k]
        return mine

    def deal(d, k):
        return remote(outg.at[k, lax.rem(me + d, devs)], arr.at[k, me], asend.at[d - 1, k], arecv.at[d - 1, k], peer(d))

    def move(pick, values):
        parts = jnp.concatenate(split3(values), axis=1).astype(bf16)
        moved = jnp.dot(pick, parts, preferred_element_type=f32)
        return moved[:, 0:128] + moved[:, 128:256] + moved[:, 256:384]

    pick = (lax.broadcasted_iota(ints, (devs * cap, local), 0) == slot_ref[...]).astype(f32).astype(bf16)
    pl.semaphore_wait(barrier, devs - 1)
    for k in range(3):
        for n in range(2):
            for d in [*range(1, half), 0]:
                within(n, d, k).start()

    def pass_on(n, k):
        for d in range(1, half):
            within(n, d, k).wait_recv()
            part[n, d - 1, k] = v_ref[order[n], facing(d), k] + got[n, d, k]
            across(n, d, k).start()

    def finish(k):
        mine = total(1, k)
        exchange(k).wait_recv()
        outg[k] = move(pick, mine + swap[1, k]).reshape(devs, cap, 128)
        for d in range(1, devs):
            deal(d, k).start()
        arr[k, me] = outg[k, me]

    for k in range(3):
        pass_on(0, k)
        pass_on(1, k)
    for k in range(3):
        swap[0, k] = total(0, k)
        exchange(k).start()
        if k > 0:
            finish(k - 1)
    finish(2)
    fetch = (lax.broadcasted_iota(ints, (local, devs * cap), 1) == place_ref[...]).astype(f32).astype(bf16)
    live = lax.broadcasted_iota(ints, (local, 128), 1) < cnt_ref[...]
    for k in range(3):
        for d in range(1, devs):
            deal(d, k).wait_recv()
        out_ref[k] = jnp.where(live, move(fetch, arr[k].reshape(devs * cap, 128)), 0.0)
    for k in range(3):
        exchange(k).wait_send()
        for n in range(2):
            for d in range(half):
                within(n, d, k).wait_send()
            for d in range(1, half):
                across(n, d, k).wait_send()
        for d in range(1, devs):
            deal(d, k).wait_send()


def per_device(positions, normals, curvature, pair_targets, pair_sources, pair_count, node_counts, drop_clusters, drop_owner):
    local, _, nodes = positions.shape
    nrow, ncol = lax.axis_size("row"), lax.axis_size("col")
    devs = nrow * ncol
    part, half = nrow // 2, ncol // 2
    cap = max(2, 2 * local // devs)
    slots = pair_targets.shape[1]
    dma = pltpu.SemaphoreType.DMA
    shape = jax.ShapeDtypeStruct
    near, far, tl, sl, lc, slot, place, owned_counts = pl.pallas_call(
        functools.partial(gather_kernel, nrow, ncol, cap),
        out_shape=(
            pltpu.VMEM((2 * ncol * local * 8, nodes), f32), pltpu.VMEM((2 * part * local * 8, nodes), f32),
            shape((4, slots), ints), shape((4, slots), ints), shape((4, 128), ints),
            pltpu.VMEM((1, local), ints), pltpu.VMEM((local, 1), ints), pltpu.VMEM((local, 1), ints)),
        in_specs=[HBM] * 8 + [SMEM], out_specs=(VMEM,) * 8,
        scratch_shapes=[
            pltpu.VMEM((3, local, nodes), f32), pltpu.VMEM((local, nodes), f32), *[pltpu.VMEM(drop_clusters.shape[::-1], ints)] * 2,
            pltpu.VMEM((1, drop_owner.shape[0]), ints), *[pltpu.VMEM((1, slots), ints)] * 2, dma((8,)),
            pltpu.VMEM((8, slots), ints), pltpu.VMEM((2, 2, 8, slots), ints),
            pltpu.VMEM((2, ncol, 3, local, nodes), f32), pltpu.VMEM((2, nrow, 6, local, nodes), f32),
            *[dma((2 * nrow - 2, 6))] * 4, *[dma((6,))] * 2, *[dma((2,))] * 2,
            *[dma((max(half - 1, 1), 2))] * 4, *[dma((2,))] * 4],
        compiler_params=pltpu.CompilerParams(collective_id=0, has_side_effects=True, vmem_limit_bytes=30 << 20),
        name="gather_blocks",
    )(*map(far_off, (jnp.transpose(positions, (1, 0, 2)), jnp.transpose(normals, (1, 0, 2)), curvature, node_counts.T,
                     drop_clusters.T, drop_owner[None, :], pair_targets, pair_sources)), pair_count)
    speeds = pl.pallas_call(
        pair_kernel,
        out_shape=pltpu.VMEM((2, ncol, 3, local, nodes), f32),
        in_specs=[SMEM] * 3 + [VMEM] * 2, out_specs=VMEM,
        scratch_shapes=[pltpu.VMEM((2 * ncol * local * 8, nodes), f32)]
        + [pltpu.VMEM((unroll, nodes, 2 * nodes), f32)] * 2 + [pltpu.VMEM((unroll, 16, nodes), bf16)] * 2,
        compiler_params=pltpu.CompilerParams(vmem_limit_bytes=30 << 20),
        name="pairs",
    )(tl, sl, lc, keep(near), keep(far))
    owned = pl.pallas_call(
        functools.partial(home_kernel, nrow, ncol, cap),
        out_shape=jax.ShapeDtypeStruct((3, local, nodes), f32),
        in_specs=[VMEM] * 4, out_specs=VMEM,
        scratch_shapes=[
            pltpu.VMEM((2, ncol - 1, 3, local, nodes), f32), pltpu.VMEM((2, max(half - 1, 1), 3, local, nodes), f32),
            pltpu.VMEM((2, 3, local, nodes), f32),
            pltpu.VMEM((3, devs, cap, nodes), f32), pltpu.VMEM((3, devs, cap, nodes), f32),
            dma((2, ncol - 1, 3)), dma((2, ncol - 1, 3)), dma((3,)), dma((3,)), dma((devs - 1, 3)), dma((devs - 1, 3)),
        ],
        compiler_params=pltpu.CompilerParams(collective_id=1, has_side_effects=True, vmem_limit_bytes=30 << 20),
        name="to_owners",
    )(keep(slot), keep(place), keep(owned_counts), keep(speeds))
    return jnp.transpose(owned, (1, 0, 2))


def solution(mesh):
    every = ("groups", "row", "col")
    in_specs = (
        P(every, None, None), P(every, None, None), P(every, None), P(every, None), P(every, None), P(every),
        P("groups", None), P("groups", None), P("groups"),
    )
    return jax.shard_map(per_device, mesh=mesh, in_specs=in_specs, out_specs=P(every, None, None), check_vma=False)
```

```python
import functools
import math

import jax
import jax.numpy as jnp
from jax import lax
from jax.experimental import pallas as pl
from jax.experimental.pallas import tpu as pltpu
from jax.sharding import PartitionSpec as P

regular_sq = 0.0025
inv_reg = 1.0 / math.sqrt(regular_sq)
stokes_scale = inv_reg / (8.0 * math.pi)
MESH = pl.DeviceIdType.MESH
VMEM = pl.BlockSpec(memory_space=pltpu.VMEM)
SMEM = pl.BlockSpec(memory_space=pltpu.SMEM)


HBM = pl.BlockSpec(memory_space=pltpu.HBM)
unroll = 16
f32, bf16, ints = jnp.float32, jnp.bfloat16, jnp.int32


def keep(x):
    return pltpu.with_memory_space_constraint(x, pltpu.VMEM)


def far_off(x):
    return pltpu.with_memory_space_constraint(x, pltpu.HBM)


def split3(x):
    high = x.astype(bf16).astype(f32)
    rest = x - high
    middle = rest.astype(bf16).astype(f32)
    return high, middle, rest - middle


def as_row(column):
    return jnp.transpose(jnp.broadcast_to(column, (column.shape[0], 128)))[0:1]


def gather_kernel(
        nrow, ncol, cap, pos_in, nrm_in, curv_in, nct_in, dct_in, own_in, tgt_in, src_in, count_ref,
        near_ref, far_ref, tl_ref, sl_ref, lc_ref, slot_ref, place_ref, cnt_ref,
        nrm_ref, curv_ref, nct_ref, dct_ref, own_ref, tgt_ref, src_ref, here_sem, mine_ref, lists_ref, t_ref, s_ref,
        zsend, zrecv, fsend, frecv, osend, orecv, bsend, brecv, xsend, xrecv, gsend, grecv, lsend, lrecv, hsend, hrecv):
    row, col = lax.axis_index("row"), lax.axis_index("col")
    core = lax.rem(col, 2)
    chip = col // 2
    half = ncol // 2
    part = nrow // 2
    i = lax.rem(row, 2)
    mate = row + 1 - 2 * i
    based = row // part == i
    me = row * ncol + col
    local = pos_in.shape[1]
    drops = own_ref.shape[1]
    per_drop = dct_ref.shape[0]
    slots = tgt_in.shape[1]
    pos_ref = s_ref.at[core, row, 0:3]
    loads = [pltpu.make_async_copy(src, dst, here_sem.at[n]) for n, (src, dst) in enumerate((
        (pos_in, pos_ref), (tgt_in, tgt_ref), (src_in, src_ref), (dct_in, dct_ref), (nct_in, nct_ref), (own_in, own_ref),
        (curv_in, curv_ref), (nrm_in, nrm_ref)))]
    for load in loads:
        load.start()
    barrier = pltpu.get_barrier_semaphore()
    for d in range(1, nrow):
        pl.semaphore_signal(barrier, inc=1, device_id={"row": lax.rem(row + d, nrow)}, device_id_type=MESH)
    for d in range(1, ncol):
        pl.semaphore_signal(barrier, inc=1, device_id={"col": lax.rem(col + d, ncol)}, device_id_type=MESH)

    def remote(src, dst, send, recv, where):
        return pltpu.make_async_remote_copy(
            src_ref=src, dst_ref=dst, send_sem=send, recv_sem=recv, device_id=where, device_id_type=MESH)

    sibling = {"col": col + 1 - 2 * core}

    def block_of(way, step):
        return jnp.clip(row - way * step, 0, nrow - 1)

    def relay(way, step, k):
        piece = s_ref.at[core, block_of(way, step), k]
        at = step if way > 0 else nrow - 1 + step
        return remote(piece, piece, zsend.at[at, k], zrecv.at[at, k], {"row": jnp.clip(row + way, 0, nrow - 1)})

    def reaches(way, block, place):
        inside = (block >= 0) & (block < nrow)
        half_of = jnp.clip(block, 0, nrow - 1) // part
        return inside & (place <= nrow - 2 + half_of if way > 0 else place >= half_of)

    def sends(way, step):
        return reaches(way, row - way * step, row + way)

    def receives(way, step):
        return reaches(way, row - way * (step + 1), row)

    def wanted(way, step):
        return receives(way, step) & (block_of(way, step + 1) // part == i)

    def onward(way, step, k):
        piece = s_ref.at[core, block_of(way, step + 1), k]
        at = step if way > 0 else nrow - 1 + step
        return remote(piece, piece, fsend.at[at, k], frecv.at[at, k], sibling)

    def start(way, step, k):
        @pl.when(sends(way, step))
        def _():
            relay(way, step, k).start()

    def own(k):
        piece = s_ref.at[core, row, k]
        return remote(piece, piece, osend.at[k], orecv.at[k], sibling)

    def beside(a):
        piece = t_ref.at[a, col]
        return remote(piece, piece, bsend.at[a], brecv.at[a], sibling)

    def facing(d):
        return 2 * lax.rem(chip + d, half) + core

    def opposite(a, d):
        piece = t_ref.at[a, col]
        return remote(piece, piece, xsend.at[d - 1, a], xrecv.at[d - 1, a], {"col": facing(d)})

    def behind(d):
        return 2 * lax.rem(chip + half - d, half) + core

    def passed(a, d):
        piece = t_ref.at[a, behind(d)]
        return remote(piece, piece, gsend.at[d - 1, a], grecv.at[d - 1, a], sibling)

    def share(a):
        beside(a).start()
        for d in range(1, half):
            opposite(a, d).start()

    def list_to(a):
        return remote(mine_ref, lists_ref.at[a, core], lsend.at[0], lrecv.at[0], {"row": mate})

    def list_on(a):
        piece = lists_ref.at[a, core]
        return remote(piece, piece, hsend.at[a], hrecv.at[a], sibling)

    loads[0].wait()
    pl.semaphore_wait(barrier, nrow + ncol - 2)
    for k in range(3):
        for way in (1, -1):
            start(way, 0, k)
        t_ref[i, col, k] = s_ref[core, row, k]
    share(i)
    for load in loads[1:]:
        load.wait()
    zero = jnp.zeros((1, slots), ints)
    mine_ref[...] = jnp.concatenate(
        [tgt_ref[...], src_ref[...], jnp.full((1, slots), count_ref[0], ints), zero, zero, zero, zero, zero], axis=0)
    list_to(i).start()
    lists_ref[i, core] = mine_ref[...]
    index = lax.broadcasted_iota(ints, (local, 1), 0)
    ids = me * local + index

    def match(chunk, carry):
        counts, owners = carry
        lanes = pl.ds(pl.multiple_of(chunk * 128, 128), 128)
        clusters, nodes_in, owner = dct_ref[:, lanes], nct_ref[:, lanes], own_ref[0:1, lanes]
        for k in range(per_drop):
            hit = ids == clusters[k:k + 1]
            counts = counts + jnp.where(hit, nodes_in[k:k + 1], 0)
            owners = owners + jnp.where(hit, owner, 0)
        return counts, owners

    none = jnp.zeros((local, 128), ints)
    counts, owners = lax.fori_loop(0, drops // 128, match, (none, none))
    home_counts = jnp.sum(counts, axis=1, keepdims=True, dtype=ints)
    home_owner = jnp.sum(owners, axis=1, keepdims=True, dtype=ints)
    scale = jnp.where(lax.broadcasted_iota(ints, (local, 128), 1) < home_counts, curv_ref[...], 0.0)
    for k in range(3):
        s_ref[core, row, 3 + k] = scale * nrm_ref[k]
        for way in (1, -1):
            start(way, 0, 3 + k)

    @pl.when(based)
    def _():
        for k in range(6):
            own(k).start()

    def spread(l, block, k):
        at = (l * part + lax.rem(block, part)) * local * 8 + (k if k < 3 else k + 1)
        far_ref[pl.ds(at, local, stride=8), :] = s_ref[l, block, k]

    def blank(l, r):
        for k in (3, 7):
            far_ref[pl.ds((l * part + r) * local * 8 + k, local, stride=8), :] = jnp.zeros((local, 128), f32)

    def arrive(step, k):
        for way in (1, -1):
            @pl.when(receives(way, step))
            def _():
                relay(way, step, k).wait_recv()
                if step < nrow - 2:
                    start(way, step + 1, k)

                @pl.when(wanted(way, step))
                def _():
                    onward(way, step, k).start()

    def collect(step, k):
        for way in (1, -1):
            @pl.when(wanted(way, step))
            def _():
                spread(core, block_of(way, step + 1), k)

    def received(step, k):
        for way in (1, -1):
            @pl.when(wanted(way, step))
            def _():
                onward(way, step, k).wait_recv()
                spread(1 - core, block_of(way, step + 1), k)

    def targets(a, c):
        square = jnp.ones((local, 128), f32)
        start = (a * ncol + c) * local * 8
        for k in range(3):
            coord = t_ref[a, c, k]
            centre = jnp.mean(coord, axis=1, keepdims=True)
            coord = (coord - centre) * inv_reg
            square = square + coord * coord
            near_ref[pl.ds(start + k, local, stride=8), :] = coord
            near_ref[pl.ds(start + 4 + k, local, stride=8), :] = jnp.broadcast_to(centre, coord.shape)
        near_ref[pl.ds(start + 3, local, stride=8), :] = square
        near_ref[pl.ds(start + 7, local, stride=8), :] = jnp.zeros((local, 128), f32)

    for k in range(3):
        arrive(0, k)
        t_ref[1 - i, col, k] = s_ref[core, mate, k]
    share(1 - i)
    list_to(1 - i).wait_recv()
    for a in range(2):
        list_on(a).start()

    owner_row = as_row(home_owner.astype(f32)).astype(ints)
    lane = lax.broadcasted_iota(ints, (local, local), 1)
    rank = jnp.sum(((owner_row == home_owner) & (lane < index)).astype(ints), axis=1, keepdims=True, dtype=ints)
    slot_ref[...] = as_row((home_owner * cap + rank).astype(f32)).astype(ints)
    drop_of = lax.div(index, per_drop)
    width = 256 if drops % 256 == 0 else 128
    before = (lax.broadcasted_iota(ints, (width, width), 0) < lax.broadcasted_iota(ints, (width, width), 1)).astype(bf16)

    def owned(chunk, carry):
        clusters, counted, base = carry
        lanes = pl.ds(pl.multiple_of(chunk * width, width), width)
        mine = own_ref[0:1, lanes] == me
        marks = jnp.broadcast_to(mine.astype(f32), (16, width)).astype(bf16)
        place = jnp.dot(marks, before, preferred_element_type=f32)[0:1].astype(ints) + base
        chosen = mine & (place == drop_of)
        clusters = clusters + jnp.where(chosen, jnp.concatenate([dct_ref[:, lanes]] * (local // per_drop), axis=0), 0)
        counted = counted + jnp.where(chosen, jnp.concatenate([nct_ref[:, lanes]] * (local // per_drop), axis=0), 0)
        return clusters, counted, base + jnp.sum(mine.astype(ints), axis=1, keepdims=True, dtype=ints)

    wide = jnp.zeros((local, width), ints)
    clusters, counted, _ = lax.fori_loop(0, drops // width, owned, (wide, wide, jnp.zeros((1, 1), ints)))
    clusters = jnp.sum(clusters, axis=1, keepdims=True, dtype=ints)
    cnt_ref[...] = jnp.sum(counted, axis=1, keepdims=True, dtype=ints)
    clusters_row = as_row(clusters.astype(f32)).astype(ints)
    anchor, anchor_row = lax.div(clusters, local), lax.div(clusters_row, local)
    same = (anchor == anchor_row) & (clusters_row < clusters)
    place_ref[...] = anchor * cap + jnp.sum(same.astype(ints), axis=1, keepdims=True, dtype=ints)

    for k in range(3, 6):
        arrive(0, k)
    for l in range(2):
        for r in range(part):
            blank(l, r)
    for a in range(2):
        targets(a, col)

    for a in range(2):
        list_on(a).wait_recv()
    lane_of = lax.broadcasted_iota(ints, (1, slots), 1)
    lowest = i * part * local
    square_rows = lax.broadcasted_iota(ints, (slots, slots), 0)
    earlier = (square_rows < lax.broadcasted_iota(ints, (slots, slots), 1)).astype(f32).astype(bf16)
    for a in range(2):
        for l in range(2):
            t, s, count = lists_ref[a, l, 0:1, :], lists_ref[a, l, 1:2, :], lists_ref[a, l, 2:3, :]
            taken = (lane_of < count) & (s >= lowest) & (s < lowest + part * local)
            marks = taken.astype(f32)
            ranks = jnp.dot(jnp.broadcast_to(marks, (16, slots)).astype(bf16), earlier, preferred_element_type=f32)[0:1]
            ranks = jnp.where(taken, ranks.astype(ints), -1)
            to = (square_rows == ranks).astype(f32).astype(bf16)
            digits = [lax.div(t, 256), lax.rem(t, 256), lax.div(s, 256), lax.rem(s, 256)]
            values = jnp.concatenate([v.astype(f32) for v in digits] + [jnp.zeros((12, slots), f32)], axis=0).astype(bf16)
            moved = lax.dot_general(values, to, (((1,), (1,)), ((), ())), preferred_element_type=f32).astype(ints)
            n = a * 2 + l
            tl_ref[n:n + 1, :] = moved[0:1] * 256 + moved[1:2] + a * ncol * local
            sl_ref[n:n + 1, :] = jnp.maximum(moved[2:3] * 256 + moved[3:4] - lowest, 0) + l * part * local
            lc_ref[n:n + 1, :] = jnp.broadcast_to(jnp.sum(marks, axis=1, keepdims=True).astype(ints), (1, 128))

    for a in range(2):
        for d in range(1, half):
            opposite(a, d).wait_recv()
            passed(a, d).start()
        beside(a).wait_recv()
        targets(a, col + 1 - 2 * core)
        for d in range(1, half):
            targets(a, behind(d))
    @pl.when(based)
    def _():
        for k in range(6):
            spread(core, row, k)
            own(k).wait_recv()
            spread(1 - core, row, k)

    for k in range(6):
        collect(0, k)
    for step in range(1, nrow - 1):
        for k in range(6):
            arrive(step, k)
            collect(step, k)
    for a in range(2):
        for d in range(1, half):
            passed(a, d).wait_recv()
            targets(a, behind(d) + 1 - 2 * core)
    for step in range(nrow - 1):
        for k in range(6):
            received(step, k)
    for k in range(6):
        @pl.when(based)
        def _():
            own(k).wait_send()

        for step in range(nrow - 1):
            for way in (1, -1):
                @pl.when(sends(way, step))
                def _():
                    relay(way, step, k).wait_send()

                @pl.when(wanted(way, step))
                def _():
                    onward(way, step, k).wait_send()
    for a in range(2):
        beside(a).wait_send()
        list_on(a).wait_send()
        for d in range(1, half):
            opposite(a, d).wait_send()
            passed(a, d).wait_send()
    list_to(i).wait_send()


def pair_kernel(tl_ref, sl_ref, lc_ref, near_ref, far_ref, v_ref, acc_ref, both_a, both_b, g_a, g_b):
    _, ncol, _, local, _ = v_ref.shape
    core = lax.rem(lax.axis_index("col"), 2)
    sub = lax.broadcasted_iota(ints, (8, 128), 0)
    low = sub < 4
    last = (sub == 3) | (sub == 7)
    scale = jnp.where(low, -2.0, 1.0).astype(f32)
    fold = jnp.where(sub == 3, 1.0, jnp.where(sub == 7, -1.0, 0.0)).astype(f32)
    some = jnp.where(low, 1.0, 0.0).astype(f32)
    unit = jnp.where(low, inv_reg, 1.0).astype(f32)
    idle = jnp.where(low, inv_reg, 0.0).astype(f32)
    nothing = jnp.zeros((32, 128), bf16)
    acc_ref[...] = jnp.zeros_like(acc_ref)
    both_b[...] = jnp.ones_like(both_b)
    g_b[...] = jnp.zeros_like(g_b)
    ends = [lc_ref[0, 0]]
    for l in range(1, 4):
        ends.append(ends[-1] + lc_ref[l, 0])
    total = ends[3]
    half = (total + 1) // 2
    first = core * half
    n = jnp.where(core == 0, half, total - half)

    def entry(j):
        j = jnp.minimum(first + jnp.clip(j, 0, jnp.maximum(n - 1, 0)), jnp.maximum(total - 1, 0))
        past = [(j >= end).astype(ints) for end in ends[:3]]
        start = jnp.where(j >= ends[2], ends[2], jnp.where(j >= ends[1], ends[1], jnp.where(j >= ends[0], ends[0], 0)))
        return past[0] + past[1] + past[2], j - start

    def tile(i):
        return pl.ds(pl.multiple_of(i * 8, 8), 8)

    def distances(block, both_ref, g_ref, us=range(unroll)):
        for u in us:
            j = block * unroll + u
            l, e = entry(j)
            t, s = tl_ref[l, e], sl_ref[l, e]
            near = near_ref[tile(t), :]
            centre = jnp.where(low, pltpu.roll(near, 4, 0), 0.0)
            high, middle, rest = split3(near)
            sums = jnp.where(sub == 0, high[3:4], jnp.where(sub == 1, middle[3:4], jnp.where(sub == 2, rest[3:4], 0.0)))
            high = jnp.where(sub < 3, high, jnp.where(sub == 3, 1.0, 0.0))
            middle = jnp.where(sub < 3, middle, 0.0)
            rest = jnp.where(sub < 3, rest, 0.0)
            high_up = pltpu.roll(high, 4, 0)
            right = jnp.concatenate([
                high + pltpu.roll(middle, 4, 0), rest + high_up, middle + high_up, sums], axis=0).astype(bf16)
            shifted = (far_ref[tile(s), :] - centre) * jnp.where(j < n, unit, idle)
            prod = shifted * jnp.where(low, shifted, pltpu.roll(shifted, 4, 0))
            prod = prod + pltpu.roll(prod, 1, 0)
            prod = prod + pltpu.roll(prod, 2, 0)
            hi, mid, lo = split3(shifted * scale + prod * fold)
            hi_up, mid_up, lo_up = pltpu.roll(hi, 4, 0), pltpu.roll(mid, 4, 0), pltpu.roll(lo, 4, 0)
            left = jnp.concatenate([
                jnp.where(low, hi, hi_up), jnp.where(low, hi, mid_up), jnp.where(low, mid, lo_up), some,
                jnp.where(low, hi_up, hi), jnp.where(low, hi_up, mid), jnp.where(low, mid_up, lo),
                jnp.zeros((8, 128), f32)], axis=0).astype(bf16)
            weights = jnp.concatenate([
                jnp.concatenate([right, nothing], axis=1), jnp.concatenate([nothing, right], axis=1)], axis=0)
            both_ref[u] = lax.dot_general(left, weights, (((0,), (0,)), ((), ())), preferred_element_type=f32)
            g_ref[u] = jnp.concatenate([jnp.where(last, 1.0, hi), jnp.where(last, 0.0, mid)], axis=0).astype(bf16)

    def speeds(block, both_ref, g_ref, us=range(unroll)):
        for u in us:
            l, e = entry(block * unroll + u)
            t = tl_ref[l, e]
            both, g = both_ref[u], g_ref[u]
            inv = lax.rsqrt(both[:, 0:128])
            weight = inv * inv * inv
            iso = inv + weight
            pro = both[:, 128:256] * weight
            iso_hi, pro_hi = iso.astype(bf16), pro.astype(bf16)
            iso_lo = (iso - iso_hi.astype(f32)).astype(bf16)
            pro_lo = (pro - pro_hi.astype(f32)).astype(bf16)
            m = jnp.concatenate([
                jnp.concatenate([iso_hi, pro_hi], axis=1), jnp.concatenate([iso_lo, pro_lo], axis=1)], axis=0)
            out = jnp.dot(jnp.concatenate([g, g], axis=1), m, preferred_element_type=f32)
            out = out[0:8] + out[8:16]
            from_iso, from_pro = out[:, 0:128], out[:, 128:256]
            acc_ref[tile(t), :] += pltpu.roll(from_iso, 4, 0) + near_ref[tile(t), :] * from_pro[3:4] + 0.5 * from_pro

    def many(i, carry):
        for u in range(unroll):
            distances(2 * i, both_a, g_a, [u])
            speeds(2 * i - 1, both_b, g_b, [u])
        for u in range(unroll):
            distances(2 * i + 1, both_b, g_b, [u])
            speeds(2 * i, both_a, g_a, [u])
        return carry

    blocks = (n + unroll - 1) // unroll
    lax.fori_loop(0, blocks // 2, many, 0)
    tail = lax.rem(blocks, 2) == 1

    @pl.when(tail)
    def _():
        distances(blocks - 1, both_a, g_a)
        speeds(blocks - 2, both_b, g_b)
        speeds(blocks - 1, both_a, g_a)

    @pl.when(jnp.logical_not(tail))
    def _():
        speeds(blocks - 1, both_b, g_b)

    for a in range(2):
        for c in range(ncol):
            for k in range(3):
                v_ref[a, c, k] = stokes_scale * acc_ref[pl.ds((a * ncol + c) * local * 8 + k, local, stride=8), :]


def home_kernel(
        nrow, ncol, cap, slot_ref, place_ref, cnt_ref, v_ref, out_ref, got, part, swap, outg, arr, vsend, vrecv, zsend, zrecv, asend, arecv):
    row, col = lax.axis_index("row"), lax.axis_index("col")
    local = out_ref.shape[1]
    devs = nrow * ncol
    me = row * ncol + col
    barrier = pltpu.get_barrier_semaphore()

    def peer(d):
        p = lax.rem(me + d, devs)
        return {"row": p // ncol, "col": lax.rem(p, ncol)}

    for d in range(1, devs):
        pl.semaphore_signal(barrier, inc=1, device_id=peer(d), device_id_type=MESH)
    half = ncol // 2
    core = lax.rem(col, 2)
    mine_x = col // 2

    def remote(src, dst, send, recv, where):
        return pltpu.make_async_remote_copy(
            src_ref=src, dst_ref=dst, send_sem=send, recv_sem=recv, device_id=where, device_id_type=MESH)

    keep_a = lax.rem(row, 2)
    order = (1 - keep_a, keep_a)

    def within(n, d, k):
        x = lax.rem(mine_x + d, half)
        return remote(
            v_ref.at[order[n], 2 * x + 1 - core, k], got.at[n, d, k], vsend.at[n, d, k], vrecv.at[n, d, k],
            {"col": col + 1 - 2 * core})

    def facing(d):
        return 2 * lax.rem(mine_x + d, half) + core

    def across(n, d, k):
        at = half + d - 1
        return remote(
            part.at[n, d - 1, k], got.at[n, at, k], vsend.at[n, at, k], vrecv.at[n, at, k], {"col": facing(d)})

    def exchange(k):
        return remote(swap.at[0, k], swap.at[1, k], zsend.at[k], zrecv.at[k], {"row": row + 1 - 2 * keep_a})

    def total(n, k):
        within(n, 0, k).wait_recv()
        mine = v_ref[order[n], col, k] + got[n, 0, k]
        for d in range(1, half):
            across(n, d, k).wait_recv()
            mine = mine + got[n, half + d - 1, k]
        return mine

    def deal(d, k):
        return remote(outg.at[k, lax.rem(me + d, devs)], arr.at[k, me], asend.at[d - 1, k], arecv.at[d - 1, k], peer(d))

    def move(pick, values):
        parts = jnp.concatenate(split3(values), axis=1).astype(bf16)
        moved = jnp.dot(pick, parts, preferred_element_type=f32)
        return moved[:, 0:128] + moved[:, 128:256] + moved[:, 256:384]

    pick = (lax.broadcasted_iota(ints, (devs * cap, local), 0) == slot_ref[...]).astype(f32).astype(bf16)
    pl.semaphore_wait(barrier, devs - 1)
    for k in range(3):
        for n in range(2):
            for d in [*range(1, half), 0]:
                within(n, d, k).start()

    def pass_on(n, k):
        for d in range(1, half):
            within(n, d, k).wait_recv()
            part[n, d - 1, k] = v_ref[order[n], facing(d), k] + got[n, d, k]
            across(n, d, k).start()

    def finish(k):
        mine = total(1, k)
        exchange(k).wait_recv()
        outg[k] = move(pick, mine + swap[1, k]).reshape(devs, cap, 128)
        for d in range(1, devs):
            deal(d, k).start()
        arr[k, me] = outg[k, me]

    for k in range(3):
        pass_on(0, k)
        pass_on(1, k)
    for k in range(3):
        swap[0, k] = total(0, k)
        exchange(k).start()
        if k > 0:
            finish(k - 1)
    finish(2)
    fetch = (lax.broadcasted_iota(ints, (local, devs * cap), 1) == place_ref[...]).astype(f32).astype(bf16)
    live = lax.broadcasted_iota(ints, (local, 128), 1) < cnt_ref[...]
    for k in range(3):
        for d in range(1, devs):
            deal(d, k).wait_recv()
        out_ref[k] = jnp.where(live, move(fetch, arr[k].reshape(devs * cap, 128)), 0.0)
    for k in range(3):
        exchange(k).wait_send()
        for n in range(2):
            for d in range(half):
                within(n, d, k).wait_send()
            for d in range(1, half):
                across(n, d, k).wait_send()
        for d in range(1, devs):
            deal(d, k).wait_send()


def per_device(positions, normals, curvature, pair_targets, pair_sources, pair_count, node_counts, drop_clusters, drop_owner):
    local, _, nodes = positions.shape
    nrow, ncol = lax.axis_size("row"), lax.axis_size("col")
    devs = nrow * ncol
    part, half = nrow // 2, ncol // 2
    cap = max(2, 2 * local // devs)
    slots = pair_targets.shape[1]
    dma = pltpu.SemaphoreType.DMA
    shape = jax.ShapeDtypeStruct
    near, far, tl, sl, lc, slot, place, owned_counts = pl.pallas_call(
        functools.partial(gather_kernel, nrow, ncol, cap),
        out_shape=(
            pltpu.VMEM((2 * ncol * local * 8, nodes), f32), pltpu.VMEM((2 * part * local * 8, nodes), f32),
            shape((4, slots), ints), shape((4, slots), ints), shape((4, 128), ints),
            pltpu.VMEM((1, local), ints), pltpu.VMEM((local, 1), ints), pltpu.VMEM((local, 1), ints)),
        in_specs=[HBM] * 8 + [SMEM], out_specs=(VMEM,) * 8,
        scratch_shapes=[
            pltpu.VMEM((3, local, nodes), f32), pltpu.VMEM((local, nodes), f32), *[pltpu.VMEM(drop_clusters.shape[::-1], ints)] * 2,
            pltpu.VMEM((1, drop_owner.shape[0]), ints), *[pltpu.VMEM((1, slots), ints)] * 2, dma((8,)),
            pltpu.VMEM((8, slots), ints), pltpu.VMEM((2, 2, 8, slots), ints),
            pltpu.VMEM((2, ncol, 3, local, nodes), f32), pltpu.VMEM((2, nrow, 6, local, nodes), f32),
            *[dma((2 * nrow - 2, 6))] * 4, *[dma((6,))] * 2, *[dma((2,))] * 2,
            *[dma((max(half - 1, 1), 2))] * 4, *[dma((2,))] * 4],
        compiler_params=pltpu.CompilerParams(collective_id=0, has_side_effects=True, vmem_limit_bytes=30 << 20),
        name="gather_blocks",
    )(*map(far_off, (jnp.transpose(positions, (1, 0, 2)), jnp.transpose(normals, (1, 0, 2)), curvature, node_counts.T,
                     drop_clusters.T, drop_owner[None, :], pair_targets, pair_sources)), pair_count)
    speeds = pl.pallas_call(
        pair_kernel,
        out_shape=pltpu.VMEM((2, ncol, 3, local, nodes), f32),
        in_specs=[SMEM] * 3 + [VMEM] * 2, out_specs=VMEM,
        scratch_shapes=[pltpu.VMEM((2 * ncol * local * 8, nodes), f32)]
        + [pltpu.VMEM((unroll, nodes, 2 * nodes), f32)] * 2 + [pltpu.VMEM((unroll, 16, nodes), bf16)] * 2,
        compiler_params=pltpu.CompilerParams(vmem_limit_bytes=30 << 20),
        name="pairs",
    )(tl, sl, lc, keep(near), keep(far))
    owned = pl.pallas_call(
        functools.partial(home_kernel, nrow, ncol, cap),
        out_shape=jax.ShapeDtypeStruct((3, local, nodes), f32),
        in_specs=[VMEM] * 4, out_specs=VMEM,
        scratch_shapes=[
            pltpu.VMEM((2, ncol - 1, 3, local, nodes), f32), pltpu.VMEM((2, max(half - 1, 1), 3, local, nodes), f32),
            pltpu.VMEM((2, 3, local, nodes), f32),
            pltpu.VMEM((3, devs, cap, nodes), f32), pltpu.VMEM((3, devs, cap, nodes), f32),
            dma((2, ncol - 1, 3)), dma((2, ncol - 1, 3)), dma((3,)), dma((3,)), dma((devs - 1, 3)), dma((devs - 1, 3)),
        ],
        compiler_params=pltpu.CompilerParams(collective_id=1, has_side_effects=True, vmem_limit_bytes=30 << 20),
        name="to_owners",
    )(keep(slot), keep(place), keep(owned_counts), keep(speeds))
    return jnp.transpose(owned, (1, 0, 2))


def solution(mesh):
    every = ("groups", "row", "col")
    in_specs = (
        P(every, None, None), P(every, None, None), P(every, None), P(every, None), P(every, None), P(every),
        P("groups", None), P("groups", None), P("groups"),
    )
    return jax.shard_map(per_device, mesh=mesh, in_specs=in_specs, out_specs=P(every, None, None), check_vma=False)
```

```python
import functools
import math

import jax
import jax.numpy as jnp
from jax import lax
from jax.experimental import pallas as pl
from jax.experimental.pallas import tpu as pltpu
from jax.sharding import PartitionSpec as P

regular_sq = 0.0025
inv_reg = 1.0 / math.sqrt(regular_sq)
stokes_scale = inv_reg / (8.0 * math.pi)
MESH = pl.DeviceIdType.MESH
VMEM = pl.BlockSpec(memory_space=pltpu.VMEM)
SMEM = pl.BlockSpec(memory_space=pltpu.SMEM)


HBM = pl.BlockSpec(memory_space=pltpu.HBM)
unroll = 24
f32, bf16, ints = jnp.float32, jnp.bfloat16, jnp.int32


def keep(x):
    return pltpu.with_memory_space_constraint(x, pltpu.VMEM)


def far_off(x):
    return pltpu.with_memory_space_constraint(x, pltpu.HBM)


def split3(x):
    high = x.astype(bf16).astype(f32)
    rest = x - high
    middle = rest.astype(bf16).astype(f32)
    return high, middle, rest - middle


def as_row(column):
    return jnp.transpose(jnp.broadcast_to(column, (column.shape[0], 128)))[0:1]


def gather_kernel(
        nrow, ncol, cap, pos_in, nrm_in, curv_in, nct_in, dct_in, own_in, tgt_in, src_in, count_ref,
        near_ref, far_ref, tl_ref, sl_ref, lc_ref, slot_ref, place_ref, cnt_ref,
        nrm_ref, curv_ref, nct_ref, dct_ref, own_ref, tgt_ref, src_ref, here_sem, mine_ref, lists_ref, t_ref, s_ref,
        zsend, zrecv, fsend, frecv, osend, orecv, bsend, brecv, xsend, xrecv, gsend, grecv, lsend, lrecv, hsend, hrecv):
    row, col = lax.axis_index("row"), lax.axis_index("col")
    core = lax.rem(col, 2)
    chip = col // 2
    half = ncol // 2
    part = nrow // 2
    i = lax.rem(row, 2)
    mate = row + 1 - 2 * i
    based = row // part == i
    me = row * ncol + col
    local = pos_in.shape[1]
    drops = own_ref.shape[1]
    per_drop = dct_ref.shape[0]
    slots = tgt_in.shape[1]
    pos_ref = s_ref.at[core, row, 0:3]
    loads = [pltpu.make_async_copy(src, dst, here_sem.at[n]) for n, (src, dst) in enumerate((
        (pos_in, pos_ref), (tgt_in, tgt_ref), (src_in, src_ref), (dct_in, dct_ref), (nct_in, nct_ref), (own_in, own_ref),
        (curv_in, curv_ref), (nrm_in, nrm_ref)))]
    for load in loads:
        load.start()
    barrier = pltpu.get_barrier_semaphore()
    for d in range(1, nrow):
        pl.semaphore_signal(barrier, inc=1, device_id={"row": lax.rem(row + d, nrow)}, device_id_type=MESH)
    for d in range(1, ncol):
        pl.semaphore_signal(barrier, inc=1, device_id={"col": lax.rem(col + d, ncol)}, device_id_type=MESH)

    def remote(src, dst, send, recv, where):
        return pltpu.make_async_remote_copy(
            src_ref=src, dst_ref=dst, send_sem=send, recv_sem=recv, device_id=where, device_id_type=MESH)

    sibling = {"col": col + 1 - 2 * core}

    def block_of(way, step):
        return jnp.clip(row - way * step, 0, nrow - 1)

    def relay(way, step, k):
        piece = s_ref.at[core, block_of(way, step), k]
        at = step if way > 0 else nrow - 1 + step
        return remote(piece, piece, zsend.at[at, k], zrecv.at[at, k], {"row": jnp.clip(row + way, 0, nrow - 1)})

    def reaches(way, block, place):
        inside = (block >= 0) & (block < nrow)
        half_of = jnp.clip(block, 0, nrow - 1) // part
        return inside & (place <= nrow - 2 + half_of if way > 0 else place >= half_of)

    def sends(way, step):
        return reaches(way, row - way * step, row + way)

    def receives(way, step):
        return reaches(way, row - way * (step + 1), row)

    def wanted(way, step):
        return receives(way, step) & (block_of(way, step + 1) // part == i)

    def onward(way, step, k):
        piece = s_ref.at[core, block_of(way, step + 1), k]
        at = step if way > 0 else nrow - 1 + step
        return remote(piece, piece, fsend.at[at, k], frecv.at[at, k], sibling)

    def start(way, step, k):
        @pl.when(sends(way, step))
        def _():
            relay(way, step, k).start()

    def own(k):
        piece = s_ref.at[core, row, k]
        return remote(piece, piece, osend.at[k], orecv.at[k], sibling)

    def beside(a):
        piece = t_ref.at[a, col]
        return remote(piece, piece, bsend.at[a], brecv.at[a], sibling)

    def facing(d):
        return 2 * lax.rem(chip + d, half) + core

    def opposite(a, d):
        piece = t_ref.at[a, col]
        return remote(piece, piece, xsend.at[d - 1, a], xrecv.at[d - 1, a], {"col": facing(d)})

    def behind(d):
        return 2 * lax.rem(chip + half - d, half) + core

    def passed(a, d):
        piece = t_ref.at[a, behind(d)]
        return remote(piece, piece, gsend.at[d - 1, a], grecv.at[d - 1, a], sibling)

    def share(a):
        beside(a).start()
        for d in range(1, half):
            opposite(a, d).start()

    def list_to(a):
        return remote(mine_ref, lists_ref.at[a, core], lsend.at[0], lrecv.at[0], {"row": mate})

    def list_on(a):
        piece = lists_ref.at[a, core]
        return remote(piece, piece, hsend.at[a], hrecv.at[a], sibling)

    loads[0].wait()
    pl.semaphore_wait(barrier, nrow + ncol - 2)
    for k in range(3):
        for way in (1, -1):
            start(way, 0, k)
        t_ref[i, col, k] = s_ref[core, row, k]
    share(i)
    for load in loads[1:]:
        load.wait()
    zero = jnp.zeros((1, slots), ints)
    mine_ref[...] = jnp.concatenate(
        [tgt_ref[...], src_ref[...], jnp.full((1, slots), count_ref[0], ints), zero, zero, zero, zero, zero], axis=0)
    list_to(i).start()
    lists_ref[i, core] = mine_ref[...]
    index = lax.broadcasted_iota(ints, (local, 1), 0)
    ids = me * local + index

    def match(chunk, carry):
        counts, owners = carry
        lanes = pl.ds(pl.multiple_of(chunk * 128, 128), 128)
        clusters, nodes_in, owner = dct_ref[:, lanes], nct_ref[:, lanes], own_ref[0:1, lanes]
        for k in range(per_drop):
            hit = ids == clusters[k:k + 1]
            counts = counts + jnp.where(hit, nodes_in[k:k + 1], 0)
            owners = owners + jnp.where(hit, owner, 0)
        return counts, owners

    none = jnp.zeros((local, 128), ints)
    counts, owners = lax.fori_loop(0, drops // 128, match, (none, none))
    home_counts = jnp.sum(counts, axis=1, keepdims=True, dtype=ints)
    home_owner = jnp.sum(owners, axis=1, keepdims=True, dtype=ints)
    scale = jnp.where(lax.broadcasted_iota(ints, (local, 128), 1) < home_counts, curv_ref[...], 0.0)
    for k in range(3):
        s_ref[core, row, 3 + k] = scale * nrm_ref[k]
        for way in (1, -1):
            start(way, 0, 3 + k)

    @pl.when(based)
    def _():
        for k in range(6):
            own(k).start()

    def spread(l, block, k):
        at = (l * part + lax.rem(block, part)) * local * 8 + (k if k < 3 else k + 1)
        far_ref[pl.ds(at, local, stride=8), :] = s_ref[l, block, k]

    def blank(l, r):
        for k in (3, 7):
            far_ref[pl.ds((l * part + r) * local * 8 + k, local, stride=8), :] = jnp.zeros((local, 128), f32)

    def arrive(step, k):
        for way in (1, -1):
            @pl.when(receives(way, step))
            def _():
                relay(way, step, k).wait_recv()
                if step < nrow - 2:
                    start(way, step + 1, k)

                @pl.when(wanted(way, step))
                def _():
                    onward(way, step, k).start()

    def collect(step, k):
        for way in (1, -1):
            @pl.when(wanted(way, step))
            def _():
                spread(core, block_of(way, step + 1), k)

    def received(step, k):
        for way in (1, -1):
            @pl.when(wanted(way, step))
            def _():
                onward(way, step, k).wait_recv()
                spread(1 - core, block_of(way, step + 1), k)

    def targets(a, c):
        square = jnp.ones((local, 128), f32)
        start = (a * ncol + c) * local * 8
        for k in range(3):
            coord = t_ref[a, c, k]
            centre = jnp.mean(coord, axis=1, keepdims=True)
            coord = (coord - centre) * inv_reg
            square = square + coord * coord
            near_ref[pl.ds(start + k, local, stride=8), :] = coord
            near_ref[pl.ds(start + 4 + k, local, stride=8), :] = jnp.broadcast_to(centre, coord.shape)
        near_ref[pl.ds(start + 3, local, stride=8), :] = square
        near_ref[pl.ds(start + 7, local, stride=8), :] = jnp.zeros((local, 128), f32)

    for k in range(3):
        arrive(0, k)
        t_ref[1 - i, col, k] = s_ref[core, mate, k]
    share(1 - i)
    list_to(1 - i).wait_recv()
    for a in range(2):
        list_on(a).start()

    owner_row = as_row(home_owner.astype(f32)).astype(ints)
    lane = lax.broadcasted_iota(ints, (local, local), 1)
    rank = jnp.sum(((owner_row == home_owner) & (lane < index)).astype(ints), axis=1, keepdims=True, dtype=ints)
    slot_ref[...] = as_row((home_owner * cap + rank).astype(f32)).astype(ints)
    drop_of = lax.div(index, per_drop)
    width = 256 if drops % 256 == 0 else 128
    before = (lax.broadcasted_iota(ints, (width, width), 0) < lax.broadcasted_iota(ints, (width, width), 1)).astype(bf16)

    def owned(chunk, carry):
        clusters, counted, base = carry
        lanes = pl.ds(pl.multiple_of(chunk * width, width), width)
        mine = own_ref[0:1, lanes] == me
        marks = jnp.broadcast_to(mine.astype(f32), (16, width)).astype(bf16)
        place = jnp.dot(marks, before, preferred_element_type=f32)[0:1].astype(ints) + base
        chosen = mine & (place == drop_of)
        clusters = clusters + jnp.where(chosen, jnp.concatenate([dct_ref[:, lanes]] * (local // per_drop), axis=0), 0)
        counted = counted + jnp.where(chosen, jnp.concatenate([nct_ref[:, lanes]] * (local // per_drop), axis=0), 0)
        return clusters, counted, base + jnp.sum(mine.astype(ints), axis=1, keepdims=True, dtype=ints)

    wide = jnp.zeros((local, width), ints)
    clusters, counted, _ = lax.fori_loop(0, drops // width, owned, (wide, wide, jnp.zeros((1, 1), ints)))
    clusters = jnp.sum(clusters, axis=1, keepdims=True, dtype=ints)
    cnt_ref[...] = jnp.sum(counted, axis=1, keepdims=True, dtype=ints)
    clusters_row = as_row(clusters.astype(f32)).astype(ints)
    anchor, anchor_row = lax.div(clusters, local), lax.div(clusters_row, local)
    same = (anchor == anchor_row) & (clusters_row < clusters)
    place_ref[...] = anchor * cap + jnp.sum(same.astype(ints), axis=1, keepdims=True, dtype=ints)

    for k in range(3, 6):
        arrive(0, k)
    for l in range(2):
        for r in range(part):
            blank(l, r)
    for a in range(2):
        targets(a, col)

    for a in range(2):
        list_on(a).wait_recv()
    lane_of = lax.broadcasted_iota(ints, (1, slots), 1)
    lowest = i * part * local
    square_rows = lax.broadcasted_iota(ints, (slots, slots), 0)
    earlier = (square_rows < lax.broadcasted_iota(ints, (slots, slots), 1)).astype(f32).astype(bf16)
    for a in range(2):
        for l in range(2):
            t, s, count = lists_ref[a, l, 0:1, :], lists_ref[a, l, 1:2, :], lists_ref[a, l, 2:3, :]
            taken = (lane_of < count) & (s >= lowest) & (s < lowest + part * local)
            marks = taken.astype(f32)
            ranks = jnp.dot(jnp.broadcast_to(marks, (16, slots)).astype(bf16), earlier, preferred_element_type=f32)[0:1]
            ranks = jnp.where(taken, ranks.astype(ints), -1)
            to = (square_rows == ranks).astype(f32).astype(bf16)
            digits = [lax.div(t, 256), lax.rem(t, 256), lax.div(s, 256), lax.rem(s, 256)]
            values = jnp.concatenate([v.astype(f32) for v in digits] + [jnp.zeros((12, slots), f32)], axis=0).astype(bf16)
            moved = lax.dot_general(values, to, (((1,), (1,)), ((), ())), preferred_element_type=f32).astype(ints)
            n = a * 2 + l
            tl_ref[n:n + 1, :] = moved[0:1] * 256 + moved[1:2] + a * ncol * local
            sl_ref[n:n + 1, :] = jnp.maximum(moved[2:3] * 256 + moved[3:4] - lowest, 0) + l * part * local
            lc_ref[n:n + 1, :] = jnp.broadcast_to(jnp.sum(marks, axis=1, keepdims=True).astype(ints), (1, 128))

    for a in range(2):
        for d in range(1, half):
            opposite(a, d).wait_recv()
            passed(a, d).start()
        beside(a).wait_recv()
        targets(a, col + 1 - 2 * core)
        for d in range(1, half):
            targets(a, behind(d))
    @pl.when(based)
    def _():
        for k in range(6):
            spread(core, row, k)
            own(k).wait_recv()
            spread(1 - core, row, k)

    for k in range(6):
        collect(0, k)
    for a in range(2):
        for d in range(1, half):
            passed(a, d).wait_recv()
            targets(a, behind(d) + 1 - 2 * core)
    for k in range(6):
        received(0, k)
    for step in range(1, nrow - 1):
        for k in range(6):
            arrive(step, k)
            collect(step, k)
    for step in range(1, nrow - 1):
        for k in range(6):
            received(step, k)
    for k in range(6):
        @pl.when(based)
        def _():
            own(k).wait_send()

        for step in range(nrow - 1):
            for way in (1, -1):
                @pl.when(sends(way, step))
                def _():
                    relay(way, step, k).wait_send()

                @pl.when(wanted(way, step))
                def _():
                    onward(way, step, k).wait_send()
    for a in range(2):
        beside(a).wait_send()
        list_on(a).wait_send()
        for d in range(1, half):
            opposite(a, d).wait_send()
            passed(a, d).wait_send()
    list_to(i).wait_send()


def pair_kernel(tl_ref, sl_ref, lc_ref, near_ref, far_ref, v_ref, acc_ref, both_a, both_b, g_a, g_b):
    _, ncol, _, local, _ = v_ref.shape
    core = lax.rem(lax.axis_index("col"), 2)
    sub = lax.broadcasted_iota(ints, (8, 128), 0)
    low = sub < 4
    last = (sub == 3) | (sub == 7)
    scale = jnp.where(low, -2.0, 1.0).astype(f32)
    fold = jnp.where(sub == 3, 1.0, jnp.where(sub == 7, -1.0, 0.0)).astype(f32)
    some = jnp.where(low, 1.0, 0.0).astype(f32)
    unit = jnp.where(low, inv_reg, 1.0).astype(f32)
    idle = jnp.where(low, inv_reg, 0.0).astype(f32)
    nothing = jnp.zeros((32, 128), bf16)
    acc_ref[...] = jnp.zeros_like(acc_ref)
    both_b[...] = jnp.ones_like(both_b)
    g_b[...] = jnp.zeros_like(g_b)
    ends = [lc_ref[0, 0]]
    for l in range(1, 4):
        ends.append(ends[-1] + lc_ref[l, 0])
    total = ends[3]
    half = (total + 1) // 2
    first = core * half
    n = jnp.where(core == 0, half, total - half)

    def entry(j):
        j = jnp.minimum(first + jnp.clip(j, 0, jnp.maximum(n - 1, 0)), jnp.maximum(total - 1, 0))
        past = [(j >= end).astype(ints) for end in ends[:3]]
        start = jnp.where(j >= ends[2], ends[2], jnp.where(j >= ends[1], ends[1], jnp.where(j >= ends[0], ends[0], 0)))
        return past[0] + past[1] + past[2], j - start

    def tile(i):
        return pl.ds(pl.multiple_of(i * 8, 8), 8)

    def distances(block, both_ref, g_ref, us=range(unroll)):
        for u in us:
            j = block * unroll + u
            l, e = entry(j)
            t, s = tl_ref[l, e], sl_ref[l, e]
            near = near_ref[tile(t), :]
            centre = jnp.where(low, pltpu.roll(near, 4, 0), 0.0)
            high, middle, rest = split3(near)
            sums = jnp.where(sub == 0, high[3:4], jnp.where(sub == 1, middle[3:4], jnp.where(sub == 2, rest[3:4], 0.0)))
            high = jnp.where(sub < 3, high, jnp.where(sub == 3, 1.0, 0.0))
            middle = jnp.where(sub < 3, middle, 0.0)
            rest = jnp.where(sub < 3, rest, 0.0)
            high_up = pltpu.roll(high, 4, 0)
            right = jnp.concatenate([
                high + pltpu.roll(middle, 4, 0), rest + high_up, middle + high_up, sums], axis=0).astype(bf16)
            shifted = (far_ref[tile(s), :] - centre) * jnp.where(j < n, unit, idle)
            prod = shifted * jnp.where(low, shifted, pltpu.roll(shifted, 4, 0))
            prod = prod + pltpu.roll(prod, 1, 0)
            prod = prod + pltpu.roll(prod, 2, 0)
            hi, mid, lo = split3(shifted * scale + prod * fold)
            hi_up, mid_up, lo_up = pltpu.roll(hi, 4, 0), pltpu.roll(mid, 4, 0), pltpu.roll(lo, 4, 0)
            left = jnp.concatenate([
                jnp.where(low, hi, hi_up), jnp.where(low, hi, mid_up), jnp.where(low, mid, lo_up), some,
                jnp.where(low, hi_up, hi), jnp.where(low, hi_up, mid), jnp.where(low, mid_up, lo),
                jnp.zeros((8, 128), f32)], axis=0).astype(bf16)
            weights = jnp.concatenate([
                jnp.concatenate([right, nothing], axis=1), jnp.concatenate([nothing, right], axis=1)], axis=0)
            both_ref[u] = lax.dot_general(left, weights, (((0,), (0,)), ((), ())), preferred_element_type=f32)
            g_ref[u] = jnp.concatenate([jnp.where(last, 1.0, hi), jnp.where(last, 0.0, mid)], axis=0).astype(bf16)

    def speeds(block, both_ref, g_ref, us=range(unroll)):
        for u in us:
            l, e = entry(block * unroll + u)
            t = tl_ref[l, e]
            both, g = both_ref[u], g_ref[u]
            inv = lax.rsqrt(both[:, 0:128])
            weight = inv * inv * inv
            iso = inv + weight
            pro = both[:, 128:256] * weight
            iso_hi, pro_hi = iso.astype(bf16), pro.astype(bf16)
            iso_lo = (iso - iso_hi.astype(f32)).astype(bf16)
            pro_lo = (pro - pro_hi.astype(f32)).astype(bf16)
            m = jnp.concatenate([
                jnp.concatenate([iso_hi, pro_hi], axis=1), jnp.concatenate([iso_lo, pro_lo], axis=1)], axis=0)
            out = jnp.dot(jnp.concatenate([g, g], axis=1), m, preferred_element_type=f32)
            out = out[0:8] + out[8:16]
            from_iso, from_pro = out[:, 0:128], out[:, 128:256]
            acc_ref[tile(t), :] += pltpu.roll(from_iso, 4, 0) + near_ref[tile(t), :] * from_pro[3:4] + 0.5 * from_pro

    def many(i, carry):
        for u in range(unroll):
            distances(2 * i, both_a, g_a, [u])
            speeds(2 * i - 1, both_b, g_b, [u])
        for u in range(unroll):
            distances(2 * i + 1, both_b, g_b, [u])
            speeds(2 * i, both_a, g_a, [u])
        return carry

    blocks = (n + unroll - 1) // unroll
    lax.fori_loop(0, blocks // 2, many, 0)
    tail = lax.rem(blocks, 2) == 1

    @pl.when(tail)
    def _():
        distances(blocks - 1, both_a, g_a)
        speeds(blocks - 2, both_b, g_b)
        speeds(blocks - 1, both_a, g_a)

    @pl.when(jnp.logical_not(tail))
    def _():
        speeds(blocks - 1, both_b, g_b)

    for a in range(2):
        for c in range(ncol):
            for k in range(3):
                v_ref[a, c, k] = stokes_scale * acc_ref[pl.ds((a * ncol + c) * local * 8 + k, local, stride=8), :]


def home_kernel(
        nrow, ncol, cap, slot_ref, place_ref, cnt_ref, v_ref, out_ref, got, part, swap, ahead, outg, arr, vsend, vrecv, zsend, zrecv, esend, erecv, asend, arecv):
    row, col = lax.axis_index("row"), lax.axis_index("col")
    local = out_ref.shape[1]
    devs = nrow * ncol
    me = row * ncol + col
    barrier = pltpu.get_barrier_semaphore()

    def peer(d):
        p = lax.rem(me + d, devs)
        return {"row": p // ncol, "col": lax.rem(p, ncol)}

    for d in range(1, devs):
        pl.semaphore_signal(barrier, inc=1, device_id=peer(d), device_id_type=MESH)
    half = ncol // 2
    core = lax.rem(col, 2)
    mine_x = col // 2

    def remote(src, dst, send, recv, where):
        return pltpu.make_async_remote_copy(
            src_ref=src, dst_ref=dst, send_sem=send, recv_sem=recv, device_id=where, device_id_type=MESH)

    keep_a = lax.rem(row, 2)
    order = (1 - keep_a, keep_a)

    def within(n, d, k):
        x = lax.rem(mine_x + d, half)
        return remote(
            v_ref.at[order[n], 2 * x + 1 - core, k], got.at[n, d, k], vsend.at[n, d, k], vrecv.at[n, d, k],
            {"col": col + 1 - 2 * core})

    def facing(d):
        return 2 * lax.rem(mine_x + d, half) + core

    def across(n, d, k):
        at = half + d - 1
        return remote(
            part.at[n, d - 1, k], got.at[n, at, k], vsend.at[n, at, k], vrecv.at[n, at, k], {"col": facing(d)})

    def exchange(k):
        return remote(swap.at[0, k], swap.at[1, k], zsend.at[k], zrecv.at[k], {"row": row + 1 - 2 * keep_a})

    def early(d, k):
        return remote(ahead.at[0, d], ahead.at[1, d], esend.at[d], erecv.at[d], {"row": row + 1 - 2 * keep_a})

    def block_at(d):
        return col if d == 0 else facing(d)

    def total(n, k):
        within(n, 0, k).wait_recv()
        mine = v_ref[order[n], col, k] + got[n, 0, k]
        for d in range(1, half):
            across(n, d, k).wait_recv()
            mine = mine + got[n, half + d - 1, k]
        return mine

    def deal(d, k):
        return remote(outg.at[k, lax.rem(me + d, devs)], arr.at[k, me], asend.at[d - 1, k], arecv.at[d - 1, k], peer(d))

    def move(pick, values):
        parts = jnp.concatenate(split3(values), axis=1).astype(bf16)
        moved = jnp.dot(pick, parts, preferred_element_type=f32)
        return moved[:, 0:128] + moved[:, 128:256] + moved[:, 256:384]

    pick = (lax.broadcasted_iota(ints, (devs * cap, local), 0) == slot_ref[...]).astype(f32).astype(bf16)
    pl.semaphore_wait(barrier, devs - 1)
    for n, k in [(0, 2), (0, 0), (1, 0), (0, 1), (1, 1), (1, 2)]:
        for d in [*range(1, half), 0]:
            within(n, d, k).start()

    def pass_on(n, k):
        for d in range(1, half):
            within(n, d, k).wait_recv()
            part[n, d - 1, k] = v_ref[order[n], facing(d), k] + got[n, d, k]
            across(n, d, k).start()

    def rows_first(k):
        for d in [*range(1, half), 0]:
            within(0, d, k).wait_recv()
            ahead[0, d] = v_ref[order[0], block_at(d), k] + got[0, d, k]
            early(d, k).start()

    def then_columns(k):
        for d in range(1, half):
            within(1, d, k).wait_recv()
            early(d, k).wait_recv()
            part[1, d - 1, k] = v_ref[order[1], facing(d), k] + got[1, d, k] + ahead[1, d]
            across(1, d, k).start()

    def spread_out(k, mine):
        outg[k] = move(pick, mine).reshape(devs, cap, 128)
        for d in range(1, devs):
            deal(d, k).start()
        arr[k, me] = outg[k, me]

    def columns_first(k):
        swap[0, k] = total(0, k)
        exchange(k).start()

    def finish(k):
        mine = total(1, k)
        exchange(k).wait_recv()
        spread_out(k, mine + swap[1, k])

    rows_first(2)
    pass_on(0, 0)
    pass_on(1, 0)
    pass_on(0, 1)
    pass_on(1, 1)
    columns_first(0)
    then_columns(2)
    finish(0)
    columns_first(1)
    finish(1)
    mine = total(1, 2)
    early(0, 2).wait_recv()
    spread_out(2, mine + ahead[1, 0])
    fetch = (lax.broadcasted_iota(ints, (local, devs * cap), 1) == place_ref[...]).astype(f32).astype(bf16)
    live = lax.broadcasted_iota(ints, (local, 128), 1) < cnt_ref[...]
    for k in range(3):
        for d in range(1, devs):
            deal(d, k).wait_recv()
        out_ref[k] = jnp.where(live, move(fetch, arr[k].reshape(devs * cap, 128)), 0.0)
    for d in range(half):
        early(d, 2).wait_send()
    for k in range(3):
        if k != 2:
            exchange(k).wait_send()
        for n in range(2):
            for d in range(half):
                within(n, d, k).wait_send()
            if k != 2 or n == 1:
                for d in range(1, half):
                    across(n, d, k).wait_send()
        for d in range(1, devs):
            deal(d, k).wait_send()


def per_device(positions, normals, curvature, pair_targets, pair_sources, pair_count, node_counts, drop_clusters, drop_owner):
    local, _, nodes = positions.shape
    nrow, ncol = lax.axis_size("row"), lax.axis_size("col")
    devs = nrow * ncol
    part, half = nrow // 2, ncol // 2
    cap = max(2, 2 * local // devs)
    slots = pair_targets.shape[1]
    dma = pltpu.SemaphoreType.DMA
    shape = jax.ShapeDtypeStruct
    near, far, tl, sl, lc, slot, place, owned_counts = pl.pallas_call(
        functools.partial(gather_kernel, nrow, ncol, cap),
        out_shape=(
            pltpu.VMEM((2 * ncol * local * 8, nodes), f32), pltpu.VMEM((2 * part * local * 8, nodes), f32),
            shape((4, slots), ints), shape((4, slots), ints), shape((4, 128), ints),
            pltpu.VMEM((1, local), ints), pltpu.VMEM((local, 1), ints), pltpu.VMEM((local, 1), ints)),
        in_specs=[HBM] * 8 + [SMEM], out_specs=(VMEM,) * 8,
        scratch_shapes=[
            pltpu.VMEM((3, local, nodes), f32), pltpu.VMEM((local, nodes), f32), *[pltpu.VMEM(drop_clusters.shape[::-1], ints)] * 2,
            pltpu.VMEM((1, drop_owner.shape[0]), ints), *[pltpu.VMEM((1, slots), ints)] * 2, dma((8,)),
            pltpu.VMEM((8, slots), ints), pltpu.VMEM((2, 2, 8, slots), ints),
            pltpu.VMEM((2, ncol, 3, local, nodes), f32), pltpu.VMEM((2, nrow, 6, local, nodes), f32),
            *[dma((2 * nrow - 2, 6))] * 4, *[dma((6,))] * 2, *[dma((2,))] * 2,
            *[dma((max(half - 1, 1), 2))] * 4, *[dma((2,))] * 4],
        compiler_params=pltpu.CompilerParams(collective_id=0, has_side_effects=True, vmem_limit_bytes=30 << 20),
        name="gather_blocks",
    )(*map(far_off, (jnp.transpose(positions, (1, 0, 2)), jnp.transpose(normals, (1, 0, 2)), curvature, node_counts.T,
                     drop_clusters.T, drop_owner[None, :], pair_targets, pair_sources)), pair_count)
    speeds = pl.pallas_call(
        pair_kernel,
        out_shape=pltpu.VMEM((2, ncol, 3, local, nodes), f32),
        in_specs=[SMEM] * 3 + [VMEM] * 2, out_specs=VMEM,
        scratch_shapes=[pltpu.VMEM((2 * ncol * local * 8, nodes), f32)]
        + [pltpu.VMEM((unroll, nodes, 2 * nodes), f32)] * 2 + [pltpu.VMEM((unroll, 16, nodes), bf16)] * 2,
        compiler_params=pltpu.CompilerParams(vmem_limit_bytes=30 << 20),
        name="pairs",
    )(tl, sl, lc, keep(near), keep(far))
    owned = pl.pallas_call(
        functools.partial(home_kernel, nrow, ncol, cap),
        out_shape=jax.ShapeDtypeStruct((3, local, nodes), f32),
        in_specs=[VMEM] * 4, out_specs=VMEM,
        scratch_shapes=[
            pltpu.VMEM((2, ncol - 1, 3, local, nodes), f32), pltpu.VMEM((2, max(half - 1, 1), 3, local, nodes), f32),
            pltpu.VMEM((2, 3, local, nodes), f32), pltpu.VMEM((2, half, local, nodes), f32),
            pltpu.VMEM((3, devs, cap, nodes), f32), pltpu.VMEM((3, devs, cap, nodes), f32),
            dma((2, ncol - 1, 3)), dma((2, ncol - 1, 3)), dma((3,)), dma((3,)), dma((half,)), dma((half,)), dma((devs - 1, 3)), dma((devs - 1, 3)),
        ],
        compiler_params=pltpu.CompilerParams(collective_id=1, has_side_effects=True, vmem_limit_bytes=30 << 20),
        name="to_owners",
    )(keep(slot), keep(place), keep(owned_counts), keep(speeds))
    return jnp.transpose(owned, (1, 0, 2))


def solution(mesh):
    every = ("groups", "row", "col")
    in_specs = (
        P(every, None, None), P(every, None, None), P(every, None), P(every, None), P(every, None), P(every),
        P("groups", None), P("groups", None), P("groups"),
    )
    return jax.shard_map(per_device, mesh=mesh, in_specs=in_specs, out_specs=P(every, None, None), check_vma=False)
```

```python
import functools
import math

import jax
import jax.numpy as jnp
from jax import lax
from jax.experimental import pallas as pl
from jax.experimental.pallas import tpu as pltpu
from jax.sharding import PartitionSpec as P

regular_sq = 0.0025
inv_reg = 1.0 / math.sqrt(regular_sq)
stokes_scale = inv_reg / (8.0 * math.pi)
MESH = pl.DeviceIdType.MESH
VMEM = pl.BlockSpec(memory_space=pltpu.VMEM)
SMEM = pl.BlockSpec(memory_space=pltpu.SMEM)


HBM = pl.BlockSpec(memory_space=pltpu.HBM)
unroll = 16
f32, bf16, ints = jnp.float32, jnp.bfloat16, jnp.int32


def keep(x):
    return pltpu.with_memory_space_constraint(x, pltpu.VMEM)


def far_off(x):
    return pltpu.with_memory_space_constraint(x, pltpu.HBM)


def split3(x):
    high = x.astype(bf16).astype(f32)
    rest = x - high
    middle = rest.astype(bf16).astype(f32)
    return high, middle, rest - middle


def as_row(column):
    return jnp.transpose(jnp.broadcast_to(column, (column.shape[0], 128)))[0:1]


def gather_kernel(
        nrow, ncol, cap, pos_in, nrm_in, curv_in, nct_in, dct_in, own_in, tgt_in, src_in, count_ref,
        near_ref, far_ref, tl_ref, sl_ref, lc_ref, slot_ref, place_ref, cnt_ref,
        nrm_ref, curv_ref, nct_ref, dct_ref, own_ref, tgt_ref, src_ref, here_sem, mine_ref, lists_ref, t_ref, s_ref,
        zsend, zrecv, fsend, frecv, osend, orecv, bsend, brecv, xsend, xrecv, gsend, grecv, lsend, lrecv, hsend, hrecv):
    row, col = lax.axis_index("row"), lax.axis_index("col")
    core = lax.rem(col, 2)
    chip = col // 2
    half = ncol // 2
    part = nrow // 2
    i = lax.rem(row, 2)
    mate = row + 1 - 2 * i
    based = row // part == i
    me = row * ncol + col
    local = pos_in.shape[1]
    drops = own_ref.shape[1]
    per_drop = dct_ref.shape[0]
    slots = tgt_in.shape[1]
    pos_ref = s_ref.at[core, row, 0:3]
    loads = [pltpu.make_async_copy(src, dst, here_sem.at[n]) for n, (src, dst) in enumerate((
        (pos_in, pos_ref), (tgt_in, tgt_ref), (src_in, src_ref), (dct_in, dct_ref), (nct_in, nct_ref), (own_in, own_ref),
        (curv_in, curv_ref), (nrm_in, nrm_ref)))]
    barrier = pltpu.get_barrier_semaphore()
    for d in range(1, nrow):
        pl.semaphore_signal(barrier, inc=1, device_id={"row": lax.rem(row + d, nrow)}, device_id_type=MESH)
    for d in range(1, ncol):
        pl.semaphore_signal(barrier, inc=1, device_id={"col": lax.rem(col + d, ncol)}, device_id_type=MESH)
    for load in loads:
        load.start()

    def remote(src, dst, send, recv, where):
        return pltpu.make_async_remote_copy(
            src_ref=src, dst_ref=dst, send_sem=send, recv_sem=recv, device_id=where, device_id_type=MESH)

    sibling = {"col": col + 1 - 2 * core}

    def block_of(way, step):
        return jnp.clip(row - way * step, 0, nrow - 1)

    def relay(way, step, k):
        piece = s_ref.at[core, block_of(way, step), k]
        at = step if way > 0 else nrow - 1 + step
        return remote(piece, piece, zsend.at[at, k], zrecv.at[at, k], {"row": jnp.clip(row + way, 0, nrow - 1)})

    def reaches(way, block, place):
        inside = (block >= 0) & (block < nrow)
        half_of = jnp.clip(block, 0, nrow - 1) // part
        return inside & (place <= nrow - 2 + half_of if way > 0 else place >= half_of)

    def sends(way, step):
        return reaches(way, row - way * step, row + way)

    def receives(way, step):
        return reaches(way, row - way * (step + 1), row)

    def wanted(way, step):
        return receives(way, step) & (block_of(way, step + 1) // part == i)

    def onward(way, step, k):
        piece = s_ref.at[core, block_of(way, step + 1), k]
        at = step if way > 0 else nrow - 1 + step
        return remote(piece, piece, fsend.at[at, k], frecv.at[at, k], sibling)

    def start(way, step, k):
        @pl.when(sends(way, step))
        def _():
            relay(way, step, k).start()

    def own(k):
        piece = s_ref.at[core, row, k]
        return remote(piece, piece, osend.at[k], orecv.at[k], sibling)

    def beside(a):
        piece = t_ref.at[a, col]
        return remote(piece, piece, bsend.at[a], brecv.at[a], sibling)

    def facing(d):
        return 2 * lax.rem(chip + d, half) + core

    def opposite(a, d):
        piece = t_ref.at[a, col]
        return remote(piece, piece, xsend.at[d - 1, a], xrecv.at[d - 1, a], {"col": facing(d)})

    def behind(d):
        return 2 * lax.rem(chip + half - d, half) + core

    def passed(a, d):
        piece = t_ref.at[a, behind(d)]
        return remote(piece, piece, gsend.at[d - 1, a], grecv.at[d - 1, a], sibling)

    def share(a):
        beside(a).start()
        for d in range(1, half):
            opposite(a, d).start()

    def list_to(a):
        return remote(mine_ref, lists_ref.at[a, core], lsend.at[0], lrecv.at[0], {"row": mate})

    def list_on(a):
        piece = lists_ref.at[a, core]
        return remote(piece, piece, hsend.at[a], hrecv.at[a], sibling)

    loads[0].wait()
    pl.semaphore_wait(barrier, nrow + ncol - 2)
    for k in range(3):
        for way in (1, -1):
            start(way, 0, k)
        t_ref[i, col, k] = s_ref[core, row, k]
    share(i)
    for load in loads[1:]:
        load.wait()
    zero = jnp.zeros((1, slots), ints)
    mine_ref[...] = jnp.concatenate(
        [tgt_ref[...], src_ref[...], jnp.full((1, slots), count_ref[0], ints), zero, zero, zero, zero, zero], axis=0)
    list_to(i).start()
    lists_ref[i, core] = mine_ref[...]
    index = lax.broadcasted_iota(ints, (local, 1), 0)
    ids = me * local + index

    def match(chunk, carry):
        counts, owners = carry
        lanes = pl.ds(pl.multiple_of(chunk * 128, 128), 128)
        clusters, nodes_in, owner = dct_ref[:, lanes], nct_ref[:, lanes], own_ref[0:1, lanes]
        for k in range(per_drop):
            hit = ids == clusters[k:k + 1]
            counts = counts + jnp.where(hit, nodes_in[k:k + 1], 0)
            owners = owners + jnp.where(hit, owner, 0)
        return counts, owners

    none = jnp.zeros((local, 128), ints)
    counts, owners = lax.fori_loop(0, drops // 128, match, (none, none))
    home_counts = jnp.sum(counts, axis=1, keepdims=True, dtype=ints)
    home_owner = jnp.sum(owners, axis=1, keepdims=True, dtype=ints)
    scale = jnp.where(lax.broadcasted_iota(ints, (local, 128), 1) < home_counts, curv_ref[...], 0.0)
    for k in range(3):
        s_ref[core, row, 3 + k] = scale * nrm_ref[k]
        for way in (1, -1):
            start(way, 0, 3 + k)

    @pl.when(based)
    def _():
        for k in range(6):
            own(k).start()

    def spread(l, block, k):
        at = (l * part + lax.rem(block, part)) * local * 8 + (k if k < 3 else k + 1)
        far_ref[pl.ds(at, local, stride=8), :] = s_ref[l, block, k]

    def blank(l, r):
        for k in (3, 7):
            far_ref[pl.ds((l * part + r) * local * 8 + k, local, stride=8), :] = jnp.zeros((local, 128), f32)

    def arrive(step, k):
        for way in (1, -1):
            @pl.when(receives(way, step))
            def _():
                relay(way, step, k).wait_recv()
                if step < nrow - 2:
                    start(way, step + 1, k)

                @pl.when(wanted(way, step))
                def _():
                    onward(way, step, k).start()

    def collect(step, k):
        for way in (1, -1):
            @pl.when(wanted(way, step))
            def _():
                spread(core, block_of(way, step + 1), k)

    def received(step, k):
        for way in (1, -1):
            @pl.when(wanted(way, step))
            def _():
                onward(way, step, k).wait_recv()
                spread(1 - core, block_of(way, step + 1), k)

    def targets(a, c):
        square = jnp.ones((local, 128), f32)
        start = (a * ncol + c) * local * 8
        for k in range(3):
            coord = t_ref[a, c, k]
            centre = jnp.mean(coord, axis=1, keepdims=True)
            coord = (coord - centre) * inv_reg
            square = square + coord * coord
            near_ref[pl.ds(start + k, local, stride=8), :] = coord
            near_ref[pl.ds(start + 4 + k, local, stride=8), :] = jnp.broadcast_to(centre, coord.shape)
        near_ref[pl.ds(start + 3, local, stride=8), :] = square
        near_ref[pl.ds(start + 7, local, stride=8), :] = jnp.zeros((local, 128), f32)

    for k in range(3):
        arrive(0, k)
        t_ref[1 - i, col, k] = s_ref[core, mate, k]
    share(1 - i)
    list_to(1 - i).wait_recv()
    for a in range(2):
        list_on(a).start()

    owner_row = as_row(home_owner.astype(f32)).astype(ints)
    lane = lax.broadcasted_iota(ints, (local, local), 1)
    rank = jnp.sum(((owner_row == home_owner) & (lane < index)).astype(ints), axis=1, keepdims=True, dtype=ints)
    slot_ref[...] = as_row((home_owner * cap + rank).astype(f32)).astype(ints)
    drop_of = lax.div(index, per_drop)
    width = 256 if drops % 256 == 0 else 128
    before = (lax.broadcasted_iota(ints, (width, width), 0) < lax.broadcasted_iota(ints, (width, width), 1)).astype(bf16)

    def owned(chunk, carry):
        clusters, counted, base = carry
        lanes = pl.ds(pl.multiple_of(chunk * width, width), width)
        mine = own_ref[0:1, lanes] == me
        marks = jnp.broadcast_to(mine.astype(f32), (16, width)).astype(bf16)
        place = jnp.dot(marks, before, preferred_element_type=f32)[0:1].astype(ints) + base
        chosen = mine & (place == drop_of)
        clusters = clusters + jnp.where(chosen, jnp.concatenate([dct_ref[:, lanes]] * (local // per_drop), axis=0), 0)
        counted = counted + jnp.where(chosen, jnp.concatenate([nct_ref[:, lanes]] * (local // per_drop), axis=0), 0)
        return clusters, counted, base + jnp.sum(mine.astype(ints), axis=1, keepdims=True, dtype=ints)

    wide = jnp.zeros((local, width), ints)
    clusters, counted, _ = lax.fori_loop(0, drops // width, owned, (wide, wide, jnp.zeros((1, 1), ints)))
    clusters = jnp.sum(clusters, axis=1, keepdims=True, dtype=ints)
    cnt_ref[...] = jnp.sum(counted, axis=1, keepdims=True, dtype=ints)
    clusters_row = as_row(clusters.astype(f32)).astype(ints)
    anchor, anchor_row = lax.div(clusters, local), lax.div(clusters_row, local)
    same = (anchor == anchor_row) & (clusters_row < clusters)
    place_ref[...] = anchor * cap + jnp.sum(same.astype(ints), axis=1, keepdims=True, dtype=ints)

    for k in range(3, 6):
        arrive(0, k)
    for l in range(2):
        for r in range(part):
            blank(l, r)
    for a in range(2):
        targets(a, col)

    for a in range(2):
        list_on(a).wait_recv()
    lane_of = lax.broadcasted_iota(ints, (1, slots), 1)
    lowest = i * part * local
    square_rows = lax.broadcasted_iota(ints, (slots, slots), 0)
    earlier = (square_rows < lax.broadcasted_iota(ints, (slots, slots), 1)).astype(f32).astype(bf16)
    for a in range(2):
        for l in range(2):
            t, s, count = lists_ref[a, l, 0:1, :], lists_ref[a, l, 1:2, :], lists_ref[a, l, 2:3, :]
            taken = (lane_of < count) & (s >= lowest) & (s < lowest + part * local)
            marks = taken.astype(f32)
            ranks = jnp.dot(jnp.broadcast_to(marks, (16, slots)).astype(bf16), earlier, preferred_element_type=f32)[0:1]
            ranks = jnp.where(taken, ranks.astype(ints), -1)
            to = (square_rows == ranks).astype(f32).astype(bf16)
            digits = [lax.div(t, 256), lax.rem(t, 256), lax.div(s, 256), lax.rem(s, 256)]
            values = jnp.concatenate([v.astype(f32) for v in digits] + [jnp.zeros((12, slots), f32)], axis=0).astype(bf16)
            moved = lax.dot_general(values, to, (((1,), (1,)), ((), ())), preferred_element_type=f32).astype(ints)
            n = a * 2 + l
            tl_ref[n:n + 1, :] = moved[0:1] * 256 + moved[1:2] + a * ncol * local
            sl_ref[n:n + 1, :] = jnp.maximum(moved[2:3] * 256 + moved[3:4] - lowest, 0) + l * part * local
            lc_ref[n:n + 1, :] = jnp.broadcast_to(jnp.sum(marks, axis=1, keepdims=True).astype(ints), (1, 128))

    for a in range(2):
        for d in range(1, half):
            opposite(a, d).wait_recv()
            passed(a, d).start()
        beside(a).wait_recv()
        targets(a, col + 1 - 2 * core)
        for d in range(1, half):
            targets(a, behind(d))
    @pl.when(based)
    def _():
        for k in range(6):
            spread(core, row, k)
            own(k).wait_recv()
            spread(1 - core, row, k)

    for k in range(6):
        collect(0, k)
    for a in range(2):
        for d in range(1, half):
            passed(a, d).wait_recv()
            targets(a, behind(d) + 1 - 2 * core)
    for k in range(6):
        received(0, k)
    for step in range(1, nrow - 1):
        for k in range(6):
            arrive(step, k)
            collect(step, k)
    for step in range(1, nrow - 1):
        for k in range(6):
            received(step, k)
    for k in range(6):
        @pl.when(based)
        def _():
            own(k).wait_send()

        for step in range(nrow - 1):
            for way in (1, -1):
                @pl.when(sends(way, step))
                def _():
                    relay(way, step, k).wait_send()

                @pl.when(wanted(way, step))
                def _():
                    onward(way, step, k).wait_send()
    for a in range(2):
        beside(a).wait_send()
        list_on(a).wait_send()
        for d in range(1, half):
            opposite(a, d).wait_send()
            passed(a, d).wait_send()
    list_to(i).wait_send()


def pair_kernel(tl_ref, sl_ref, lc_ref, near_ref, far_ref, v_ref, acc_ref, both_a, both_b, g_a, g_b):
    _, ncol, _, local, _ = v_ref.shape
    core = lax.rem(lax.axis_index("col"), 2)
    sub = lax.broadcasted_iota(ints, (8, 128), 0)
    low = sub < 4
    last = (sub == 3) | (sub == 7)
    scale = jnp.where(low, -2.0, 1.0).astype(f32)
    fold = jnp.where(sub == 3, 1.0, jnp.where(sub == 7, -1.0, 0.0)).astype(f32)
    some = jnp.where(low, 1.0, 0.0).astype(f32)
    unit = jnp.where(low, inv_reg, 1.0).astype(f32)
    idle = jnp.where(low, inv_reg, 0.0).astype(f32)
    nothing = jnp.zeros((32, 128), bf16)
    acc_ref[...] = jnp.zeros_like(acc_ref)
    both_b[...] = jnp.ones_like(both_b)
    g_b[...] = jnp.zeros_like(g_b)
    ends = [lc_ref[0, 0]]
    for l in range(1, 4):
        ends.append(ends[-1] + lc_ref[l, 0])
    total = ends[3]
    half = (total + 1) // 2
    first = core * half
    n = jnp.where(core == 0, half, total - half)

    def entry(j):
        j = jnp.minimum(first + jnp.clip(j, 0, jnp.maximum(n - 1, 0)), jnp.maximum(total - 1, 0))
        past = [(j >= end).astype(ints) for end in ends[:3]]
        start = jnp.where(j >= ends[2], ends[2], jnp.where(j >= ends[1], ends[1], jnp.where(j >= ends[0], ends[0], 0)))
        return past[0] + past[1] + past[2], j - start

    def tile(i):
        return pl.ds(pl.multiple_of(i * 8, 8), 8)

    def distances(block, both_ref, g_ref, us=range(unroll)):
        for u in us:
            j = block * unroll + u
            l, e = entry(j)
            t, s = tl_ref[l, e], sl_ref[l, e]
            near = near_ref[tile(t), :]
            centre = jnp.where(low, pltpu.roll(near, 4, 0), 0.0)
            high, middle, rest = split3(near)
            sums = jnp.where(sub == 0, high[3:4], jnp.where(sub == 1, middle[3:4], jnp.where(sub == 2, rest[3:4], 0.0)))
            high = jnp.where(sub < 3, high, jnp.where(sub == 3, 1.0, 0.0))
            middle = jnp.where(sub < 3, middle, 0.0)
            rest = jnp.where(sub < 3, rest, 0.0)
            high_up = pltpu.roll(high, 4, 0)
            right = jnp.concatenate([
                high + pltpu.roll(middle, 4, 0), rest + high_up, middle + high_up, sums], axis=0).astype(bf16)
            shifted = (far_ref[tile(s), :] - centre) * jnp.where(j < n, unit, idle)
            prod = shifted * jnp.where(low, shifted, pltpu.roll(shifted, 4, 0))
            prod = prod + pltpu.roll(prod, 1, 0)
            prod = prod + pltpu.roll(prod, 2, 0)
            hi, mid, lo = split3(shifted * scale + prod * fold)
            hi_up, mid_up, lo_up = pltpu.roll(hi, 4, 0), pltpu.roll(mid, 4, 0), pltpu.roll(lo, 4, 0)
            left = jnp.concatenate([
                jnp.where(low, hi, hi_up), jnp.where(low, hi, mid_up), jnp.where(low, mid, lo_up), some,
                jnp.where(low, hi_up, hi), jnp.where(low, hi_up, mid), jnp.where(low, mid_up, lo),
                jnp.zeros((8, 128), f32)], axis=0).astype(bf16)
            weights = jnp.concatenate([
                jnp.concatenate([right, nothing], axis=1), jnp.concatenate([nothing, right], axis=1)], axis=0)
            both_ref[u] = lax.dot_general(left, weights, (((0,), (0,)), ((), ())), preferred_element_type=f32)
            g_ref[u] = jnp.concatenate([jnp.where(last, 1.0, hi), jnp.where(last, 0.0, mid)], axis=0).astype(bf16)

    def speeds(block, both_ref, g_ref, us=range(unroll)):
        for u in us:
            l, e = entry(block * unroll + u)
            t = tl_ref[l, e]
            both, g = both_ref[u], g_ref[u]
            inv = lax.rsqrt(both[:, 0:128])
            weight = inv * inv * inv
            iso = inv + weight
            pro = both[:, 128:256] * weight
            iso_hi, pro_hi = iso.astype(bf16), pro.astype(bf16)
            iso_lo = (iso - iso_hi.astype(f32)).astype(bf16)
            pro_lo = (pro - pro_hi.astype(f32)).astype(bf16)
            m = jnp.concatenate([
                jnp.concatenate([iso_hi, pro_hi], axis=1), jnp.concatenate([iso_lo, pro_lo], axis=1)], axis=0)
            out = jnp.dot(jnp.concatenate([g, g], axis=1), m, preferred_element_type=f32)
            out = out[0:8] + out[8:16]
            from_iso, from_pro = out[:, 0:128], out[:, 128:256]
            acc_ref[tile(t), :] += pltpu.roll(from_iso, 4, 0) + near_ref[tile(t), :] * from_pro[3:4] + 0.5 * from_pro

    def many(i, carry):
        for u in range(unroll):
            distances(2 * i, both_a, g_a, [u])
            speeds(2 * i - 1, both_b, g_b, [u])
        for u in range(unroll):
            distances(2 * i + 1, both_b, g_b, [u])
            speeds(2 * i, both_a, g_a, [u])
        return carry

    blocks = (n + unroll - 1) // unroll
    lax.fori_loop(0, blocks // 2, many, 0)
    tail = lax.rem(blocks, 2) == 1

    @pl.when(tail)
    def _():
        distances(blocks - 1, both_a, g_a)
        speeds(blocks - 2, both_b, g_b)
        speeds(blocks - 1, both_a, g_a)

    @pl.when(jnp.logical_not(tail))
    def _():
        speeds(blocks - 1, both_b, g_b)

    for a in range(2):
        for c in range(ncol):
            for k in range(3):
                v_ref[a, c, k] = stokes_scale * acc_ref[pl.ds((a * ncol + c) * local * 8 + k, local, stride=8), :]


def home_kernel(
        nrow, ncol, cap, slot_ref, place_ref, cnt_ref, v_ref, out_ref, got, part, swap, ahead, outg, arr, vsend, vrecv, zsend, zrecv, esend, erecv, asend, arecv):
    row, col = lax.axis_index("row"), lax.axis_index("col")
    local = out_ref.shape[1]
    devs = nrow * ncol
    me = row * ncol + col
    barrier = pltpu.get_barrier_semaphore()

    def peer(d):
        p = lax.rem(me + d, devs)
        return {"row": p // ncol, "col": lax.rem(p, ncol)}

    for d in range(1, devs):
        pl.semaphore_signal(barrier, inc=1, device_id=peer(d), device_id_type=MESH)
    half = ncol // 2
    core = lax.rem(col, 2)
    mine_x = col // 2

    def remote(src, dst, send, recv, where):
        return pltpu.make_async_remote_copy(
            src_ref=src, dst_ref=dst, send_sem=send, recv_sem=recv, device_id=where, device_id_type=MESH)

    keep_a = lax.rem(row, 2)
    order = (1 - keep_a, keep_a)

    def within(n, d, k):
        x = lax.rem(mine_x + d, half)
        return remote(
            v_ref.at[order[n], 2 * x + 1 - core, k], got.at[n, d, k], vsend.at[n, d, k], vrecv.at[n, d, k],
            {"col": col + 1 - 2 * core})

    def facing(d):
        return 2 * lax.rem(mine_x + d, half) + core

    def across(n, d, k):
        at = half + d - 1
        return remote(
            part.at[n, d - 1, k], got.at[n, at, k], vsend.at[n, at, k], vrecv.at[n, at, k], {"col": facing(d)})

    def exchange(k):
        return remote(swap.at[0, k], swap.at[1, k], zsend.at[k], zrecv.at[k], {"row": row + 1 - 2 * keep_a})

    def early(d, k):
        return remote(ahead.at[0, d], ahead.at[1, d], esend.at[d], erecv.at[d], {"row": row + 1 - 2 * keep_a})

    def block_at(d):
        return col if d == 0 else facing(d)

    def total(n, k):
        within(n, 0, k).wait_recv()
        mine = v_ref[order[n], col, k] + got[n, 0, k]
        for d in range(1, half):
            across(n, d, k).wait_recv()
            mine = mine + got[n, half + d - 1, k]
        return mine

    def deal(d, k):
        return remote(outg.at[k, lax.rem(me + d, devs)], arr.at[k, me], asend.at[d - 1, k], arecv.at[d - 1, k], peer(d))

    def move(pick, values):
        parts = jnp.concatenate(split3(values), axis=1).astype(bf16)
        moved = jnp.dot(pick, parts, preferred_element_type=f32)
        return moved[:, 0:128] + moved[:, 128:256] + moved[:, 256:384]

    pick = (lax.broadcasted_iota(ints, (devs * cap, local), 0) == slot_ref[...]).astype(f32).astype(bf16)
    pl.semaphore_wait(barrier, devs - 1)
    for n, k in [(0, 2), (0, 0), (1, 0), (0, 1), (1, 1), (1, 2)]:
        for d in [*range(1, half), 0]:
            within(n, d, k).start()

    def pass_on(n, k):
        for d in range(1, half):
            within(n, d, k).wait_recv()
            part[n, d - 1, k] = v_ref[order[n], facing(d), k] + got[n, d, k]
            across(n, d, k).start()

    def rows_first(k):
        for d in [*range(1, half), 0]:
            within(0, d, k).wait_recv()
            ahead[0, d] = v_ref[order[0], block_at(d), k] + got[0, d, k]
            early(d, k).start()

    def then_columns(k):
        for d in range(1, half):
            within(1, d, k).wait_recv()
            early(d, k).wait_recv()
            part[1, d - 1, k] = v_ref[order[1], facing(d), k] + got[1, d, k] + ahead[1, d]
            across(1, d, k).start()

    def spread_out(k, mine):
        outg[k] = move(pick, mine).reshape(devs, cap, 128)
        for d in range(1, devs):
            deal(d, k).start()
        arr[k, me] = outg[k, me]

    def columns_first(k):
        swap[0, k] = total(0, k)
        exchange(k).start()

    def finish(k):
        mine = total(1, k)
        exchange(k).wait_recv()
        spread_out(k, mine + swap[1, k])

    rows_first(2)
    pass_on(0, 0)
    pass_on(1, 0)
    pass_on(0, 1)
    pass_on(1, 1)
    columns_first(0)
    then_columns(2)
    finish(0)
    columns_first(1)
    finish(1)
    mine = total(1, 2)
    early(0, 2).wait_recv()
    spread_out(2, mine + ahead[1, 0])
    fetch = (lax.broadcasted_iota(ints, (local, devs * cap), 1) == place_ref[...]).astype(f32).astype(bf16)
    live = lax.broadcasted_iota(ints, (local, 128), 1) < cnt_ref[...]
    for k in range(3):
        for d in range(1, devs):
            deal(d, k).wait_recv()
        out_ref[k] = jnp.where(live, move(fetch, arr[k].reshape(devs * cap, 128)), 0.0)
    for d in range(half):
        early(d, 2).wait_send()
    for k in range(3):
        if k != 2:
            exchange(k).wait_send()
        for n in range(2):
            for d in range(half):
                within(n, d, k).wait_send()
            if k != 2 or n == 1:
                for d in range(1, half):
                    across(n, d, k).wait_send()
        for d in range(1, devs):
            deal(d, k).wait_send()


def per_device(positions, normals, curvature, pair_targets, pair_sources, pair_count, node_counts, drop_clusters, drop_owner):
    local, _, nodes = positions.shape
    nrow, ncol = lax.axis_size("row"), lax.axis_size("col")
    devs = nrow * ncol
    part, half = nrow // 2, ncol // 2
    cap = max(2, 2 * local // devs)
    slots = pair_targets.shape[1]
    dma = pltpu.SemaphoreType.DMA
    shape = jax.ShapeDtypeStruct
    near, far, tl, sl, lc, slot, place, owned_counts = pl.pallas_call(
        functools.partial(gather_kernel, nrow, ncol, cap),
        out_shape=(
            pltpu.VMEM((2 * ncol * local * 8, nodes), f32), pltpu.VMEM((2 * part * local * 8, nodes), f32),
            shape((4, slots), ints), shape((4, slots), ints), shape((4, 128), ints),
            pltpu.VMEM((1, local), ints), pltpu.VMEM((local, 1), ints), pltpu.VMEM((local, 1), ints)),
        in_specs=[HBM] * 8 + [SMEM], out_specs=(VMEM,) * 8,
        scratch_shapes=[
            pltpu.VMEM((3, local, nodes), f32), pltpu.VMEM((local, nodes), f32), *[pltpu.VMEM(drop_clusters.shape[::-1], ints)] * 2,
            pltpu.VMEM((1, drop_owner.shape[0]), ints), *[pltpu.VMEM((1, slots), ints)] * 2, dma((8,)),
            pltpu.VMEM((8, slots), ints), pltpu.VMEM((2, 2, 8, slots), ints),
            pltpu.VMEM((2, ncol, 3, local, nodes), f32), pltpu.VMEM((2, nrow, 6, local, nodes), f32),
            *[dma((2 * nrow - 2, 6))] * 4, *[dma((6,))] * 2, *[dma((2,))] * 2,
            *[dma((max(half - 1, 1), 2))] * 4, *[dma((2,))] * 4],
        compiler_params=pltpu.CompilerParams(collective_id=0, has_side_effects=True, vmem_limit_bytes=30 << 20),
        name="gather_blocks",
    )(*map(far_off, (jnp.transpose(positions, (1, 0, 2)), jnp.transpose(normals, (1, 0, 2)), curvature, node_counts.T,
                     drop_clusters.T, drop_owner[None, :], pair_targets, pair_sources)), pair_count)
    speeds = pl.pallas_call(
        pair_kernel,
        out_shape=pltpu.VMEM((2, ncol, 3, local, nodes), f32),
        in_specs=[SMEM] * 3 + [VMEM] * 2, out_specs=VMEM,
        scratch_shapes=[pltpu.VMEM((2 * ncol * local * 8, nodes), f32)]
        + [pltpu.VMEM((unroll, nodes, 2 * nodes), f32)] * 2 + [pltpu.VMEM((unroll, 16, nodes), bf16)] * 2,
        compiler_params=pltpu.CompilerParams(vmem_limit_bytes=30 << 20),
        name="pairs",
    )(tl, sl, lc, keep(near), keep(far))
    owned = pl.pallas_call(
        functools.partial(home_kernel, nrow, ncol, cap),
        out_shape=jax.ShapeDtypeStruct((3, local, nodes), f32),
        in_specs=[VMEM] * 4, out_specs=VMEM,
        scratch_shapes=[
            pltpu.VMEM((2, ncol - 1, 3, local, nodes), f32), pltpu.VMEM((2, max(half - 1, 1), 3, local, nodes), f32),
            pltpu.VMEM((2, 3, local, nodes), f32), pltpu.VMEM((2, half, local, nodes), f32),
            pltpu.VMEM((3, devs, cap, nodes), f32), pltpu.VMEM((3, devs, cap, nodes), f32),
            dma((2, ncol - 1, 3)), dma((2, ncol - 1, 3)), dma((3,)), dma((3,)), dma((half,)), dma((half,)), dma((devs - 1, 3)), dma((devs - 1, 3)),
        ],
        compiler_params=pltpu.CompilerParams(collective_id=1, has_side_effects=True, vmem_limit_bytes=30 << 20),
        name="to_owners",
    )(keep(slot), keep(place), keep(owned_counts), keep(speeds))
    return jnp.transpose(owned, (1, 0, 2))


def solution(mesh):
    every = ("groups", "row", "col")
    in_specs = (
        P(every, None, None), P(every, None, None), P(every, None), P(every, None), P(every, None), P(every),
        P("groups", None), P("groups", None), P("groups"),
    )
    return jax.shard_map(per_device, mesh=mesh, in_specs=in_specs, out_specs=P(every, None, None), check_vma=False)
```

```python
import functools
import math

import jax
import jax.numpy as jnp
from jax import lax
from jax.experimental import pallas as pl
from jax.experimental.pallas import tpu as pltpu
from jax.sharding import PartitionSpec as P

regular_sq = 0.0025
inv_reg = 1.0 / math.sqrt(regular_sq)
stokes_scale = inv_reg / (8.0 * math.pi)
MESH = pl.DeviceIdType.MESH
VMEM = pl.BlockSpec(memory_space=pltpu.VMEM)
SMEM = pl.BlockSpec(memory_space=pltpu.SMEM)


HBM = pl.BlockSpec(memory_space=pltpu.HBM)
unroll = 24
f32, bf16, ints = jnp.float32, jnp.bfloat16, jnp.int32


def keep(x):
    return pltpu.with_memory_space_constraint(x, pltpu.VMEM)


def far_off(x):
    return pltpu.with_memory_space_constraint(x, pltpu.HBM)


def split3(x):
    high = x.astype(bf16).astype(f32)
    rest = x - high
    middle = rest.astype(bf16).astype(f32)
    return high, middle, rest - middle


def as_row(column):
    return jnp.transpose(jnp.broadcast_to(column, (column.shape[0], 128)))[0:1]


def gather_kernel(
        nrow, ncol, cap, pos_in, nrm_in, curv_in, nct_in, dct_in, own_in, tgt_in, src_in, count_ref,
        near_ref, far_ref, tl_ref, sl_ref, lc_ref, slot_ref, place_ref, cnt_ref,
        nrm_ref, curv_ref, nct_ref, dct_ref, own_ref, tgt_ref, src_ref, here_sem, mine_ref, lists_ref, t_ref, s_ref,
        zsend, zrecv, fsend, frecv, osend, orecv, bsend, brecv, xsend, xrecv, gsend, grecv, lsend, lrecv, hsend, hrecv):
    row, col = lax.axis_index("row"), lax.axis_index("col")
    core = lax.rem(col, 2)
    chip = col // 2
    half = ncol // 2
    part = nrow // 2
    i = lax.rem(row, 2)
    mate = row + 1 - 2 * i
    based = row // part == i
    me = row * ncol + col
    local = pos_in.shape[1]
    drops = own_ref.shape[1]
    per_drop = dct_ref.shape[0]
    slots = tgt_in.shape[1]
    pos_ref = s_ref.at[core, row, 0:3]
    loads = [pltpu.make_async_copy(src, dst, here_sem.at[n]) for n, (src, dst) in enumerate((
        (pos_in, pos_ref), (tgt_in, tgt_ref), (src_in, src_ref), (dct_in, dct_ref), (nct_in, nct_ref), (own_in, own_ref),
        (curv_in, curv_ref), (nrm_in, nrm_ref)))]
    barrier = pltpu.get_barrier_semaphore()
    for d in range(1, nrow):
        pl.semaphore_signal(barrier, inc=1, device_id={"row": lax.rem(row + d, nrow)}, device_id_type=MESH)
    for d in range(1, ncol):
        pl.semaphore_signal(barrier, inc=1, device_id={"col": lax.rem(col + d, ncol)}, device_id_type=MESH)
    for load in loads:
        load.start()

    def remote(src, dst, send, recv, where):
        return pltpu.make_async_remote_copy(
            src_ref=src, dst_ref=dst, send_sem=send, recv_sem=recv, device_id=where, device_id_type=MESH)

    sibling = {"col": col + 1 - 2 * core}

    def block_of(way, step):
        return jnp.clip(row - way * step, 0, nrow - 1)

    def relay(way, step, k):
        piece = s_ref.at[core, block_of(way, step), k]
        at = step if way > 0 else nrow - 1 + step
        return remote(piece, piece, zsend.at[at, k], zrecv.at[at, k], {"row": jnp.clip(row + way, 0, nrow - 1)})

    def reaches(way, block, place):
        inside = (block >= 0) & (block < nrow)
        half_of = jnp.clip(block, 0, nrow - 1) // part
        return inside & (place <= nrow - 2 + half_of if way > 0 else place >= half_of)

    def sends(way, step):
        return reaches(way, row - way * step, row + way)

    def receives(way, step):
        return reaches(way, row - way * (step + 1), row)

    def wanted(way, step):
        return receives(way, step) & (block_of(way, step + 1) // part == i)

    def onward(way, step, k):
        piece = s_ref.at[core, block_of(way, step + 1), k]
        at = step if way > 0 else nrow - 1 + step
        return remote(piece, piece, fsend.at[at, k], frecv.at[at, k], sibling)

    def start(way, step, k):
        @pl.when(sends(way, step))
        def _():
            relay(way, step, k).start()

    def own(k):
        piece = s_ref.at[core, row, k]
        return remote(piece, piece, osend.at[k], orecv.at[k], sibling)

    def beside(a):
        piece = t_ref.at[a, col]
        return remote(piece, piece, bsend.at[a], brecv.at[a], sibling)

    def facing(d):
        return 2 * lax.rem(chip + d, half) + core

    def opposite(a, d):
        piece = t_ref.at[a, col]
        return remote(piece, piece, xsend.at[d - 1, a], xrecv.at[d - 1, a], {"col": facing(d)})

    def behind(d):
        return 2 * lax.rem(chip + half - d, half) + core

    def passed(a, d):
        piece = t_ref.at[a, behind(d)]
        return remote(piece, piece, gsend.at[d - 1, a], grecv.at[d - 1, a], sibling)

    def share(a):
        beside(a).start()
        for d in range(1, half):
            opposite(a, d).start()

    def list_to(a):
        return remote(mine_ref, lists_ref.at[a, core], lsend.at[0], lrecv.at[0], {"row": mate})

    def list_on(a):
        piece = lists_ref.at[a, core]
        return remote(piece, piece, hsend.at[a], hrecv.at[a], sibling)

    loads[0].wait()
    pl.semaphore_wait(barrier, nrow + ncol - 2)
    for k in range(3):
        for way in (1, -1):
            start(way, 0, k)
        t_ref[i, col, k] = s_ref[core, row, k]
    share(i)
    for load in loads[1:]:
        load.wait()
    zero = jnp.zeros((1, slots), ints)
    mine_ref[...] = jnp.concatenate(
        [tgt_ref[...], src_ref[...], jnp.full((1, slots), count_ref[0], ints), zero, zero, zero, zero, zero], axis=0)
    list_to(i).start()
    lists_ref[i, core] = mine_ref[...]
    index = lax.broadcasted_iota(ints, (local, 1), 0)
    ids = me * local + index

    def match(chunk, carry):
        counts, owners = carry
        lanes = pl.ds(pl.multiple_of(chunk * 128, 128), 128)
        clusters, nodes_in, owner = dct_ref[:, lanes], nct_ref[:, lanes], own_ref[0:1, lanes]
        for k in range(per_drop):
            hit = ids == clusters[k:k + 1]
            counts = counts + jnp.where(hit, nodes_in[k:k + 1], 0)
            owners = owners + jnp.where(hit, owner, 0)
        return counts, owners

    none = jnp.zeros((local, 128), ints)
    counts, owners = lax.fori_loop(0, drops // 128, match, (none, none))
    home_counts = jnp.sum(counts, axis=1, keepdims=True, dtype=ints)
    home_owner = jnp.sum(owners, axis=1, keepdims=True, dtype=ints)
    scale = jnp.where(lax.broadcasted_iota(ints, (local, 128), 1) < home_counts, curv_ref[...], 0.0)
    for k in range(3):
        s_ref[core, row, 3 + k] = scale * nrm_ref[k]
        for way in (1, -1):
            start(way, 0, 3 + k)

    @pl.when(based)
    def _():
        for k in range(6):
            own(k).start()

    def spread(l, block, k):
        at = (l * part + lax.rem(block, part)) * local * 8 + (k if k < 3 else k + 1)
        far_ref[pl.ds(at, local, stride=8), :] = s_ref[l, block, k]

    def blank(l, r):
        for k in (3, 7):
            far_ref[pl.ds((l * part + r) * local * 8 + k, local, stride=8), :] = jnp.zeros((local, 128), f32)

    def arrive(step, k):
        for way in (1, -1):
            @pl.when(receives(way, step))
            def _():
                relay(way, step, k).wait_recv()
                if step < nrow - 2:
                    start(way, step + 1, k)

                @pl.when(wanted(way, step))
                def _():
                    onward(way, step, k).start()

    def collect(step, k):
        for way in (1, -1):
            @pl.when(wanted(way, step))
            def _():
                spread(core, block_of(way, step + 1), k)

    def received(step, k):
        for way in (1, -1):
            @pl.when(wanted(way, step))
            def _():
                onward(way, step, k).wait_recv()
                spread(1 - core, block_of(way, step + 1), k)

    def targets(a, c):
        square = jnp.ones((local, 128), f32)
        start = (a * ncol + c) * local * 8
        for k in range(3):
            coord = t_ref[a, c, k]
            centre = jnp.mean(coord, axis=1, keepdims=True)
            coord = (coord - centre) * inv_reg
            square = square + coord * coord
            near_ref[pl.ds(start + k, local, stride=8), :] = coord
            near_ref[pl.ds(start + 4 + k, local, stride=8), :] = jnp.broadcast_to(centre, coord.shape)
        near_ref[pl.ds(start + 3, local, stride=8), :] = square
        near_ref[pl.ds(start + 7, local, stride=8), :] = jnp.zeros((local, 128), f32)

    for k in range(3):
        arrive(0, k)
        t_ref[1 - i, col, k] = s_ref[core, mate, k]
    share(1 - i)
    list_to(1 - i).wait_recv()
    for a in range(2):
        list_on(a).start()

    owner_row = as_row(home_owner.astype(f32)).astype(ints)
    lane = lax.broadcasted_iota(ints, (local, local), 1)
    rank = jnp.sum(((owner_row == home_owner) & (lane < index)).astype(ints), axis=1, keepdims=True, dtype=ints)
    slot_ref[...] = as_row((home_owner * cap + rank).astype(f32)).astype(ints)
    drop_of = lax.div(index, per_drop)
    width = 256 if drops % 256 == 0 else 128
    before = (lax.broadcasted_iota(ints, (width, width), 0) < lax.broadcasted_iota(ints, (width, width), 1)).astype(bf16)

    def owned(chunk, carry):
        clusters, counted, base = carry
        lanes = pl.ds(pl.multiple_of(chunk * width, width), width)
        mine = own_ref[0:1, lanes] == me
        marks = jnp.broadcast_to(mine.astype(f32), (16, width)).astype(bf16)
        place = jnp.dot(marks, before, preferred_element_type=f32)[0:1].astype(ints) + base
        chosen = mine & (place == drop_of)
        clusters = clusters + jnp.where(chosen, jnp.concatenate([dct_ref[:, lanes]] * (local // per_drop), axis=0), 0)
        counted = counted + jnp.where(chosen, jnp.concatenate([nct_ref[:, lanes]] * (local // per_drop), axis=0), 0)
        return clusters, counted, base + jnp.sum(mine.astype(ints), axis=1, keepdims=True, dtype=ints)

    wide = jnp.zeros((local, width), ints)
    clusters, counted, _ = lax.fori_loop(0, drops // width, owned, (wide, wide, jnp.zeros((1, 1), ints)))
    clusters = jnp.sum(clusters, axis=1, keepdims=True, dtype=ints)
    cnt_ref[...] = jnp.sum(counted, axis=1, keepdims=True, dtype=ints)
    clusters_row = as_row(clusters.astype(f32)).astype(ints)
    anchor, anchor_row = lax.div(clusters, local), lax.div(clusters_row, local)
    same = (anchor == anchor_row) & (clusters_row < clusters)
    place_ref[...] = anchor * cap + jnp.sum(same.astype(ints), axis=1, keepdims=True, dtype=ints)

    for k in range(3, 6):
        arrive(0, k)
    for l in range(2):
        for r in range(part):
            blank(l, r)
    for a in range(2):
        targets(a, col)

    for a in range(2):
        list_on(a).wait_recv()
    lane_of = lax.broadcasted_iota(ints, (1, slots), 1)
    lowest = i * part * local
    square_rows = lax.broadcasted_iota(ints, (slots, slots), 0)
    earlier = (square_rows < lax.broadcasted_iota(ints, (slots, slots), 1)).astype(f32).astype(bf16)
    for a in range(2):
        for l in range(2):
            t, s, count = lists_ref[a, l, 0:1, :], lists_ref[a, l, 1:2, :], lists_ref[a, l, 2:3, :]
            taken = (lane_of < count) & (s >= lowest) & (s < lowest + part * local)
            marks = taken.astype(f32)
            ranks = jnp.dot(jnp.broadcast_to(marks, (16, slots)).astype(bf16), earlier, preferred_element_type=f32)[0:1]
            ranks = jnp.where(taken, ranks.astype(ints), -1)
            to = (square_rows == ranks).astype(f32).astype(bf16)
            digits = [lax.div(t, 256), lax.rem(t, 256), lax.div(s, 256), lax.rem(s, 256)]
            values = jnp.concatenate([v.astype(f32) for v in digits] + [jnp.zeros((12, slots), f32)], axis=0).astype(bf16)
            moved = lax.dot_general(values, to, (((1,), (1,)), ((), ())), preferred_element_type=f32).astype(ints)
            n = a * 2 + l
            tl_ref[n:n + 1, :] = moved[0:1] * 256 + moved[1:2] + a * ncol * local
            sl_ref[n:n + 1, :] = jnp.maximum(moved[2:3] * 256 + moved[3:4] - lowest, 0) + l * part * local
            lc_ref[n:n + 1, :] = jnp.broadcast_to(jnp.sum(marks, axis=1, keepdims=True).astype(ints), (1, 128))

    for a in range(2):
        for d in range(1, half):
            opposite(a, d).wait_recv()
            passed(a, d).start()
        beside(a).wait_recv()
        targets(a, col + 1 - 2 * core)
        for d in range(1, half):
            targets(a, behind(d))
    @pl.when(based)
    def _():
        for k in range(6):
            spread(core, row, k)
            own(k).wait_recv()
            spread(1 - core, row, k)

    for k in range(6):
        collect(0, k)
    for a in range(2):
        for d in range(1, half):
            passed(a, d).wait_recv()
            targets(a, behind(d) + 1 - 2 * core)
    for k in range(6):
        received(0, k)
    for step in range(1, nrow - 1):
        for k in range(6):
            arrive(step, k)
            collect(step, k)
    for step in range(1, nrow - 1):
        for k in range(6):
            received(step, k)
    for k in range(6):
        @pl.when(based)
        def _():
            own(k).wait_send()

        for step in range(nrow - 1):
            for way in (1, -1):
                @pl.when(sends(way, step))
                def _():
                    relay(way, step, k).wait_send()

                @pl.when(wanted(way, step))
                def _():
                    onward(way, step, k).wait_send()
    for a in range(2):
        beside(a).wait_send()
        list_on(a).wait_send()
        for d in range(1, half):
            opposite(a, d).wait_send()
            passed(a, d).wait_send()
    list_to(i).wait_send()


def pair_kernel(tl_ref, sl_ref, lc_ref, near_ref, far_ref, v_ref, acc_ref, both_a, both_b, g_a, g_b):
    _, ncol, _, local, _ = v_ref.shape
    core = lax.rem(lax.axis_index("col"), 2)
    sub = lax.broadcasted_iota(ints, (8, 128), 0)
    low = sub < 4
    last = (sub == 3) | (sub == 7)
    scale = jnp.where(low, -2.0, 1.0).astype(f32)
    fold = jnp.where(sub == 3, 1.0, jnp.where(sub == 7, -1.0, 0.0)).astype(f32)
    some = jnp.where(low, 1.0, 0.0).astype(f32)
    unit = jnp.where(low, inv_reg, 1.0).astype(f32)
    idle = jnp.where(low, inv_reg, 0.0).astype(f32)
    nothing = jnp.zeros((32, 128), bf16)
    acc_ref[...] = jnp.zeros_like(acc_ref)
    both_b[...] = jnp.ones_like(both_b)
    g_b[...] = jnp.zeros_like(g_b)
    ends = [lc_ref[0, 0]]
    for l in range(1, 4):
        ends.append(ends[-1] + lc_ref[l, 0])
    total = ends[3]
    half = (total + 1) // 2
    first = core * half
    n = jnp.where(core == 0, half, total - half)

    def entry(j):
        j = jnp.minimum(first + jnp.clip(j, 0, jnp.maximum(n - 1, 0)), jnp.maximum(total - 1, 0))
        past = [(j >= end).astype(ints) for end in ends[:3]]
        start = jnp.where(j >= ends[2], ends[2], jnp.where(j >= ends[1], ends[1], jnp.where(j >= ends[0], ends[0], 0)))
        return past[0] + past[1] + past[2], j - start

    def tile(i):
        return pl.ds(pl.multiple_of(i * 8, 8), 8)

    def distances(block, both_ref, g_ref, us=range(unroll)):
        for u in us:
            j = block * unroll + u
            l, e = entry(j)
            t, s = tl_ref[l, e], sl_ref[l, e]
            near = near_ref[tile(t), :]
            centre = jnp.where(low, pltpu.roll(near, 4, 0), 0.0)
            high, middle, rest = split3(near)
            sums = jnp.where(sub == 0, high[3:4], jnp.where(sub == 1, middle[3:4], jnp.where(sub == 2, rest[3:4], 0.0)))
            high = jnp.where(sub < 3, high, jnp.where(sub == 3, 1.0, 0.0))
            middle = jnp.where(sub < 3, middle, 0.0)
            rest = jnp.where(sub < 3, rest, 0.0)
            high_up = pltpu.roll(high, 4, 0)
            right = jnp.concatenate([
                high + pltpu.roll(middle, 4, 0), rest + high_up, middle + high_up, sums], axis=0).astype(bf16)
            shifted = (far_ref[tile(s), :] - centre) * jnp.where(j < n, unit, idle)
            prod = shifted * jnp.where(low, shifted, pltpu.roll(shifted, 4, 0))
            prod = prod + pltpu.roll(prod, 1, 0)
            prod = prod + pltpu.roll(prod, 2, 0)
            hi, mid, lo = split3(shifted * scale + prod * fold)
            hi_up, mid_up, lo_up = pltpu.roll(hi, 4, 0), pltpu.roll(mid, 4, 0), pltpu.roll(lo, 4, 0)
            left = jnp.concatenate([
                jnp.where(low, hi, hi_up), jnp.where(low, hi, mid_up), jnp.where(low, mid, lo_up), some,
                jnp.where(low, hi_up, hi), jnp.where(low, hi_up, mid), jnp.where(low, mid_up, lo),
                jnp.zeros((8, 128), f32)], axis=0).astype(bf16)
            weights = jnp.concatenate([
                jnp.concatenate([right, nothing], axis=1), jnp.concatenate([nothing, right], axis=1)], axis=0)
            both_ref[u] = lax.dot_general(left, weights, (((0,), (0,)), ((), ())), preferred_element_type=f32)
            g_ref[u] = jnp.concatenate([jnp.where(last, 1.0, hi), jnp.where(last, 0.0, mid)], axis=0).astype(bf16)

    def speeds(block, both_ref, g_ref, us=range(unroll)):
        for u in us:
            l, e = entry(block * unroll + u)
            t = tl_ref[l, e]
            both, g = both_ref[u], g_ref[u]
            inv = lax.rsqrt(both[:, 0:128])
            weight = inv * inv * inv
            iso = inv + weight
            pro = both[:, 128:256] * weight
            iso_hi, pro_hi = iso.astype(bf16), pro.astype(bf16)
            iso_lo = (iso - iso_hi.astype(f32)).astype(bf16)
            pro_lo = (pro - pro_hi.astype(f32)).astype(bf16)
            m = jnp.concatenate([
                jnp.concatenate([iso_hi, pro_hi], axis=1), jnp.concatenate([iso_lo, pro_lo], axis=1)], axis=0)
            out = jnp.dot(jnp.concatenate([g, g], axis=1), m, preferred_element_type=f32)
            out = out[0:8] + out[8:16]
            from_iso, from_pro = out[:, 0:128], out[:, 128:256]
            acc_ref[tile(t), :] += pltpu.roll(from_iso, 4, 0) + near_ref[tile(t), :] * from_pro[3:4] + 0.5 * from_pro

    def many(i, carry):
        for u in range(unroll):
            distances(2 * i, both_a, g_a, [u])
            speeds(2 * i - 1, both_b, g_b, [u])
        for u in range(unroll):
            distances(2 * i + 1, both_b, g_b, [u])
            speeds(2 * i, both_a, g_a, [u])
        return carry

    blocks = (n + unroll - 1) // unroll
    lax.fori_loop(0, blocks // 2, many, 0)
    tail = lax.rem(blocks, 2) == 1

    @pl.when(tail)
    def _():
        distances(blocks - 1, both_a, g_a)
        speeds(blocks - 2, both_b, g_b)
        speeds(blocks - 1, both_a, g_a)

    @pl.when(jnp.logical_not(tail))
    def _():
        speeds(blocks - 1, both_b, g_b)

    for a in range(2):
        for c in range(ncol):
            for k in range(3):
                v_ref[a, c, k] = stokes_scale * acc_ref[pl.ds((a * ncol + c) * local * 8 + k, local, stride=8), :]


def home_kernel(
        nrow, ncol, cap, slot_ref, place_ref, cnt_ref, v_ref, out_ref, got, part, swap, ahead, outg, arr, vsend, vrecv, zsend, zrecv, esend, erecv, asend, arecv):
    row, col = lax.axis_index("row"), lax.axis_index("col")
    local = out_ref.shape[1]
    devs = nrow * ncol
    me = row * ncol + col
    barrier = pltpu.get_barrier_semaphore()

    def peer(d):
        p = lax.rem(me + d, devs)
        return {"row": p // ncol, "col": lax.rem(p, ncol)}

    for d in range(1, devs):
        pl.semaphore_signal(barrier, inc=1, device_id=peer(d), device_id_type=MESH)
    half = ncol // 2
    core = lax.rem(col, 2)
    mine_x = col // 2

    def remote(src, dst, send, recv, where):
        return pltpu.make_async_remote_copy(
            src_ref=src, dst_ref=dst, send_sem=send, recv_sem=recv, device_id=where, device_id_type=MESH)

    keep_a = lax.rem(row, 2)
    order = (1 - keep_a, keep_a)

    def within(n, d, k):
        x = lax.rem(mine_x + d, half)
        return remote(
            v_ref.at[order[n], 2 * x + 1 - core, k], got.at[n, d, k], vsend.at[n, d, k], vrecv.at[n, d, k],
            {"col": col + 1 - 2 * core})

    def facing(d):
        return 2 * lax.rem(mine_x + d, half) + core

    def across(n, d, k):
        at = half + d - 1
        return remote(
            part.at[n, d - 1, k], got.at[n, at, k], vsend.at[n, at, k], vrecv.at[n, at, k], {"col": facing(d)})

    def exchange(k):
        return remote(swap.at[0, k], swap.at[1, k], zsend.at[k], zrecv.at[k], {"row": row + 1 - 2 * keep_a})

    def early(d, k):
        return remote(ahead.at[0, d], ahead.at[1, d], esend.at[d], erecv.at[d], {"row": row + 1 - 2 * keep_a})

    def block_at(d):
        return col if d == 0 else facing(d)

    def total(n, k):
        within(n, 0, k).wait_recv()
        mine = v_ref[order[n], col, k] + got[n, 0, k]
        for d in range(1, half):
            across(n, d, k).wait_recv()
            mine = mine + got[n, half + d - 1, k]
        return mine

    def deal(d, k):
        return remote(outg.at[k, lax.rem(me + d, devs)], arr.at[k, me], asend.at[d - 1, k], arecv.at[d - 1, k], peer(d))

    def move(pick, values):
        parts = jnp.concatenate(split3(values), axis=1).astype(bf16)
        moved = jnp.dot(pick, parts, preferred_element_type=f32)
        return moved[:, 0:128] + moved[:, 128:256] + moved[:, 256:384]

    pick = (lax.broadcasted_iota(ints, (devs * cap, local), 0) == slot_ref[...]).astype(f32).astype(bf16)
    pl.semaphore_wait(barrier, devs - 1)
    for n, k in [(0, 2), (0, 0), (1, 0), (0, 1), (1, 1), (1, 2)]:
        for d in [*range(1, half), 0]:
            within(n, d, k).start()

    def pass_on(n, k):
        for d in range(1, half):
            within(n, d, k).wait_recv()
            part[n, d - 1, k] = v_ref[order[n], facing(d), k] + got[n, d, k]
            across(n, d, k).start()

    def rows_first(k):
        for d in [*range(1, half), 0]:
            within(0, d, k).wait_recv()
            ahead[0, d] = v_ref[order[0], block_at(d), k] + got[0, d, k]
            early(d, k).start()

    def then_columns(k):
        for d in range(1, half):
            within(1, d, k).wait_recv()
            early(d, k).wait_recv()
            part[1, d - 1, k] = v_ref[order[1], facing(d), k] + got[1, d, k] + ahead[1, d]
            across(1, d, k).start()

    def spread_out(k, mine):
        outg[k] = move(pick, mine).reshape(devs, cap, 128)
        for d in range(1, devs):
            deal(d, k).start()
        arr[k, me] = outg[k, me]

    def columns_first(k):
        swap[0, k] = total(0, k)
        exchange(k).start()

    def finish(k):
        mine = total(1, k)
        exchange(k).wait_recv()
        spread_out(k, mine + swap[1, k])

    rows_first(2)
    pass_on(0, 0)
    pass_on(1, 0)
    pass_on(0, 1)
    pass_on(1, 1)
    columns_first(0)
    then_columns(2)
    finish(0)
    columns_first(1)
    finish(1)
    mine = total(1, 2)
    early(0, 2).wait_recv()
    spread_out(2, mine + ahead[1, 0])
    fetch = (lax.broadcasted_iota(ints, (local, devs * cap), 1) == place_ref[...]).astype(f32).astype(bf16)
    live = lax.broadcasted_iota(ints, (local, 128), 1) < cnt_ref[...]
    for k in range(3):
        for d in range(1, devs):
            deal(d, k).wait_recv()
        out_ref[k] = jnp.where(live, move(fetch, arr[k].reshape(devs * cap, 128)), 0.0)
    for d in range(half):
        early(d, 2).wait_send()
    for k in range(3):
        if k != 2:
            exchange(k).wait_send()
        for n in range(2):
            for d in range(half):
                within(n, d, k).wait_send()
            if k != 2 or n == 1:
                for d in range(1, half):
                    across(n, d, k).wait_send()
        for d in range(1, devs):
            deal(d, k).wait_send()


def per_device(positions, normals, curvature, pair_targets, pair_sources, pair_count, node_counts, drop_clusters, drop_owner):
    local, _, nodes = positions.shape
    nrow, ncol = lax.axis_size("row"), lax.axis_size("col")
    devs = nrow * ncol
    part, half = nrow // 2, ncol // 2
    cap = max(2, 2 * local // devs)
    slots = pair_targets.shape[1]
    dma = pltpu.SemaphoreType.DMA
    shape = jax.ShapeDtypeStruct
    near, far, tl, sl, lc, slot, place, owned_counts = pl.pallas_call(
        functools.partial(gather_kernel, nrow, ncol, cap),
        out_shape=(
            pltpu.VMEM((2 * ncol * local * 8, nodes), f32), pltpu.VMEM((2 * part * local * 8, nodes), f32),
            shape((4, slots), ints), shape((4, slots), ints), shape((4, 128), ints),
            pltpu.VMEM((1, local), ints), pltpu.VMEM((local, 1), ints), pltpu.VMEM((local, 1), ints)),
        in_specs=[HBM] * 8 + [SMEM], out_specs=(VMEM,) * 8,
        scratch_shapes=[
            pltpu.VMEM((3, local, nodes), f32), pltpu.VMEM((local, nodes), f32), *[pltpu.VMEM(drop_clusters.shape[::-1], ints)] * 2,
            pltpu.VMEM((1, drop_owner.shape[0]), ints), *[pltpu.VMEM((1, slots), ints)] * 2, dma((8,)),
            pltpu.VMEM((8, slots), ints), pltpu.VMEM((2, 2, 8, slots), ints),
            pltpu.VMEM((2, ncol, 3, local, nodes), f32), pltpu.VMEM((2, nrow, 6, local, nodes), f32),
            *[dma((2 * nrow - 2, 6))] * 4, *[dma((6,))] * 2, *[dma((2,))] * 2,
            *[dma((max(half - 1, 1), 2))] * 4, *[dma((2,))] * 4],
        compiler_params=pltpu.CompilerParams(collective_id=0, has_side_effects=True, vmem_limit_bytes=30 << 20),
        name="gather_blocks",
    )(*map(far_off, (jnp.transpose(positions, (1, 0, 2)), jnp.transpose(normals, (1, 0, 2)), curvature, node_counts.T,
                     drop_clusters.T, drop_owner[None, :], pair_targets, pair_sources)), pair_count)
    speeds = pl.pallas_call(
        pair_kernel,
        out_shape=pltpu.VMEM((2, ncol, 3, local, nodes), f32),
        in_specs=[SMEM] * 3 + [VMEM] * 2, out_specs=VMEM,
        scratch_shapes=[pltpu.VMEM((2 * ncol * local * 8, nodes), f32)]
        + [pltpu.VMEM((unroll, nodes, 2 * nodes), f32)] * 2 + [pltpu.VMEM((unroll, 16, nodes), bf16)] * 2,
        compiler_params=pltpu.CompilerParams(vmem_limit_bytes=30 << 20),
        name="pairs",
    )(tl, sl, lc, keep(near), keep(far))
    owned = pl.pallas_call(
        functools.partial(home_kernel, nrow, ncol, cap),
        out_shape=jax.ShapeDtypeStruct((3, local, nodes), f32),
        in_specs=[VMEM] * 4, out_specs=VMEM,
        scratch_shapes=[
            pltpu.VMEM((2, ncol - 1, 3, local, nodes), f32), pltpu.VMEM((2, max(half - 1, 1), 3, local, nodes), f32),
            pltpu.VMEM((2, 3, local, nodes), f32), pltpu.VMEM((2, half, local, nodes), f32),
            pltpu.VMEM((3, devs, cap, nodes), f32), pltpu.VMEM((3, devs, cap, nodes), f32),
            dma((2, ncol - 1, 3)), dma((2, ncol - 1, 3)), dma((3,)), dma((3,)), dma((half,)), dma((half,)), dma((devs - 1, 3)), dma((devs - 1, 3)),
        ],
        compiler_params=pltpu.CompilerParams(collective_id=1, has_side_effects=True, vmem_limit_bytes=30 << 20),
        name="to_owners",
    )(keep(slot), keep(place), keep(owned_counts), keep(speeds))
    return jnp.transpose(owned, (1, 0, 2))


def solution(mesh):
    every = ("groups", "row", "col")
    in_specs = (
        P(every, None, None), P(every, None, None), P(every, None), P(every, None), P(every, None), P(every),
        P("groups", None), P("groups", None), P("groups"),
    )
    return jax.shard_map(per_device, mesh=mesh, in_specs=in_specs, out_specs=P(every, None, None), check_vma=False)
```
